32 devices in a mesh: groups: 2 (over y), ep: 4 (over z), tp: 4 (over x, core).
Axes of the slice: x: 2, y: 2, z: 4, core: 2. Of those that a mesh axis runs over, the one named last changes fastest.
Arguments:
- tokens: bfloat16 [1024, 3584], P(('groups', 'ep'), 'tp'), parts along dimension 0, may hold values from -6 to 6
- expert_ids: int32 [1024, 8], P(('groups', 'ep')), parts along dimension 0, may hold values from 0 to 255, as said below
- route_scores: float32 [1024, 8], P(('groups', 'ep')), parts along dimension 0, may hold values from -6 to 6
- w_gate: bfloat16 [4, 3584, 512], P('ep', None, 'tp'), may hold values from -0.09375 to 0.09375
- w_up: bfloat16 [4, 3584, 512], P('ep', None, 'tp'), may hold values from -0.09375 to 0.09375
- w_down: bfloat16 [4, 512, 3584], P('ep', 'tp'), may hold values from -0.1875 to 0.1875
Outputs:
- routed_out: bfloat16 [1024, 3584], P(('groups', 'ep'), 'tp'), parts along dimension 0
The draws below stay inside these ranges and needn't reach their ends.
There are 2 independent parts, one for each index of `groups`. The reference program is written for one: setup_inputs(seed, part) draws one part's arguments, and reference() takes and returns one part's arrays. A program takes and returns all parts, laid end to end along the dimension named above; an argument that names none is the same for every part. Nothing has to cross between parts.
Inputs may be any that keep to these rules, and one draw needn't show every extreme that they name: `expert_ids`: each token names 8 different experts, one from each range k * 32 to (k + 1) * 32 - 1 in some order. Among the 128 tokens of one index of ep no expert is named by more than 8 tokens.
All inputs are finite; a program needn't handle non-finite values.
Results may differ from the reference program's by a relative error of at most 0.013.
Values may be sent and summed in bfloat16 or wider, within the bound.
No kernel may reach another device: no remote copies, remote signals or barrier semaphores. Data moves between devices by JAX's collectives and lax.ppermute only.
A program may use at most 64 MiB of HBM per device.

```python
import jax
import jax.numpy as jnp
from jax import lax

D = 3584
H = 1024
TOP = 8
GROUPW = 32
ROWS = 128
CAP = 8
RESIDENT = 2
H_DEV = 128
TOKENS = 512
N_EP = 4
N_TP = 4


def pick_block(block_key, favored, tickets):
    shuffle_key, spread_key = jax.random.split(block_key)
    mixed = jax.random.permutation(shuffle_key, tickets)
    ordering = jnp.argsort((mixed != favored).astype(jnp.int32), stable=True)
    chosen = mixed[ordering][:ROWS]
    return jax.random.permutation(spread_key, chosen)


def shuffle_row(row_key, values):
    return jax.random.permutation(row_key, values)


def draw_expert_ids(key, part):
    key = jax.random.fold_in(key, 11)
    hot_key, ticket_key, row_key = jax.random.split(key, 3)
    hot_expert = jax.random.randint(hot_key, (), 0, min(RESIDENT, GROUPW)).astype(jnp.int32)
    tickets = jnp.arange(GROUPW * CAP, dtype=jnp.int32) // CAP
    block_keys = jax.random.split(ticket_key, N_EP * TOP)
    favored = jax.random.randint(jax.random.fold_in(ticket_key, 1), (N_EP * TOP,), 0, GROUPW).astype(jnp.int32)
    column = jnp.arange(N_EP * TOP, dtype=jnp.int32) % TOP
    favored = jnp.where(column == 0, hot_expert, favored)
    picked = jax.vmap(pick_block, in_axes=(0, 0, None))(block_keys, favored, tickets)
    picked = picked.reshape(N_EP, TOP, ROWS)
    routed = picked + (jnp.arange(TOP, dtype=jnp.int32) * GROUPW)[None, :, None]
    routed = jnp.transpose(routed, (0, 2, 1)).reshape(N_EP * ROWS, TOP)
    row_keys = jax.random.split(row_key, N_EP * ROWS)
    return jax.vmap(shuffle_row)(row_keys, routed).astype(jnp.int32)


def levels(key, dims, cuts, least, high):
    factor_of = 1.0
    for axis_at, blocks in cuts:
        draws = jax.random.uniform(jax.random.fold_in(jax.random.fold_in(key, 6), axis_at), (blocks,), jnp.float32, least / len(cuts), high / len(cuts))
        factor_of = factor_of * jnp.repeat(jnp.exp(draws), dims[axis_at] // blocks).reshape((-1,) + (1,) * (len(dims) - 1 - axis_at))
    return factor_of


def gaussian(stream_key, extent, scale, most, cuts=(), kind=jnp.bfloat16):
    entries = scale * jax.random.normal(stream_key, extent, jnp.float32)
    if cuts:
        entries = entries * levels(stream_key, extent, cuts, -0.22, 0.18)
    return jnp.clip(entries, -most, most).astype(kind)


def setup_inputs(seed: int = 0, part: int = 0) -> dict:
    keys = jax.random.split(jax.random.key(seed), 7)
    part_splits = jax.random.split(jax.random.fold_in(keys[6], part), 7)
    tokens = gaussian(part_splits[0], (TOKENS, D), 1.0, 6.0, ((0, 4), (1, 4)))
    expert_ids = draw_expert_ids(jax.random.fold_in(jax.random.fold_in(keys[6], part), 71), part)
    route_scores = gaussian(part_splits[2], (TOKENS, TOP), 1.5, 6.0, ((0, 4),), jnp.float32)
    w_gate = gaussian(keys[3], (N_EP, D, H // 2), D ** -0.5, 0.09375, ((0, 4), (2, 4)))
    w_up = gaussian(keys[4], (N_EP, D, H // 2), D ** -0.5, 0.09375, ((0, 4), (2, 4)))
    w_down = gaussian(keys[5], (N_EP, H // 2, D), H ** -0.5, 0.1875, ((0, 4), (1, 4)))
    return {"tokens": tokens, "expert_ids": expert_ids, "route_scores": route_scores, "w_gate": w_gate, "w_up": w_up, "w_down": w_down}


def expert_block(expert_in, gate_weight, up_weight, down_weight):
    gate_act = jnp.dot(expert_in, gate_weight, preferred_element_type=jnp.float32)
    up_act = jnp.dot(expert_in, up_weight, preferred_element_type=jnp.float32)
    hidden = (jax.nn.silu(gate_act) * up_act).astype(jnp.bfloat16)
    slots = hidden.shape[0]
    blocks = 2 * N_TP
    split_hidden = hidden.reshape(slots, blocks, H_DEV).astype(jnp.float32)
    split_down = down_weight.reshape(blocks, H_DEV, D).astype(jnp.float32)
    partial_value = jnp.einsum("sqh,qhd->sqd", split_hidden, split_down, precision=lax.Precision.HIGHEST).astype(jnp.bfloat16)
    return jnp.sum(partial_value.astype(jnp.float32), axis=1)


def run_expert(packed):
    return expert_block(packed[0], packed[1], packed[2], packed[3])


def reference(tokens, expert_ids, route_scores, w_gate, w_up, w_down):
    squashed = jax.nn.sigmoid(route_scores)
    weights = 2.5 * squashed / jnp.sum(squashed, axis=1, keepdims=True)
    gate_full = jnp.transpose(w_gate.reshape(RESIDENT, 2, D, H // 2), (0, 2, 1, 3)).reshape(RESIDENT, D, H)
    up_full = jnp.transpose(w_up.reshape(RESIDENT, 2, D, H // 2), (0, 2, 1, 3)).reshape(RESIDENT, D, H)
    down_full = w_down.reshape(RESIDENT, H, D)
    flat_ids = expert_ids.reshape(N_EP, ROWS * TOP)
    onehot = (flat_ids[:, :, None] == jnp.arange(RESIDENT, dtype=jnp.int32)[None, None, :]).astype(jnp.int32)
    slot_index = jnp.sum((jnp.cumsum(onehot, axis=1) - 1) * onehot, axis=2)
    resident = jnp.sum(onehot, axis=2)
    source = jnp.arange(N_EP, dtype=jnp.int32)[:, None]
    outside = RESIDENT * N_EP * CAP
    target = jnp.where(resident > 0, flat_ids * (N_EP * CAP) + source * CAP + slot_index, outside)
    target = target.reshape(TOKENS, TOP).astype(jnp.int32)
    buffer = jnp.zeros((outside, D), jnp.bfloat16)
    for column in range(TOP):
        buffer = buffer.at[target[:, column]].set(tokens, mode="drop")
    outputs = lax.map(run_expert, (buffer.reshape(RESIDENT, N_EP * CAP, D), gate_full, up_full, down_full))
    flat_out = outputs.reshape(outside, D)
    running = jnp.zeros((TOKENS, D), jnp.float32)
    for column in range(TOP):
        chosen = jnp.take(flat_out, jnp.minimum(target[:, column], outside - 1), axis=0)
        inside = target[:, column] < outside
        running = running + jnp.where(inside[:, None], weights[:, column:column + 1] * chosen, 0.0)
    return running.astype(jnp.bfloat16)
```

```python
import jax
import jax.numpy as jnp
from jax import lax
from jax.experimental import pallas as pl
from jax.experimental.pallas import tpu as pltpu
from jax.sharding import PartitionSpec as P

CAP = 8


def route(ep_count, ids_ref, scores_ref, tokens_ref, outgoing_ref, match_ref, weight_ref):
    row_count = ids_ref.shape[0]
    slot_rows = outgoing_ref.shape[0]
    ids = ids_ref[...].astype(jnp.float32)
    expert = jnp.min(ids, axis=1, keepdims=True)
    squashed = jax.nn.sigmoid(scores_ref[...])
    chosen = jnp.sum(jnp.where(ids == expert, squashed, 0.0), axis=1, keepdims=True)
    weight_ref[...] = 2.5 * chosen / jnp.sum(squashed, axis=1, keepdims=True)
    lanes = lax.broadcasted_iota(jnp.int32, (row_count, 128), 1).astype(jnp.float32)
    onehot = jnp.where(expert == lanes, 1.0, 0.0)
    earlier = jnp.where(
        lax.broadcasted_iota(jnp.int32, (row_count, row_count), 1)
        < lax.broadcasted_iota(jnp.int32, (row_count, row_count), 0),
        1.0,
        0.0,
    ).astype(jnp.bfloat16)
    counts = jnp.dot(earlier, onehot.astype(jnp.bfloat16), preferred_element_type=jnp.float32)
    slot = jnp.sum(counts * onehot, axis=1, keepdims=True)
    code = expert * CAP + slot
    column = lax.broadcasted_iota(jnp.int32, (row_count, slot_rows), 1)
    index = lax.rem(column, ep_count * CAP)
    wanted = (index // (2 * CAP)) * CAP + lax.rem(index, CAP)
    match = jnp.where(code == wanted.astype(jnp.float32), 1.0, 0.0).astype(jnp.bfloat16)
    match_ref[...] = match
    outgoing_ref[...] = lax.dot_general(
        match, tokens_ref[...], (((0,), (0,)), ((), ())), preferred_element_type=jnp.float32
    ).astype(jnp.bfloat16)


def experts(tp_count, rows_ref, gate_ref, up_ref, down_ref, out_ref):
    slot_count = rows_ref.shape[0] // tp_count
    features = rows_ref.shape[1]
    gate_act = jnp.zeros((slot_count, gate_ref.shape[2]), jnp.float32)
    up_act = jnp.zeros((slot_count, up_ref.shape[2]), jnp.float32)
    for part in range(tp_count):
        rows = rows_ref[part * slot_count : (part + 1) * slot_count, :]
        columns = slice(part * features, (part + 1) * features)
        gate_act += jnp.dot(rows, gate_ref[0, columns, :], preferred_element_type=jnp.float32)
        up_act += jnp.dot(rows, up_ref[0, columns, :], preferred_element_type=jnp.float32)
    hidden = (gate_act / (1.0 + jnp.exp(-gate_act)) * up_act).astype(jnp.bfloat16)
    for part in range(tp_count):
        columns = slice(part * features, (part + 1) * features)
        out_ref[part * slot_count : (part + 1) * slot_count, :] = jnp.dot(
            hidden, down_ref[0, :, columns], preferred_element_type=jnp.float32
        ).astype(jnp.bfloat16)


def combine(match_ref, weight_ref, returned_ref, out_ref):
    summed = jnp.dot(match_ref[...], returned_ref[...], preferred_element_type=jnp.float32)
    out_ref[...] = (weight_ref[...] * summed).astype(jnp.bfloat16)


def shards(tokens, expert_ids, route_scores, w_gate, w_up, w_down):
    row_count, features = tokens.shape
    ep_count, tp_count = lax.axis_size("ep"), lax.axis_size("tp")
    slot_rows = ep_count * tp_count * CAP
    limit = pltpu.CompilerParams(vmem_limit_bytes=32 * 1024 * 1024)
    outgoing, match, weight = pl.pallas_call(
        lambda *refs: route(ep_count, *refs),
        out_shape=(
            jax.ShapeDtypeStruct((slot_rows, features), jnp.bfloat16),
            jax.ShapeDtypeStruct((row_count, slot_rows), jnp.bfloat16),
            jax.ShapeDtypeStruct((row_count, 1), jnp.float32),
        ),
        compiler_params=limit,
        name="route",
    )(expert_ids, route_scores, tokens)
    incoming = lax.all_to_all(outgoing, ("tp", "ep"), split_axis=0, concat_axis=0, tiled=True)
    partial_value = pl.pallas_call(
        lambda *refs: experts(tp_count, *refs),
        out_shape=jax.ShapeDtypeStruct((slot_rows, features), jnp.bfloat16),
        compiler_params=limit,
        name="experts",
    )(incoming, w_gate, w_up, w_down)
    returned = lax.all_to_all(partial_value, ("tp", "ep"), split_axis=0, concat_axis=0, tiled=True)
    return pl.pallas_call(
        combine,
        out_shape=jax.ShapeDtypeStruct((row_count, features), jnp.bfloat16),
        compiler_params=limit,
        name="combine",
    )(match, weight, returned)


def solution(mesh):
    placed = (
        P(("groups", "ep"), "tp"),
        P(("groups", "ep"), None),
        P(("groups", "ep"), None),
        P("ep", None, "tp"),
        P("ep", None, "tp"),
        P("ep", "tp", None),
    )
    return jax.shard_map(
        shards, mesh=mesh, in_specs=placed, out_specs=P(("groups", "ep"), "tp"), check_vma=False
    )
```

```python
import jax
import jax.numpy as jnp
from jax import lax
from jax.experimental import pallas as pl
from jax.experimental.pallas import tpu as pltpu
from jax.sharding import PartitionSpec as P

CAP = 8
AXES = ("tp", "ep")
LIMIT = pltpu.CompilerParams(vmem_limit_bytes=16 * 1024 * 1024)


def iota(shape, dim):
    return lax.broadcasted_iota(jnp.int32, shape, dim)


def to_column(row):
    size = row.shape[1]
    square = (size, size)
    return jnp.sum(jnp.where(iota(square, 0) == iota(square, 1), row, 0.0), axis=1, keepdims=True)


def route(ep_count, resident, gathered, ids_ref, scores_ref, tokens_ref, outgoing_ref, match_ref, weight_ref):
    row_count = ids_ref.shape[1]
    slot_rows = match_ref.shape[1]
    ids = ids_ref[...].astype(jnp.float32)
    expert = jnp.min(ids, axis=0, keepdims=True)
    squashed = jax.nn.sigmoid(scores_ref[...])
    chosen = jnp.sum(jnp.where(ids == expert, squashed, 0.0), axis=0, keepdims=True)
    weight = 2.5 * chosen / jnp.sum(squashed, axis=0, keepdims=True)
    onehot_shape = (-(-resident // 16) * 16, row_count)
    onehot = jnp.where(expert == iota(onehot_shape, 0).astype(jnp.float32), 1.0, 0.0)
    square = (row_count, row_count)
    earlier = jnp.where(iota(square, 0) < iota(square, 1), 1.0, 0.0).astype(jnp.bfloat16)
    counts = jnp.dot(onehot.astype(jnp.bfloat16), earlier, preferred_element_type=jnp.float32)
    code = expert * CAP + jnp.sum(counts * onehot, axis=0, keepdims=True)
    send_rows = outgoing_ref.shape[0]
    row = iota((send_rows, row_count), 0)
    if gathered:
        wanted = row
    else:
        index = lax.rem(row, ep_count * CAP)
        wanted = (index // (2 * CAP)) * CAP + lax.rem(index, CAP)
    dispatch = jnp.where(code == wanted.astype(jnp.float32), 1.0, 0.0).astype(jnp.bfloat16)
    outgoing_ref[...] = jnp.dot(
        dispatch, tokens_ref[...], preferred_element_type=jnp.float32
    ).astype(jnp.bfloat16)
    column = iota((row_count, slot_rows), 1)
    source = lax.rem(column // CAP, ep_count)
    if gathered:
        source = lax.rem(lax.axis_index("ep") + ep_count - source, ep_count)
    returned = (source // 2) * CAP + lax.rem(column, CAP)
    match_ref[...] = jnp.where(to_column(code) == returned.astype(jnp.float32), 1.0, 0.0).astype(
        jnp.bfloat16
    )
    weight_ref[...] = to_column(weight)


def experts(ep_count, tp_count, resident, gathered, rows_ref, gate_ref, up_ref, down_ref, *out_refs):
    features = down_ref.shape[2] // tp_count
    part_rows = resident * ep_count * CAP if gathered else rows_ref.shape[0] // tp_count
    gate_act = jnp.zeros((part_rows, gate_ref.shape[2]), jnp.float32)
    up_act = jnp.zeros((part_rows, up_ref.shape[2]), jnp.float32)
    for part in range(tp_count):
        columns = slice(part * features, (part + 1) * features)
        if gathered:
            offsets = [(block * tp_count + part) * features for block in range(ep_count)]
            rows = jnp.concatenate([rows_ref[:, at : at + features] for at in offsets], axis=0)
        else:
            rows = rows_ref[part * part_rows : (part + 1) * part_rows, :]
        gate_act += jnp.dot(rows, gate_ref[0, columns, :], preferred_element_type=jnp.float32)
        up_act += jnp.dot(rows, up_ref[0, columns, :], preferred_element_type=jnp.float32)
    hidden = (gate_act / (1.0 + jnp.exp(-gate_act)) * up_act).astype(jnp.bfloat16)
    if not gathered:
        for part in range(tp_count):
            columns = slice(part * features, (part + 1) * features)
            out_refs[0][part * part_rows : (part + 1) * part_rows, :] = jnp.dot(
                hidden, down_ref[0, :, columns], preferred_element_type=jnp.float32
            ).astype(jnp.bfloat16)
        return
    here, lane = lax.axis_index("ep"), lax.axis_index("tp")
    picked_shape = (ep_count * CAP, part_rows)
    picked_row, held_row = iota(picked_shape, 0), iota(picked_shape, 1)
    block = lax.rem(here + picked_row // CAP, ep_count)
    origin = (block * resident + here // 2) * CAP + lax.rem(picked_row, CAP)
    pick = jnp.where(held_row == origin, 1.0, 0.0).astype(jnp.bfloat16)
    picked = jnp.dot(pick, hidden, preferred_element_type=jnp.float32).astype(jnp.bfloat16)
    for part in range(tp_count):
        start = pl.multiple_of(lax.rem(lane + part, tp_count) * features, features)
        values = jnp.dot(
            picked, down_ref[0, :, pl.ds(start, features)], preferred_element_type=jnp.float32
        ).astype(jnp.bfloat16)
        for block in range(ep_count):
            out_refs[part * ep_count + block][...] = values[block * CAP : (block + 1) * CAP, :]


def combine(match_ref, weight_ref, *refs):
    returned = jnp.concatenate([ref[...] for ref in refs[:-1]], axis=0)
    summed = jnp.dot(match_ref[...], returned, preferred_element_type=jnp.float32)
    refs[-1][...] = (weight_ref[...] * summed).astype(jnp.bfloat16)


def shards(tokens, expert_ids, route_scores, w_gate, w_up, w_down):
    row_count, features = tokens.shape
    ep_count, tp_count = lax.axis_size("ep"), lax.axis_size("tp")
    resident = ep_count // 2
    peers = ep_count * tp_count
    gathered = peers <= 16
    slot_rows = peers * CAP
    outgoing, match, weight = pl.pallas_call(
        lambda *refs: route(ep_count, resident, gathered, *refs),
        out_shape=(
            jax.ShapeDtypeStruct((resident * CAP if gathered else slot_rows, features), jnp.bfloat16),
            jax.ShapeDtypeStruct((row_count, slot_rows), jnp.bfloat16),
            jax.ShapeDtypeStruct((row_count, 1), jnp.float32),
        ),
        compiler_params=LIMIT,
        name="route",
    )(expert_ids.T, route_scores.T, tokens)
    if gathered:
        incoming = lax.all_gather(outgoing, ("ep", "tp"), axis=1, tiled=True)
        chunk = jax.ShapeDtypeStruct((CAP, features), jnp.bfloat16)
        partial_shape = (chunk,) * peers
    else:
        incoming = lax.all_to_all(outgoing, AXES, split_axis=0, concat_axis=0, tiled=True)
        partial_shape = (jax.ShapeDtypeStruct((slot_rows, features), jnp.bfloat16),)
    partial_values = pl.pallas_call(
        lambda *refs: experts(ep_count, tp_count, resident, gathered, *refs),
        out_shape=partial_shape,
        compiler_params=LIMIT,
        name="experts",
    )(incoming, w_gate, w_up, w_down)
    if gathered:
        returned = list(partial_values)
        for part in range(tp_count):
            for block in range(ep_count):
                which = part * ep_count + block
                if which:
                    pairs = [
                        (z * tp_count + f, (z + block) % ep_count * tp_count + (f + part) % tp_count)
                        for f in range(tp_count)
                        for z in range(ep_count)
                    ]
                    returned[which] = lax.ppermute(partial_values[which], ("ep", "tp"), pairs)
    else:
        returned = [
            lax.all_to_all(partial_values[0], AXES, split_axis=0, concat_axis=0, tiled=True)
        ]
    return pl.pallas_call(
        combine,
        out_shape=jax.ShapeDtypeStruct((row_count, features), jnp.bfloat16),
        compiler_params=LIMIT,
        name="combine",
    )(match, weight, *returned)


def solution(mesh):
    placed = (
        P(("groups", "ep"), "tp"),
        P(("groups", "ep"), None),
        P(("groups", "ep"), None),
        P("ep", None, "tp"),
        P("ep", None, "tp"),
        P("ep", "tp", None),
    )
    return jax.shard_map(
        shards, mesh=mesh, in_specs=placed, out_specs=P(("groups", "ep"), "tp"), check_vma=False
    )
```

```python
import jax
import jax.numpy as jnp
from jax import lax
from jax.experimental import pallas as pl
from jax.experimental.pallas import tpu as pltpu
from jax.sharding import PartitionSpec as P

CAP = 8
PIECE = 32
WEIGHT_PARTS = 4
AXES = ("tp", "ep")
LIMIT = pltpu.CompilerParams(vmem_limit_bytes=16 * 1024 * 1024)


def iota(shape, dim):
    return lax.broadcasted_iota(jnp.int32, shape, dim)


def to_column(row):
    size = row.shape[1]
    square = (size, size)
    return jnp.sum(jnp.where(iota(square, 0) == iota(square, 1), row, 0.0), axis=1, keepdims=True)


def route(ep_count, resident, *refs):
    ids_hbm, scores_hbm, tokens_hbm, outgoing_ref, match_ref, weight_ref = refs[:3] + refs[6:9]
    ids_ref, scores_ref, tokens_ref, sems, weight_sems = refs[12:]
    row_count = ids_ref.shape[1]
    slot_rows = match_ref.shape[1]
    parts = row_count // PIECE
    copies = [
        pltpu.make_async_copy(ids_hbm, ids_ref, sems.at[parts]),
        pltpu.make_async_copy(scores_hbm, scores_ref, sems.at[parts + 1]),
    ] + [
        pltpu.make_async_copy(
            tokens_hbm.at[pl.ds(part * PIECE, PIECE), :],
            tokens_ref.at[pl.ds(part * PIECE, PIECE), :],
            sems.at[part],
        )
        for part in range(parts)
    ]
    pieces = [
        pltpu.make_async_copy(
            source.at[:, pl.ds(part * size, size), :],
            target.at[:, pl.ds(part * size, size), :],
            weight_sems.at[which * WEIGHT_PARTS + part],
        )
        for which, (source, target) in enumerate(zip(refs[3:6], refs[9:12]))
        for size in [source.shape[1] // WEIGHT_PARTS]
        for part in range(WEIGHT_PARTS)
    ]
    for copy in copies + pieces:
        copy.start()
    square = (row_count, row_count)
    earlier = jnp.where(iota(square, 0) < iota(square, 1), 1.0, 0.0).astype(jnp.bfloat16)
    copies[0].wait()
    ids = ids_ref[...].astype(jnp.float32)
    expert = jnp.min(ids, axis=0, keepdims=True)
    onehot_shape = (-(-resident // 16) * 16, row_count)
    onehot = jnp.where(expert == iota(onehot_shape, 0).astype(jnp.float32), 1.0, 0.0)
    counts = jnp.dot(onehot.astype(jnp.bfloat16), earlier, preferred_element_type=jnp.float32)
    code = expert * CAP + jnp.sum(counts * onehot, axis=0, keepdims=True)
    index = lax.rem(iota((slot_rows, row_count), 0), ep_count * CAP)
    wanted = (index // (2 * CAP)) * CAP + lax.rem(index, CAP)
    dispatch = jnp.where(code == wanted.astype(jnp.float32), 1.0, 0.0).astype(jnp.bfloat16)
    index = lax.rem(iota((row_count, slot_rows), 1), ep_count * CAP)
    wanted = (index // (2 * CAP)) * CAP + lax.rem(index, CAP)
    match_ref[...] = jnp.where(to_column(code) == wanted.astype(jnp.float32), 1.0, 0.0).astype(
        jnp.bfloat16
    )
    copies[1].wait()
    squashed = jax.nn.sigmoid(scores_ref[...])
    chosen = jnp.sum(jnp.where(ids == expert, squashed, 0.0), axis=0, keepdims=True)
    weight_ref[...] = to_column(2.5 * chosen / jnp.sum(squashed, axis=0, keepdims=True))
    for copy in copies[2:]:
        copy.wait()
    outgoing_ref[...] = jnp.dot(
        dispatch, tokens_ref[...], preferred_element_type=jnp.float32
    ).astype(jnp.bfloat16)
    for piece in pieces:
        piece.wait()


def experts(tp_count, rows_ref, gate_ref, up_ref, down_ref, out_ref):
    part_rows, features = rows_ref.shape[0] // tp_count, rows_ref.shape[1]
    gate_act = jnp.zeros((part_rows, gate_ref.shape[2]), jnp.float32)
    up_act = jnp.zeros((part_rows, up_ref.shape[2]), jnp.float32)
    for part in range(tp_count):
        rows = rows_ref[part * part_rows : (part + 1) * part_rows, :]
        columns = slice(part * features, (part + 1) * features)
        gate_act += jnp.dot(rows, gate_ref[0, columns, :], preferred_element_type=jnp.float32)
        up_act += jnp.dot(rows, up_ref[0, columns, :], preferred_element_type=jnp.float32)
    hidden = (gate_act / (1.0 + jnp.exp(-gate_act)) * up_act).astype(jnp.bfloat16)
    for part in range(tp_count):
        columns = slice(part * features, (part + 1) * features)
        out_ref[part * part_rows : (part + 1) * part_rows, :] = jnp.dot(
            hidden, down_ref[0, :, columns], preferred_element_type=jnp.float32
        ).astype(jnp.bfloat16)


def combine(match_ref, weight_ref, returned_ref, out_ref):
    summed = jnp.dot(match_ref[...], returned_ref[...], preferred_element_type=jnp.float32)
    out_ref[...] = (weight_ref[...] * summed).astype(jnp.bfloat16)


def shards(tokens, expert_ids, route_scores, w_gate, w_up, w_down):
    row_count, features = tokens.shape
    ep_count, tp_count = lax.axis_size("ep"), lax.axis_size("tp")
    slot_rows = ep_count * tp_count * CAP
    top_count = expert_ids.shape[1]
    inputs = (expert_ids.T, route_scores.T, tokens, w_gate, w_up, w_down)
    inputs = [pltpu.with_memory_space_constraint(value, pltpu.HBM) for value in inputs]
    outgoing, match, weight, *held = pl.pallas_call(
        lambda *refs: route(ep_count, ep_count // 2, *refs),
        in_specs=[pl.BlockSpec(memory_space=pltpu.HBM)] * 6,
        out_shape=(
            jax.ShapeDtypeStruct((slot_rows, features), jnp.bfloat16),
            jax.ShapeDtypeStruct((row_count, slot_rows), jnp.bfloat16),
            jax.ShapeDtypeStruct((row_count, 1), jnp.float32),
        )
        + tuple(jax.ShapeDtypeStruct(value.shape, value.dtype) for value in (w_gate, w_up, w_down)),
        scratch_shapes=[
            pltpu.VMEM((top_count, row_count), jnp.int32),
            pltpu.VMEM((top_count, row_count), jnp.float32),
            pltpu.VMEM((row_count, features), jnp.bfloat16),
            pltpu.SemaphoreType.DMA((row_count // PIECE + 2,)),
            pltpu.SemaphoreType.DMA((3 * WEIGHT_PARTS,)),
        ],
        compiler_params=LIMIT,
        name="route",
    )(*inputs)
    incoming = lax.all_to_all(outgoing, AXES, split_axis=0, concat_axis=0, tiled=True)
    partial_value = pl.pallas_call(
        lambda *refs: experts(tp_count, *refs),
        out_shape=jax.ShapeDtypeStruct((slot_rows, features), jnp.bfloat16),
        compiler_params=LIMIT,
        name="experts",
    )(incoming, *held)
    returned = lax.all_to_all(partial_value, AXES, split_axis=0, concat_axis=0, tiled=True)
    return pl.pallas_call(
        combine,
        out_shape=jax.ShapeDtypeStruct((row_count, features), jnp.bfloat16),
        compiler_params=LIMIT,
        name="combine",
    )(match, weight, returned)


def solution(mesh):
    placed = (
        P(("groups", "ep"), "tp"),
        P(("groups", "ep"), None),
        P(("groups", "ep"), None),
        P("ep", None, "tp"),
        P("ep", None, "tp"),
        P("ep", "tp", None),
    )
    return jax.shard_map(
        shards, mesh=mesh, in_specs=placed, out_specs=P(("groups", "ep"), "tp"), check_vma=False
    )
```

```python
import jax
import jax.numpy as jnp
from jax import lax
from jax.experimental import pallas as pl
from jax.experimental.pallas import tpu as pltpu
from jax.sharding import PartitionSpec as P

CAP = 8
PIECE = 32
WEIGHT_PARTS = 4
AXES = ("chip", "ep")
LIMIT = pltpu.CompilerParams(vmem_limit_bytes=16 * 1024 * 1024)


def iota(shape, dim):
    return lax.broadcasted_iota(jnp.int32, shape, dim)


def to_column(row):
    size = row.shape[1]
    square = (size, size)
    return jnp.sum(jnp.where(iota(square, 0) == iota(square, 1), row, 0.0), axis=1, keepdims=True)


def route(ep_count, resident, *refs):
    ids_hbm, scores_hbm, tokens_hbm, outgoing_ref, match_ref, weight_ref = refs[:3] + refs[6:9]
    ids_ref, scores_ref, tokens_ref, sems, weight_sems = refs[12:]
    row_count = ids_ref.shape[1]
    slot_rows = match_ref.shape[1]
    parts = row_count // PIECE
    copies = [
        pltpu.make_async_copy(ids_hbm, ids_ref, sems.at[parts]),
        pltpu.make_async_copy(scores_hbm, scores_ref, sems.at[parts + 1]),
    ] + [
        pltpu.make_async_copy(
            tokens_hbm.at[pl.ds(part * PIECE, PIECE), :],
            tokens_ref.at[pl.ds(part * PIECE, PIECE), :],
            sems.at[part],
        )
        for part in range(parts)
    ]
    pieces = [
        pltpu.make_async_copy(
            source.at[:, pl.ds(part * size, size), :],
            target.at[:, pl.ds(part * size, size), :],
            weight_sems.at[which * WEIGHT_PARTS + part],
        )
        for which, (source, target) in enumerate(zip(refs[3:6], refs[9:12]))
        for size in [source.shape[1] // WEIGHT_PARTS]
        for part in range(WEIGHT_PARTS)
    ]
    for copy in copies + pieces:
        copy.start()
    square = (row_count, row_count)
    earlier = jnp.where(iota(square, 0) < iota(square, 1), 1.0, 0.0).astype(jnp.bfloat16)
    copies[0].wait()
    ids = ids_ref[...].astype(jnp.float32)
    expert = jnp.min(ids, axis=0, keepdims=True)
    onehot_shape = (-(-resident // 16) * 16, row_count)
    onehot = jnp.where(expert == iota(onehot_shape, 0).astype(jnp.float32), 1.0, 0.0)
    counts = jnp.dot(onehot.astype(jnp.bfloat16), earlier, preferred_element_type=jnp.float32)
    code = expert * CAP + jnp.sum(counts * onehot, axis=0, keepdims=True)
    index = lax.rem(iota((slot_rows, row_count), 0), ep_count * CAP)
    wanted = (index // (2 * CAP)) * CAP + lax.rem(index, CAP)
    dispatch = jnp.where(code == wanted.astype(jnp.float32), 1.0, 0.0).astype(jnp.bfloat16)
    index = lax.rem(iota((row_count, slot_rows), 1), ep_count * CAP)
    wanted = (index // (2 * CAP)) * CAP + lax.rem(index, CAP)
    match_ref[...] = jnp.where(to_column(code) == wanted.astype(jnp.float32), 1.0, 0.0).astype(
        jnp.bfloat16
    )
    copies[1].wait()
    squashed = jax.nn.sigmoid(scores_ref[...])
    chosen = jnp.sum(jnp.where(ids == expert, squashed, 0.0), axis=0, keepdims=True)
    weight_ref[...] = to_column(2.5 * chosen / jnp.sum(squashed, axis=0, keepdims=True))
    for copy in copies[2:]:
        copy.wait()
    outgoing_ref[...] = jnp.dot(
        dispatch, tokens_ref[...], preferred_element_type=jnp.float32
    ).astype(jnp.bfloat16)
    for piece in pieces:
        piece.wait()


def lift(tp_count, ep_count, own, rows_ref, gate_ref, up_ref):
    part_rows, features = ep_count * CAP, rows_ref.shape[1]
    core = lax.axis_index("core")
    core = core if own else 1 - core
    gate_act = jnp.zeros((part_rows, gate_ref.shape[2]), jnp.float32)
    up_act = jnp.zeros((part_rows, up_ref.shape[2]), jnp.float32)
    for chip in range(tp_count // 2):
        rows = rows_ref[chip * part_rows : (chip + 1) * part_rows, :]
        start = pl.multiple_of((2 * chip + core) * features, features)
        columns = pl.ds(start, features)
        gate_act += jnp.dot(rows, gate_ref[0, columns, :], preferred_element_type=jnp.float32)
        up_act += jnp.dot(rows, up_ref[0, columns, :], preferred_element_type=jnp.float32)
    return gate_act, up_act


def begin(tp_count, ep_count, rows_ref, gate_ref, up_ref, gate_act_ref, up_act_ref):
    gate_act_ref[...], up_act_ref[...] = lift(tp_count, ep_count, True, rows_ref, gate_ref, up_ref)


def finish(tp_count, ep_count, *refs):
    rows_ref, gate_act_ref, up_act_ref, gate_ref, up_ref, down_ref, mine_ref, other_ref = refs
    part_rows, features = ep_count * CAP, rows_ref.shape[1]
    gate_act, up_act = lift(tp_count, ep_count, False, rows_ref, gate_ref, up_ref)
    gate_act += gate_act_ref[...]
    up_act += up_act_ref[...]
    hidden = (gate_act / (1.0 + jnp.exp(-gate_act)) * up_act).astype(jnp.bfloat16)
    core = lax.axis_index("core")
    for out_ref, target in ((other_ref, 1 - core), (mine_ref, core)):
        for chip in range(tp_count // 2):
            start = pl.multiple_of((2 * chip + target) * features, features)
            out_ref[chip * part_rows : (chip + 1) * part_rows, :] = jnp.dot(
                hidden, down_ref[0, :, pl.ds(start, features)], preferred_element_type=jnp.float32
            ).astype(jnp.bfloat16)


def add(mine_ref, other_ref, out_ref):
    total = mine_ref[...].astype(jnp.float32) + other_ref[...].astype(jnp.float32)
    out_ref[...] = total.astype(jnp.bfloat16)


def combine(match_ref, weight_ref, returned_ref, out_ref):
    summed = jnp.dot(match_ref[...], returned_ref[...], preferred_element_type=jnp.float32)
    out_ref[...] = (weight_ref[...] * summed).astype(jnp.bfloat16)


def shards(tokens, expert_ids, route_scores, w_gate, w_up, w_down):
    row_count, features = tokens.shape
    ep_count, tp_count = lax.axis_size("ep"), 2 * lax.axis_size("chip")
    slot_rows = ep_count * tp_count // 2 * CAP
    top_count = expert_ids.shape[1]
    hidden_count = w_gate.shape[2]
    inputs = (expert_ids.T, route_scores.T, tokens, w_gate, w_up, w_down)
    inputs = [pltpu.with_memory_space_constraint(value, pltpu.HBM) for value in inputs]
    outgoing, match, weight, *held = pl.pallas_call(
        lambda *refs: route(ep_count, ep_count // 2, *refs),
        in_specs=[pl.BlockSpec(memory_space=pltpu.HBM)] * 6,
        out_shape=(
            jax.ShapeDtypeStruct((slot_rows, features), jnp.bfloat16),
            jax.ShapeDtypeStruct((row_count, slot_rows), jnp.bfloat16),
            jax.ShapeDtypeStruct((row_count, 1), jnp.float32),
        )
        + tuple(jax.ShapeDtypeStruct(value.shape, value.dtype) for value in (w_gate, w_up, w_down)),
        scratch_shapes=[
            pltpu.VMEM((top_count, row_count), jnp.int32),
            pltpu.VMEM((top_count, row_count), jnp.float32),
            pltpu.VMEM((row_count, features), jnp.bfloat16),
            pltpu.SemaphoreType.DMA((row_count // PIECE + 2,)),
            pltpu.SemaphoreType.DMA((3 * WEIGHT_PARTS,)),
        ],
        compiler_params=LIMIT,
        name="route",
    )(*inputs)
    swap = [(0, 1), (1, 0)]
    incoming = lax.all_to_all(outgoing, AXES, split_axis=0, concat_axis=0, tiled=True)
    across = lax.ppermute(incoming, "core", swap)
    acts = (jax.ShapeDtypeStruct((ep_count * CAP, hidden_count), jnp.float32),) * 2
    begun = pl.pallas_call(
        lambda *refs: begin(tp_count, ep_count, *refs),
        out_shape=acts,
        compiler_params=LIMIT,
        name="begin",
    )(incoming, held[0], held[1])
    half = jax.ShapeDtypeStruct((slot_rows, features), jnp.bfloat16)
    mine, other = pl.pallas_call(
        lambda *refs: finish(tp_count, ep_count, *refs),
        out_shape=(half, half),
        compiler_params=LIMIT,
        name="finish",
    )(across, *begun, *held)
    summed = pl.pallas_call(add, out_shape=half, compiler_params=LIMIT, name="add")(
        mine, lax.ppermute(other, "core", swap)
    )
    returned = lax.all_to_all(summed, AXES, split_axis=0, concat_axis=0, tiled=True)
    return pl.pallas_call(
        combine,
        out_shape=jax.ShapeDtypeStruct((row_count, features), jnp.bfloat16),
        compiler_params=LIMIT,
        name="combine",
    )(match, weight, returned)


def solution(mesh):
    groups, ep_count, tp_count = (mesh.shape[name] for name in ("groups", "ep", "tp"))
    split = jax.sharding.Mesh(
        mesh.devices.reshape(groups, ep_count, tp_count // 2, 2), ("groups", "ep", "chip", "core")
    )
    tp = ("chip", "core")
    placed = (
        P(("groups", "ep"), tp),
        P(("groups", "ep"), None),
        P(("groups", "ep"), None),
        P("ep", None, tp),
        P("ep", None, tp),
        P("ep", tp, None),
    )
    return jax.shard_map(
        shards, mesh=split, in_specs=placed, out_specs=P(("groups", "ep"), tp), check_vma=False
    )
```

```python
import jax
import jax.numpy as jnp
from jax import lax
from jax.experimental import pallas as pl
from jax.experimental.pallas import tpu as pltpu
from jax.sharding import PartitionSpec as P

CAP = 8
PIECE = 32
WEIGHT_PARTS = 4
NEAR = ("chip", "half")
SWAP = [(0, 1), (1, 0)]
LIMIT = pltpu.CompilerParams(vmem_limit_bytes=16 * 1024 * 1024)


def iota(shape, dim):
    return lax.broadcasted_iota(jnp.int32, shape, dim)


def to_column(row):
    size = row.shape[1]
    square = (size, size)
    return jnp.sum(jnp.where(iota(square, 0) == iota(square, 1), row, 0.0), axis=1, keepdims=True)


def slot_codes(ids, resident):
    row_count = ids.shape[1]
    expert = jnp.min(ids, axis=0, keepdims=True)
    onehot_shape = (-(-resident // 16) * 16, row_count)
    onehot = jnp.where(expert == iota(onehot_shape, 0).astype(jnp.float32), 1.0, 0.0)
    square = (row_count, row_count)
    earlier = jnp.where(iota(square, 0) < iota(square, 1), 1.0, 0.0).astype(jnp.bfloat16)
    counts = jnp.dot(onehot.astype(jnp.bfloat16), earlier, preferred_element_type=jnp.float32)
    return expert * CAP + jnp.sum(counts * onehot, axis=0, keepdims=True), expert


def block_codes(index, resident):
    if resident == 2:
        index = lax.rem(index + lax.axis_index("expert") * CAP, resident * CAP)
    return index.astype(jnp.float32)


def route(resident, ids_hbm, tokens_hbm, *refs):
    out_refs, (ids_ref, tokens_ref, sems) = refs[:-3], refs[-3:]
    row_count = ids_ref.shape[1]
    parts = row_count // PIECE
    copies = [pltpu.make_async_copy(ids_hbm, ids_ref, sems.at[parts])] + [
        pltpu.make_async_copy(
            tokens_hbm.at[pl.ds(part * PIECE, PIECE), :],
            tokens_ref.at[pl.ds(part * PIECE, PIECE), :],
            sems.at[part],
        )
        for part in range(parts)
    ]
    for copy in copies:
        copy.start()
    copies[0].wait()
    code, _ = slot_codes(ids_ref[...].astype(jnp.float32), resident)
    rows = iota((resident * CAP, row_count), 0)
    dispatch = jnp.where(code == block_codes(rows, resident), 1.0, 0.0).astype(jnp.bfloat16)
    for copy in copies[1:]:
        copy.wait()
    outgoing = jnp.dot(dispatch, tokens_ref[...], preferred_element_type=jnp.float32).astype(
        jnp.bfloat16
    )
    size = resident * CAP // len(out_refs)
    for which, out_ref in enumerate(out_refs):
        out_ref[...] = outgoing[which * size : (which + 1) * size, :]


def prepare(resident, ids_ref, scores_ref, _, *refs):
    weights, (match_ref, weight_ref), held, sems = refs[:3], refs[3:5], refs[5:8], refs[8]
    pieces = [
        pltpu.make_async_copy(
            source.at[:, pl.ds(part * size, size), :],
            target.at[:, pl.ds(part * size, size), :],
            sems.at[which * WEIGHT_PARTS + part],
        )
        for which, (source, target) in enumerate(zip(weights, held))
        for size in [source.shape[1] // WEIGHT_PARTS]
        for part in range(WEIGHT_PARTS)
    ]
    for piece in pieces:
        piece.start()
    ids = ids_ref[...].astype(jnp.float32)
    code, expert = slot_codes(ids, resident)
    wanted = block_codes(iota(match_ref.shape, 1), resident)
    match_ref[...] = jnp.where(to_column(code) == wanted, 1.0, 0.0).astype(jnp.bfloat16)
    squashed = jax.nn.sigmoid(scores_ref[...])
    chosen = jnp.sum(jnp.where(ids == expert, squashed, 0.0), axis=0, keepdims=True)
    weight_ref[...] = to_column(2.5 * chosen / jnp.sum(squashed, axis=0, keepdims=True))
    for piece in pieces:
        piece.wait()


def pack(_, *refs):
    rows = jnp.concatenate([ref[...] for ref in refs[:-1]], axis=0)
    size = rows.shape[0]
    for member in range(refs[-1].shape[0] // size):
        refs[-1][member * size : (member + 1) * size, :] = rows


def lift(chips, own, rows_ref, gate_ref, up_ref):
    part_rows, features = rows_ref.shape[0] // chips, rows_ref.shape[1]
    core = lax.axis_index("core")
    core = core if own else 1 - core
    gate_act = jnp.zeros((part_rows, gate_ref.shape[2]), jnp.float32)
    up_act = jnp.zeros((part_rows, up_ref.shape[2]), jnp.float32)
    for chip in range(chips):
        rows = rows_ref[chip * part_rows : (chip + 1) * part_rows, :]
        columns = pl.ds(pl.multiple_of((2 * chip + core) * features, features), features)
        gate_act += jnp.dot(rows, gate_ref[0, columns, :], preferred_element_type=jnp.float32)
        up_act += jnp.dot(rows, up_ref[0, columns, :], preferred_element_type=jnp.float32)
    return gate_act, up_act


def begin(chips, rows_ref, gate_ref, up_ref, gate_act_ref, up_act_ref):
    gate_act_ref[...], up_act_ref[...] = lift(chips, True, rows_ref, gate_ref, up_ref)


def finish(chips, *refs):
    rows_ref, gate_act_ref, up_act_ref, gate_ref, up_ref, down_ref, mine_ref, other_ref = refs
    part_rows, features = rows_ref.shape[0] // chips, rows_ref.shape[1]
    gate_act, up_act = lift(chips, False, rows_ref, gate_ref, up_ref)
    gate_act += gate_act_ref[...]
    up_act += up_act_ref[...]
    hidden = (gate_act / (1.0 + jnp.exp(-gate_act)) * up_act).astype(jnp.bfloat16)
    core = lax.axis_index("core")
    for out_ref, target in ((other_ref, 1 - core), (mine_ref, core)):
        for chip in range(chips):
            start = pl.multiple_of((2 * chip + target) * features, features)
            out_ref[chip * part_rows : (chip + 1) * part_rows, :] = jnp.dot(
                hidden, down_ref[0, :, pl.ds(start, features)], preferred_element_type=jnp.float32
            ).astype(jnp.bfloat16)


def add(mine_ref, other_ref, out_ref):
    total = mine_ref[...].astype(jnp.float32) + other_ref[...].astype(jnp.float32)
    out_ref[...] = total.astype(jnp.bfloat16)


def total(rows_ref, *out_refs):
    size = out_refs[0].shape[0]
    count = rows_ref.shape[0] // (size * len(out_refs))
    for which, out_ref in enumerate(out_refs):
        summed = jnp.zeros(out_ref.shape, jnp.float32)
        for member in range(count):
            start = (member * len(out_refs) + which) * size
            summed += rows_ref[start : start + size, :].astype(jnp.float32)
        out_ref[...] = summed.astype(jnp.bfloat16)


def combine(match_ref, weight_ref, *refs):
    returned = jnp.concatenate([ref[...] for ref in refs[:-1]], axis=0)
    summed = jnp.dot(match_ref[...], returned, preferred_element_type=jnp.float32)
    refs[-1][...] = (weight_ref[...] * summed).astype(jnp.bfloat16)


def across_experts(blocks, resident):
    if resident == 2:
        return [blocks[0], lax.ppermute(blocks[1], "expert", SWAP)]
    return [lax.all_to_all(blocks[0], "expert", split_axis=0, concat_axis=0, tiled=True)]


def shards(tokens, expert_ids, route_scores, w_gate, w_up, w_down):
    row_count, features = tokens.shape
    top_count, hidden_count = expert_ids.shape[1], w_gate.shape[2]
    resident, chips = lax.axis_size("expert"), lax.axis_size("chip")
    kept = resident * CAP
    members = 2 * chips
    call = lambda kernel, name, out_shape, **rest: pl.pallas_call(
        kernel, out_shape=out_shape, name=name, compiler_params=LIMIT, **rest
    )
    rows_of = lambda count: jax.ShapeDtypeStruct((count, features), jnp.bfloat16)
    blocks_shape = (rows_of(CAP),) * 2 if resident == 2 else (rows_of(kept),)
    ids, scores = expert_ids.T, route_scores.T
    far = lambda value: pltpu.with_memory_space_constraint(value, pltpu.HBM)
    hbm = pl.BlockSpec(memory_space=pltpu.HBM)

    outgoing = call(
        lambda *refs: route(resident, *refs),
        "route",
        blocks_shape,
        in_specs=[hbm] * 2,
        scratch_shapes=[
            pltpu.VMEM((top_count, row_count), jnp.int32),
            pltpu.VMEM((row_count, features), jnp.bfloat16),
            pltpu.SemaphoreType.DMA((row_count // PIECE + 1,)),
        ],
    )(far(ids), far(tokens))
    weights = (w_gate, w_up, w_down)
    vmem = pl.BlockSpec(memory_space=pltpu.VMEM)
    match, weight, *held = call(
        lambda *refs: prepare(resident, *refs),
        "prepare",
        (
            jax.ShapeDtypeStruct((row_count, kept), jnp.bfloat16),
            jax.ShapeDtypeStruct((row_count, 1), jnp.float32),
        )
        + tuple(jax.ShapeDtypeStruct(value.shape, value.dtype) for value in weights),
        in_specs=[vmem] * 2 + [pl.BlockSpec(memory_space=pl.ANY)] + [hbm] * 3,
        scratch_shapes=[pltpu.SemaphoreType.DMA((3 * WEIGHT_PARTS,))],
        cost_estimate=pl.CostEstimate(
            flops=0, bytes_accessed=2 * sum(value.nbytes for value in weights), transcendentals=0
        ),
    )(ids, scores, outgoing[0], *(far(value) for value in weights))
    arrived = across_experts(outgoing, resident)
    packed = call(
        pack,
        "pack",
        rows_of(members * kept),
        in_specs=[pl.BlockSpec(memory_space=pl.ANY)] + [vmem] * len(arrived),
    )(weight, *arrived)
    incoming = lax.all_to_all(packed, NEAR, split_axis=0, concat_axis=0, tiled=True)
    across = lax.ppermute(incoming, "core", SWAP)
    acts = (jax.ShapeDtypeStruct((2 * kept, hidden_count), jnp.float32),) * 2
    begun = call(lambda *refs: begin(chips, *refs), "begin", acts)(incoming, held[0], held[1])
    mine, other = call(
        lambda *refs: finish(chips, *refs), "finish", (rows_of(members * kept),) * 2
    )(across, *begun, *held)
    summed = call(add, "add", rows_of(members * kept))(mine, lax.ppermute(other, "core", SWAP))
    returned = lax.all_to_all(summed, NEAR, split_axis=0, concat_axis=0, tiled=True)
    blocks = call(total, "total", blocks_shape)(returned)
    return call(combine, "combine", rows_of(row_count))(
        match, weight, *across_experts(blocks, resident)
    )


def solution(mesh):
    groups, ep_count, tp_count = (mesh.shape[name] for name in ("groups", "ep", "tp"))
    split = jax.sharding.Mesh(
        mesh.devices.reshape(groups, ep_count // 2, 2, tp_count // 2, 2),
        ("groups", "expert", "half", "chip", "core"),
    )
    ep, tp = ("expert", "half"), ("chip", "core")
    placed = (
        P(("groups", *ep), tp),
        P(("groups", *ep), None),
        P(("groups", *ep), None),
        P(ep, None, tp),
        P(ep, None, tp),
        P(ep, tp, None),
    )
    return jax.shard_map(
        shards, mesh=split, in_specs=placed, out_specs=P(("groups", *ep), tp), check_vma=False
    )
```

```python
import jax
import jax.numpy as jnp
from jax import lax
from jax.experimental import pallas as pl
from jax.experimental.pallas import tpu as pltpu
from jax.sharding import PartitionSpec as P

CAP = 8
PIECE = 32
FAR = ("chip", "ep")
SWAP = [(0, 1), (1, 0)]
LIMIT = pltpu.CompilerParams(vmem_limit_bytes=16 * 1024 * 1024)


def iota(shape, dim):
    return lax.broadcasted_iota(jnp.int32, shape, dim)


def to_column(row):
    size = row.shape[1]
    square = (size, size)
    return jnp.sum(jnp.where(iota(square, 0) == iota(square, 1), row, 0.0), axis=1, keepdims=True)


def slot_codes(ids, resident):
    row_count = ids.shape[1]
    expert = jnp.min(ids, axis=0, keepdims=True)
    onehot_shape = (-(-resident // 16) * 16, row_count)
    onehot = jnp.where(expert == iota(onehot_shape, 0).astype(jnp.float32), 1.0, 0.0)
    square = (row_count, row_count)
    earlier = jnp.where(iota(square, 0) < iota(square, 1), 1.0, 0.0).astype(jnp.bfloat16)
    counts = jnp.dot(onehot.astype(jnp.bfloat16), earlier, preferred_element_type=jnp.float32)
    return expert * CAP + jnp.sum(counts * onehot, axis=0, keepdims=True), expert


def row_codes(index, ep_count):
    index = lax.rem(index, ep_count * CAP)
    return ((index // (2 * CAP)) * CAP + lax.rem(index, CAP)).astype(jnp.float32)


def route(ep_count, ids_hbm, tokens_hbm, outgoing_ref, ids_ref, tokens_ref, sems):
    row_count = ids_ref.shape[1]
    parts = row_count // PIECE
    copies = [pltpu.make_async_copy(ids_hbm, ids_ref, sems.at[parts])] + [
        pltpu.make_async_copy(
            tokens_hbm.at[pl.ds(part * PIECE, PIECE), :],
            tokens_ref.at[pl.ds(part * PIECE, PIECE), :],
            sems.at[part],
        )
        for part in range(parts)
    ]
    for copy in copies:
        copy.start()
    copies[0].wait()
    code, _ = slot_codes(ids_ref[...].astype(jnp.float32), ep_count // 2)
    wanted = row_codes(iota((outgoing_ref.shape[0], row_count), 0), ep_count)
    dispatch = jnp.where(code == wanted, 1.0, 0.0).astype(jnp.bfloat16)
    for copy in copies[1:]:
        copy.wait()
    outgoing_ref[...] = jnp.dot(
        dispatch, tokens_ref[...], preferred_element_type=jnp.float32
    ).astype(jnp.bfloat16)


def score(ep_count, ids_ref, scores_ref, _, match_ref, weight_ref):
    ids = ids_ref[...].astype(jnp.float32)
    code, expert = slot_codes(ids, ep_count // 2)
    wanted = row_codes(iota(match_ref.shape, 1), ep_count)
    match_ref[...] = jnp.where(to_column(code) == wanted, 1.0, 0.0).astype(jnp.bfloat16)
    squashed = jax.nn.sigmoid(scores_ref[...])
    chosen = jnp.sum(jnp.where(ids == expert, squashed, 0.0), axis=0, keepdims=True)
    weight_ref[...] = to_column(2.5 * chosen / jnp.sum(squashed, axis=0, keepdims=True))


def lift(chips, own, rows_ref, gate_ref, up_ref):
    part_rows, features = rows_ref.shape[0] // chips, rows_ref.shape[1]
    core = lax.axis_index("core")
    core = core if own else 1 - core
    gate_act = jnp.zeros((part_rows, gate_ref.shape[2]), jnp.float32)
    up_act = jnp.zeros((part_rows, up_ref.shape[2]), jnp.float32)
    for chip in range(chips):
        rows = rows_ref[chip * part_rows : (chip + 1) * part_rows, :]
        columns = pl.ds(pl.multiple_of((2 * chip + core) * features, features), features)
        gate_act += jnp.dot(rows, gate_ref[0, columns, :], preferred_element_type=jnp.float32)
        up_act += jnp.dot(rows, up_ref[0, columns, :], preferred_element_type=jnp.float32)
    return gate_act, up_act


def lower(chips, own, hidden, down_ref, out_ref):
    part_rows, features = out_ref.shape[0] // chips, out_ref.shape[1]
    core = lax.axis_index("core")
    core = core if own else 1 - core
    for chip in range(chips):
        columns = pl.ds(pl.multiple_of((2 * chip + core) * features, features), features)
        out_ref[chip * part_rows : (chip + 1) * part_rows, :] = jnp.dot(
            hidden, down_ref[0, :, columns], preferred_element_type=jnp.float32
        ).astype(jnp.bfloat16)


def begin(chips, rows_ref, gate_ref, up_ref, gate_act_ref, up_act_ref):
    gate_act_ref[...], up_act_ref[...] = lift(chips, True, rows_ref, gate_ref, up_ref)


def theirs(chips, *refs):
    rows_ref, gate_act_ref, up_act_ref, gate_ref, up_ref, down_ref, hidden_ref, other_ref = refs
    gate_act, up_act = lift(chips, False, rows_ref, gate_ref, up_ref)
    gate_act += gate_act_ref[...]
    up_act += up_act_ref[...]
    hidden = (gate_act / (1.0 + jnp.exp(-gate_act)) * up_act).astype(jnp.bfloat16)
    hidden_ref[...] = hidden
    lower(chips, False, hidden, down_ref, other_ref)


def ours(chips, hidden_ref, down_ref, mine_ref):
    lower(chips, True, hidden_ref[...], down_ref, mine_ref)


def add(mine_ref, other_ref, out_ref):
    total = mine_ref[...].astype(jnp.float32) + other_ref[...].astype(jnp.float32)
    out_ref[...] = total.astype(jnp.bfloat16)


def combine(match_ref, weight_ref, returned_ref, out_hbm, out_ref, sems):
    copies = []
    for part in range(out_ref.shape[0] // PIECE):
        rows = pl.ds(part * PIECE, PIECE)
        summed = jnp.dot(match_ref[rows, :], returned_ref[...], preferred_element_type=jnp.float32)
        out_ref[rows, :] = (weight_ref[rows, :] * summed).astype(jnp.bfloat16)
        copies.append(pltpu.make_async_copy(out_ref.at[rows, :], out_hbm.at[rows, :], sems.at[part]))
        copies[-1].start()
    for copy in copies:
        copy.wait()


def shards(tokens, expert_ids, route_scores, w_gate, w_up, w_down):
    row_count, features = tokens.shape
    top_count, hidden_count = expert_ids.shape[1], w_gate.shape[2]
    ep_count, chips = lax.axis_size("ep"), lax.axis_size("chip")
    slot_count = ep_count * CAP
    half = jax.ShapeDtypeStruct((chips * slot_count, features), jnp.bfloat16)
    ids, scores = expert_ids.T, route_scores.T
    hbm, vmem = (pl.BlockSpec(memory_space=space) for space in (pltpu.HBM, pltpu.VMEM))
    anywhere = pl.BlockSpec(memory_space=pl.ANY)

    def call(kernel, name, out_shape, **rest):
        return pl.pallas_call(kernel, out_shape=out_shape, name=name, compiler_params=LIMIT, **rest)

    outgoing = call(
        lambda *refs: route(ep_count, *refs),
        "route",
        half,
        in_specs=[hbm] * 2,
        scratch_shapes=[
            pltpu.VMEM((top_count, row_count), jnp.int32),
            pltpu.VMEM((row_count, features), jnp.bfloat16),
            pltpu.SemaphoreType.DMA((row_count // PIECE + 1,)),
        ],
        cost_estimate=pl.CostEstimate(flops=2 * 10**9, bytes_accessed=0, transcendentals=0),
    )(*(pltpu.with_memory_space_constraint(value, pltpu.HBM) for value in (ids, tokens)))
    incoming = lax.all_to_all(outgoing, FAR, split_axis=0, concat_axis=0, tiled=True)
    across = lax.ppermute(incoming, "core", SWAP)
    acts = (jax.ShapeDtypeStruct((slot_count, hidden_count), jnp.float32),) * 2
    begun = call(lambda *refs: begin(chips, *refs), "begin", acts)(incoming, w_gate, w_up)
    hidden_shape = jax.ShapeDtypeStruct((slot_count, hidden_count), jnp.bfloat16)
    hidden, other = call(lambda *refs: theirs(chips, *refs), "theirs", (hidden_shape, half))(
        across, *begun, w_gate, w_up, w_down
    )
    crossed = lax.ppermute(other, "core", SWAP)
    mine = call(lambda *refs: ours(chips, *refs), "ours", half)(hidden, w_down)
    match, weight = call(
        lambda *refs: score(ep_count, *refs),
        "score",
        (
            jax.ShapeDtypeStruct((row_count, chips * slot_count), jnp.bfloat16),
            jax.ShapeDtypeStruct((row_count, 1), jnp.float32),
        ),
        in_specs=[vmem] * 2 + [anywhere],
    )(ids, scores, other)
    summed = call(add, "add", half)(mine, crossed)
    returned = lax.all_to_all(summed, FAR, split_axis=0, concat_axis=0, tiled=True)
    return call(
        combine,
        "combine",
        jax.ShapeDtypeStruct((row_count, features), jnp.bfloat16),
        out_specs=hbm,
        scratch_shapes=[
            pltpu.VMEM((row_count, features), jnp.bfloat16),
            pltpu.SemaphoreType.DMA((row_count // PIECE,)),
        ],
    )(match, weight, returned)


def solution(mesh):
    groups, ep_count, tp_count = (mesh.shape[name] for name in ("groups", "ep", "tp"))
    split = jax.sharding.Mesh(
        mesh.devices.reshape(groups, ep_count, tp_count // 2, 2), ("groups", "ep", "chip", "core")
    )
    tp = ("chip", "core")
    placed = (
        P(("groups", "ep"), tp),
        P(("groups", "ep"), None),
        P(("groups", "ep"), None),
        P("ep", None, tp),
        P("ep", None, tp),
        P("ep", tp, None),
    )
    return jax.shard_map(
        shards, mesh=split, in_specs=placed, out_specs=P(("groups", "ep"), tp), check_vma=False
    )
```

```python
import jax
import jax.numpy as jnp
from jax import lax
from jax.experimental import pallas as pl
from jax.experimental.pallas import tpu as pltpu
from jax.sharding import PartitionSpec as P

CAP = 8
PIECE = 32
FAR = ("chip", "ep")
SWAP = [(0, 1), (1, 0)]
LIMIT = pltpu.CompilerParams(vmem_limit_bytes=16 * 1024 * 1024)


def iota(shape, dim):
    return lax.broadcasted_iota(jnp.int32, shape, dim)


def to_column(row):
    size = row.shape[1]
    square = (size, size)
    return jnp.sum(jnp.where(iota(square, 0) == iota(square, 1), row, 0.0), axis=1, keepdims=True)


def slot_codes(ids, resident):
    row_count = ids.shape[1]
    expert = jnp.min(ids, axis=0, keepdims=True)
    onehot_shape = (-(-resident // 16) * 16, row_count)
    onehot = jnp.where(expert == iota(onehot_shape, 0).astype(jnp.float32), 1.0, 0.0)
    square = (row_count, row_count)
    earlier = jnp.where(iota(square, 0) < iota(square, 1), 1.0, 0.0).astype(jnp.bfloat16)
    counts = jnp.dot(onehot.astype(jnp.bfloat16), earlier, preferred_element_type=jnp.float32)
    return expert * CAP + jnp.sum(counts * onehot, axis=0, keepdims=True), expert


def row_codes(index, ep_count):
    index = lax.rem(index, ep_count * CAP)
    return ((index // (2 * CAP)) * CAP + lax.rem(index, CAP)).astype(jnp.float32)


def route(ep_count, ids_hbm, tokens_hbm, outgoing_ref, ids_ref, tokens_ref, sems):
    row_count = ids_ref.shape[1]
    parts = row_count // PIECE
    copies = [pltpu.make_async_copy(ids_hbm, ids_ref, sems.at[parts])] + [
        pltpu.make_async_copy(
            tokens_hbm.at[pl.ds(part * PIECE, PIECE), :],
            tokens_ref.at[pl.ds(part * PIECE, PIECE), :],
            sems.at[part],
        )
        for part in range(parts)
    ]
    for copy in copies:
        copy.start()
    copies[0].wait()
    code, _ = slot_codes(ids_ref[...].astype(jnp.float32), ep_count // 2)
    wanted = row_codes(iota((outgoing_ref.shape[0], row_count), 0), ep_count)
    dispatch = jnp.where(code == wanted, 1.0, 0.0).astype(jnp.bfloat16)
    for copy in copies[1:]:
        copy.wait()
    outgoing_ref[...] = jnp.dot(
        dispatch, tokens_ref[...], preferred_element_type=jnp.float32
    ).astype(jnp.bfloat16)


def score(ep_count, ids_ref, scores_ref, _, match_ref, weight_ref):
    ids = ids_ref[...].astype(jnp.float32)
    code, expert = slot_codes(ids, ep_count // 2)
    wanted = row_codes(iota(match_ref.shape, 1), ep_count)
    match_ref[...] = jnp.where(to_column(code) == wanted, 1.0, 0.0).astype(jnp.bfloat16)
    squashed = jax.nn.sigmoid(scores_ref[...])
    chosen = jnp.sum(jnp.where(ids == expert, squashed, 0.0), axis=0, keepdims=True)
    weight_ref[...] = to_column(2.5 * chosen / jnp.sum(squashed, axis=0, keepdims=True))


def lift(chips, own, rows_ref, gate_ref, up_ref):
    part_rows, features = rows_ref.shape[0] // chips, rows_ref.shape[1]
    core = lax.axis_index("core")
    core = core if own else 1 - core
    gate_act = jnp.zeros((part_rows, gate_ref.shape[2]), jnp.float32)
    up_act = jnp.zeros((part_rows, up_ref.shape[2]), jnp.float32)
    for chip in range(chips):
        rows = rows_ref[chip * part_rows : (chip + 1) * part_rows, :]
        columns = pl.ds(pl.multiple_of((2 * chip + core) * features, features), features)
        gate_act += jnp.dot(rows, gate_ref[0, columns, :], preferred_element_type=jnp.float32)
        up_act += jnp.dot(rows, up_ref[0, columns, :], preferred_element_type=jnp.float32)
    return gate_act, up_act


def lower(chips, own, hidden, down_ref, out_ref):
    part_rows, features = out_ref.shape[0] // chips, out_ref.shape[1]
    core = lax.axis_index("core")
    core = core if own else 1 - core
    for chip in range(chips):
        columns = pl.ds(pl.multiple_of((2 * chip + core) * features, features), features)
        out_ref[chip * part_rows : (chip + 1) * part_rows, :] = jnp.dot(
            hidden, down_ref[0, :, columns], preferred_element_type=jnp.float32
        ).astype(jnp.bfloat16)


def begin(chips, rows_ref, gate_ref, up_ref, gate_act_ref, up_act_ref):
    gate_act_ref[...], up_act_ref[...] = lift(chips, True, rows_ref, gate_ref, up_ref)


def theirs(chips, *refs):
    rows_ref, gate_act_ref, up_act_ref, gate_ref, up_ref, down_ref, hidden_ref, other_ref = refs
    gate_act, up_act = lift(chips, False, rows_ref, gate_ref, up_ref)
    gate_act += gate_act_ref[...]
    up_act += up_act_ref[...]
    hidden = (gate_act / (1.0 + jnp.exp(-gate_act)) * up_act).astype(jnp.bfloat16)
    hidden_ref[...] = hidden
    lower(chips, False, hidden, down_ref, other_ref)


def ours(chips, hidden_ref, down_ref, mine_ref):
    lower(chips, True, hidden_ref[...], down_ref, mine_ref)


def add(mine_ref, other_ref, _, out_ref):
    total = mine_ref[...].astype(jnp.float32) + other_ref[...].astype(jnp.float32)
    out_ref[...] = total.astype(jnp.bfloat16)


def combine(match_ref, weight_ref, returned_ref, out_hbm, out_ref, sems):
    copies = []
    for part in range(out_ref.shape[0] // PIECE):
        rows = pl.ds(part * PIECE, PIECE)
        summed = jnp.dot(match_ref[rows, :], returned_ref[...], preferred_element_type=jnp.float32)
        out_ref[rows, :] = (weight_ref[rows, :] * summed).astype(jnp.bfloat16)
        copies.append(pltpu.make_async_copy(out_ref.at[rows, :], out_hbm.at[rows, :], sems.at[part]))
        copies[-1].start()
    for copy in copies:
        copy.wait()


def shards(tokens, expert_ids, route_scores, w_gate, w_up, w_down):
    row_count, features = tokens.shape
    top_count, hidden_count = expert_ids.shape[1], w_gate.shape[2]
    ep_count, chips = lax.axis_size("ep"), lax.axis_size("chip")
    slot_count = ep_count * CAP
    half = jax.ShapeDtypeStruct((chips * slot_count, features), jnp.bfloat16)
    ids, scores = expert_ids.T, route_scores.T
    hbm, vmem = (pl.BlockSpec(memory_space=space) for space in (pltpu.HBM, pltpu.VMEM))
    anywhere = pl.BlockSpec(memory_space=pl.ANY)

    def call(kernel, name, out_shape, **rest):
        return pl.pallas_call(kernel, out_shape=out_shape, name=name, compiler_params=LIMIT, **rest)

    outgoing = call(
        lambda *refs: route(ep_count, *refs),
        "route",
        half,
        in_specs=[hbm] * 2,
        scratch_shapes=[
            pltpu.VMEM((top_count, row_count), jnp.int32),
            pltpu.VMEM((row_count, features), jnp.bfloat16),
            pltpu.SemaphoreType.DMA((row_count // PIECE + 1,)),
        ],
        cost_estimate=pl.CostEstimate(flops=2 * 10**9, bytes_accessed=0, transcendentals=0),
    )(*(pltpu.with_memory_space_constraint(value, pltpu.HBM) for value in (ids, tokens)))
    incoming = lax.all_to_all(outgoing, FAR, split_axis=0, concat_axis=0, tiled=True)
    across = lax.ppermute(incoming, "core", SWAP)
    acts = (jax.ShapeDtypeStruct((slot_count, hidden_count), jnp.float32),) * 2
    begun = call(lambda *refs: begin(chips, *refs), "begin", acts)(incoming, w_gate, w_up)
    hidden_shape = jax.ShapeDtypeStruct((slot_count, hidden_count), jnp.bfloat16)
    hidden, other = call(lambda *refs: theirs(chips, *refs), "theirs", (hidden_shape, half))(
        across, *begun, w_gate, w_up, w_down
    )
    crossed = lax.ppermute(other, "core", SWAP)
    mine = call(lambda *refs: ours(chips, *refs), "ours", half)(hidden, w_down)
    match, weight = call(
        lambda *refs: score(ep_count, *refs),
        "score",
        (
            jax.ShapeDtypeStruct((row_count, chips * slot_count), jnp.bfloat16),
            jax.ShapeDtypeStruct((row_count, 1), jnp.float32),
        ),
        in_specs=[vmem] * 2 + [anywhere],
    )(ids, scores, other)
    summed = call(add, "add", half, in_specs=[vmem] * 2 + [anywhere])(mine, crossed, weight)
    returned = lax.all_to_all(summed, FAR, split_axis=0, concat_axis=0, tiled=True)
    return call(
        combine,
        "combine",
        jax.ShapeDtypeStruct((row_count, features), jnp.bfloat16),
        out_specs=hbm,
        scratch_shapes=[
            pltpu.VMEM((row_count, features), jnp.bfloat16),
            pltpu.SemaphoreType.DMA((row_count // PIECE,)),
        ],
    )(match, weight, returned)


def solution(mesh):
    groups, ep_count, tp_count = (mesh.shape[name] for name in ("groups", "ep", "tp"))
    split = jax.sharding.Mesh(
        mesh.devices.reshape(groups, ep_count, tp_count // 2, 2), ("groups", "ep", "chip", "core")
    )
    tp = ("chip", "core")
    placed = (
        P(("groups", "ep"), tp),
        P(("groups", "ep"), None),
        P(("groups", "ep"), None),
        P("ep", None, tp),
        P("ep", None, tp),
        P("ep", tp, None),
    )
    return jax.shard_map(
        shards, mesh=split, in_specs=placed, out_specs=P(("groups", "ep"), tp), check_vma=False
    )
```

```python
import jax
import jax.numpy as jnp
from jax import lax
from jax.experimental import pallas as pl
from jax.experimental.pallas import tpu as pltpu
from jax.sharding import PartitionSpec as P

CAP = 8
PIECE = 32
FAR = ("ep", "chip", "core")
SWAP = [(0, 1), (1, 0)]
LIMIT = pltpu.CompilerParams(vmem_limit_bytes=16 * 1024 * 1024)


def iota(shape, dim):
    return lax.broadcasted_iota(jnp.int32, shape, dim)


def to_column(row):
    size = row.shape[1]
    square = (size, size)
    return jnp.sum(jnp.where(iota(square, 0) == iota(square, 1), row, 0.0), axis=1, keepdims=True)


def slot_codes(ids, resident):
    row_count = ids.shape[1]
    expert = jnp.min(ids, axis=0, keepdims=True)
    onehot_shape = (-(-resident // 16) * 16, row_count)
    onehot = jnp.where(expert == iota(onehot_shape, 0).astype(jnp.float32), 1.0, 0.0)
    square = (row_count, row_count)
    earlier = jnp.where(iota(square, 0) < iota(square, 1), 1.0, 0.0).astype(jnp.bfloat16)
    counts = jnp.dot(onehot.astype(jnp.bfloat16), earlier, preferred_element_type=jnp.float32)
    return expert * CAP + jnp.sum(counts * onehot, axis=0, keepdims=True), expert


def row_codes(index, ep_count):
    index = lax.rem(index, ep_count * CAP)
    return ((index // (2 * CAP)) * CAP + lax.rem(index, CAP)).astype(jnp.float32)


def route(ep_count, ids_hbm, tokens_hbm, outgoing_ref, ids_ref, tokens_ref, sems):
    row_count = ids_ref.shape[1]
    parts = row_count // PIECE
    copies = [pltpu.make_async_copy(ids_hbm, ids_ref, sems.at[parts])] + [
        pltpu.make_async_copy(
            tokens_hbm.at[pl.ds(part * PIECE, PIECE), :],
            tokens_ref.at[pl.ds(part * PIECE, PIECE), :],
            sems.at[part],
        )
        for part in range(parts)
    ]
    for copy in copies:
        copy.start()
    copies[0].wait()
    code, _ = slot_codes(ids_ref[...].astype(jnp.float32), ep_count // 2)
    wanted = row_codes(iota((outgoing_ref.shape[0], row_count), 0), ep_count)
    dispatch = jnp.where(code == wanted, 1.0, 0.0).astype(jnp.bfloat16)
    for copy in copies[1:]:
        copy.wait()
    outgoing_ref[...] = jnp.dot(
        dispatch, tokens_ref[...], preferred_element_type=jnp.float32
    ).astype(jnp.bfloat16)


def score(ep_count, ids_ref, scores_ref, _, match_ref, weight_ref):
    ids = ids_ref[...].astype(jnp.float32)
    code, expert = slot_codes(ids, ep_count // 2)
    wanted = row_codes(iota(match_ref.shape, 1), ep_count)
    match_ref[...] = jnp.where(to_column(code) == wanted, 1.0, 0.0).astype(jnp.bfloat16)
    squashed = jax.nn.sigmoid(scores_ref[...])
    chosen = jnp.sum(jnp.where(ids == expert, squashed, 0.0), axis=0, keepdims=True)
    weight_ref[...] = to_column(2.5 * chosen / jnp.sum(squashed, axis=0, keepdims=True))


def far_groups(ep_count, chips):
    return [
        [(z * chips + x) * 2 + (side + x) % 2 for x in range(chips) for z in range(ep_count)]
        for side in range(2)
    ]


def columns_of(chip, own, features):
    core = lax.rem(lax.axis_index("core") + lax.axis_index("chip") + chip + (0 if own else 1), 2)
    return pl.ds(pl.multiple_of((2 * chip + core) * features, features), features)


def lift(chips, own, rows_ref, gate_ref, up_ref):
    part_rows, features = rows_ref.shape[0] // chips, rows_ref.shape[1]
    gate_act = jnp.zeros((part_rows, gate_ref.shape[2]), jnp.float32)
    up_act = jnp.zeros((part_rows, up_ref.shape[2]), jnp.float32)
    for chip in range(chips):
        rows = rows_ref[chip * part_rows : (chip + 1) * part_rows, :]
        columns = columns_of(chip, own, features)
        gate_act += jnp.dot(rows, gate_ref[0, columns, :], preferred_element_type=jnp.float32)
        up_act += jnp.dot(rows, up_ref[0, columns, :], preferred_element_type=jnp.float32)
    return gate_act, up_act


def lower(chips, own, hidden, down_ref, out_ref):
    part_rows, features = out_ref.shape[0] // chips, out_ref.shape[1]
    for chip in range(chips):
        columns = columns_of(chip, own, features)
        out_ref[chip * part_rows : (chip + 1) * part_rows, :] = jnp.dot(
            hidden, down_ref[0, :, columns], preferred_element_type=jnp.float32
        ).astype(jnp.bfloat16)


def begin(chips, rows_ref, gate_ref, up_ref, gate_act_ref, up_act_ref):
    gate_act_ref[...], up_act_ref[...] = lift(chips, True, rows_ref, gate_ref, up_ref)


def theirs(chips, *refs):
    rows_ref, gate_act_ref, up_act_ref, gate_ref, up_ref, down_ref, hidden_ref, other_ref = refs
    gate_act, up_act = lift(chips, False, rows_ref, gate_ref, up_ref)
    gate_act += gate_act_ref[...]
    up_act += up_act_ref[...]
    hidden = (gate_act / (1.0 + jnp.exp(-gate_act)) * up_act).astype(jnp.bfloat16)
    hidden_ref[...] = hidden
    lower(chips, False, hidden, down_ref, other_ref)


def ours(chips, hidden_ref, down_ref, mine_ref):
    lower(chips, True, hidden_ref[...], down_ref, mine_ref)


def add(mine_ref, other_ref, _, out_ref):
    total = mine_ref[...].astype(jnp.float32) + other_ref[...].astype(jnp.float32)
    out_ref[...] = total.astype(jnp.bfloat16)


def combine(match_ref, weight_ref, returned_ref, out_hbm, out_ref, sems):
    copies = []
    for part in range(out_ref.shape[0] // PIECE):
        rows = pl.ds(part * PIECE, PIECE)
        summed = jnp.dot(match_ref[rows, :], returned_ref[...], preferred_element_type=jnp.float32)
        out_ref[rows, :] = (weight_ref[rows, :] * summed).astype(jnp.bfloat16)
        copies.append(pltpu.make_async_copy(out_ref.at[rows, :], out_hbm.at[rows, :], sems.at[part]))
        copies[-1].start()
    for copy in copies:
        copy.wait()


def shards(tokens, expert_ids, route_scores, w_gate, w_up, w_down):
    row_count, features = tokens.shape
    top_count, hidden_count = expert_ids.shape[1], w_gate.shape[2]
    ep_count, chips = lax.axis_size("ep"), lax.axis_size("chip")
    slot_count = ep_count * CAP
    half = jax.ShapeDtypeStruct((chips * slot_count, features), jnp.bfloat16)
    ids, scores = expert_ids.T, route_scores.T
    hbm, vmem = (pl.BlockSpec(memory_space=space) for space in (pltpu.HBM, pltpu.VMEM))
    anywhere = pl.BlockSpec(memory_space=pl.ANY)

    def exchange(rows):
        groups = far_groups(ep_count, chips)
        return lax.all_to_all(rows, FAR, 0, 0, axis_index_groups=groups, tiled=True)

    def call(kernel, name, out_shape, **rest):
        return pl.pallas_call(kernel, out_shape=out_shape, name=name, compiler_params=LIMIT, **rest)

    outgoing = call(
        lambda *refs: route(ep_count, *refs),
        "route",
        half,
        in_specs=[hbm] * 2,
        scratch_shapes=[
            pltpu.VMEM((top_count, row_count), jnp.int32),
            pltpu.VMEM((row_count, features), jnp.bfloat16),
            pltpu.SemaphoreType.DMA((row_count // PIECE + 1,)),
        ],
        cost_estimate=pl.CostEstimate(flops=2 * 10**9, bytes_accessed=0, transcendentals=0),
    )(*(pltpu.with_memory_space_constraint(value, pltpu.HBM) for value in (ids, tokens)))
    incoming = exchange(outgoing)
    across = lax.ppermute(incoming, "core", SWAP)
    acts = (jax.ShapeDtypeStruct((slot_count, hidden_count), jnp.float32),) * 2
    begun = call(lambda *refs: begin(chips, *refs), "begin", acts)(incoming, w_gate, w_up)
    hidden_shape = jax.ShapeDtypeStruct((slot_count, hidden_count), jnp.bfloat16)
    hidden, other = call(lambda *refs: theirs(chips, *refs), "theirs", (hidden_shape, half))(
        across, *begun, w_gate, w_up, w_down
    )
    crossed = lax.ppermute(other, "core", SWAP)
    mine = call(lambda *refs: ours(chips, *refs), "ours", half)(hidden, w_down)
    match, weight = call(
        lambda *refs: score(ep_count, *refs),
        "score",
        (
            jax.ShapeDtypeStruct((row_count, chips * slot_count), jnp.bfloat16),
            jax.ShapeDtypeStruct((row_count, 1), jnp.float32),
        ),
        in_specs=[vmem] * 2 + [anywhere],
    )(ids, scores, other)
    summed = call(add, "add", half, in_specs=[vmem] * 2 + [anywhere])(mine, crossed, weight)
    returned = exchange(summed)
    return call(
        combine,
        "combine",
        jax.ShapeDtypeStruct((row_count, features), jnp.bfloat16),
        out_specs=hbm,
        scratch_shapes=[
            pltpu.VMEM((row_count, features), jnp.bfloat16),
            pltpu.SemaphoreType.DMA((row_count // PIECE,)),
        ],
    )(match, weight, returned)


def solution(mesh):
    groups, ep_count, tp_count = (mesh.shape[name] for name in ("groups", "ep", "tp"))
    split = jax.sharding.Mesh(
        mesh.devices.reshape(groups, ep_count, tp_count // 2, 2), ("groups", "ep", "chip", "core")
    )
    tp = ("chip", "core")
    placed = (
        P(("groups", "ep"), tp),
        P(("groups", "ep"), None),
        P(("groups", "ep"), None),
        P("ep", None, tp),
        P("ep", None, tp),
        P("ep", tp, None),
    )
    return jax.shard_map(
        shards, mesh=split, in_specs=placed, out_specs=P(("groups", "ep"), tp), check_vma=False
    )
```

```python
import jax
import jax.numpy as jnp
from jax import lax
from jax.experimental import pallas as pl
from jax.experimental.pallas import tpu as pltpu
from jax.sharding import PartitionSpec as P

CAP = 8
PIECE = 32
FAR = ("ep", "chip", "core")
SWAP = [(0, 1), (1, 0)]
LIMIT = pltpu.CompilerParams(vmem_limit_bytes=16 * 1024 * 1024)


def iota(shape, dim):
    return lax.broadcasted_iota(jnp.int32, shape, dim)


def to_column(row):
    size = row.shape[1]
    square = (size, size)
    return jnp.sum(jnp.where(iota(square, 0) == iota(square, 1), row, 0.0), axis=1, keepdims=True)


def slot_codes(ids, resident):
    row_count = ids.shape[1]
    expert = jnp.min(ids, axis=0, keepdims=True)
    onehot_shape = (-(-resident // 16) * 16, row_count)
    onehot = jnp.where(expert == iota(onehot_shape, 0).astype(jnp.float32), 1.0, 0.0)
    square = (row_count, row_count)
    earlier = jnp.where(iota(square, 0) < iota(square, 1), 1.0, 0.0).astype(jnp.bfloat16)
    counts = jnp.dot(onehot.astype(jnp.bfloat16), earlier, preferred_element_type=jnp.float32)
    return expert * CAP + jnp.sum(counts * onehot, axis=0, keepdims=True), expert


def row_codes(index, ep_count):
    index = lax.rem(index, ep_count * CAP)
    return ((index // (2 * CAP)) * CAP + lax.rem(index, CAP)).astype(jnp.float32)


def route(ep_count, ids_hbm, tokens_hbm, outgoing_ref, ids_ref, tokens_ref, sems):
    row_count = ids_ref.shape[1]
    parts = row_count // PIECE
    copies = [pltpu.make_async_copy(ids_hbm, ids_ref, sems.at[parts])] + [
        pltpu.make_async_copy(
            tokens_hbm.at[pl.ds(part * PIECE, PIECE), :],
            tokens_ref.at[pl.ds(part * PIECE, PIECE), :],
            sems.at[part],
        )
        for part in range(parts)
    ]
    for copy in copies:
        copy.start()
    copies[0].wait()
    code, _ = slot_codes(ids_ref[...].astype(jnp.float32), ep_count // 2)
    wanted = row_codes(iota((outgoing_ref.shape[0], row_count), 0), ep_count)
    dispatch = jnp.where(code == wanted, 1.0, 0.0).astype(jnp.bfloat16)
    for copy in copies[1:]:
        copy.wait()
    outgoing_ref[...] = jnp.dot(
        dispatch, tokens_ref[...], preferred_element_type=jnp.float32
    ).astype(jnp.bfloat16)


def score(ep_count, ids_ref, scores_ref, _, match_ref, weight_ref):
    ids = ids_ref[...].astype(jnp.float32)
    code, expert = slot_codes(ids, ep_count // 2)
    wanted = row_codes(iota(match_ref.shape, 1), ep_count)
    match_ref[...] = jnp.where(to_column(code) == wanted, 1.0, 0.0).astype(jnp.bfloat16)
    squashed = jax.nn.sigmoid(scores_ref[...])
    chosen = jnp.sum(jnp.where(ids == expert, squashed, 0.0), axis=0, keepdims=True)
    weight_ref[...] = to_column(2.5 * chosen / jnp.sum(squashed, axis=0, keepdims=True))


def far_groups(ep_count, chips):
    return [
        [(z * chips + x) * 2 + (side + x) % 2 for x in range(chips) for z in range(ep_count)]
        for side in range(2)
    ]


def columns_of(chip, features):
    core = lax.rem(lax.axis_index("core") + lax.axis_index("chip") + chip, 2)
    return pl.ds(pl.multiple_of((2 * chip + core) * features, features), features)


def lift(chips, rows_ref, *refs):
    weights, acts_ref = refs[:4], refs[4]
    part_rows, features = rows_ref.shape[0] // chips, rows_ref.shape[1]
    width = 2 * weights[0].shape[2]
    for pair in range(2):
        acts = jnp.zeros((part_rows, width), jnp.float32)
        for chip in range(chips):
            rows = rows_ref[chip * part_rows : (chip + 1) * part_rows, :]
            columns = columns_of(chip, features)
            both = [ref[0, columns, :] for ref in weights[2 * pair : 2 * pair + 2]]
            acts += jnp.dot(
                rows, jnp.concatenate(both, axis=1), preferred_element_type=jnp.float32
            )
        acts_ref[:, pair * width : (pair + 1) * width] = acts


def finish(chips, acts_ref, across_ref, down_ref, across_down_ref, out_ref):
    part_rows, features = out_ref.shape[0] // chips, out_ref.shape[1]
    width = acts_ref.shape[1] // 4
    hidden = []
    for pair in range(2):
        gate_act, up_act = (
            acts_ref[:, (2 * pair + which) * width : (2 * pair + which + 1) * width]
            + across_ref[:, (2 - 2 * pair + which) * width : (3 - 2 * pair + which) * width]
            for which in range(2)
        )
        hidden.append((gate_act / (1.0 + jnp.exp(-gate_act)) * up_act).astype(jnp.bfloat16))
    for chip in range(chips):
        columns = columns_of(chip, features)
        summed = jnp.dot(hidden[0], down_ref[0, :, columns], preferred_element_type=jnp.float32)
        summed += jnp.dot(
            hidden[1], across_down_ref[0, :, columns], preferred_element_type=jnp.float32
        )
        out_ref[chip * part_rows : (chip + 1) * part_rows, :] = summed.astype(jnp.bfloat16)


def combine(match_ref, weight_ref, returned_ref, out_hbm, out_ref, sems):
    copies = []
    for part in range(out_ref.shape[0] // PIECE):
        rows = pl.ds(part * PIECE, PIECE)
        summed = jnp.dot(match_ref[rows, :], returned_ref[...], preferred_element_type=jnp.float32)
        out_ref[rows, :] = (weight_ref[rows, :] * summed).astype(jnp.bfloat16)
        copies.append(pltpu.make_async_copy(out_ref.at[rows, :], out_hbm.at[rows, :], sems.at[part]))
        copies[-1].start()
    for copy in copies:
        copy.wait()


def shards(tokens, expert_ids, route_scores, w_gate, w_up, w_down):
    row_count, features = tokens.shape
    top_count, hidden_count = expert_ids.shape[1], w_gate.shape[2]
    ep_count, chips = lax.axis_size("ep"), lax.axis_size("chip")
    slot_count = ep_count * CAP
    half = jax.ShapeDtypeStruct((chips * slot_count, features), jnp.bfloat16)
    ids, scores = expert_ids.T, route_scores.T
    hbm, vmem = (pl.BlockSpec(memory_space=space) for space in (pltpu.HBM, pltpu.VMEM))
    anywhere = pl.BlockSpec(memory_space=pl.ANY)

    def exchange(rows):
        groups = far_groups(ep_count, chips)
        return lax.all_to_all(rows, FAR, 0, 0, axis_index_groups=groups, tiled=True)

    def call(kernel, name, out_shape, **rest):
        return pl.pallas_call(kernel, out_shape=out_shape, name=name, compiler_params=LIMIT, **rest)

    across = [lax.ppermute(value, "core", SWAP) for value in (w_gate, w_up, w_down)]
    outgoing = call(
        lambda *refs: route(ep_count, *refs),
        "route",
        half,
        in_specs=[hbm] * 2,
        scratch_shapes=[
            pltpu.VMEM((top_count, row_count), jnp.int32),
            pltpu.VMEM((row_count, features), jnp.bfloat16),
            pltpu.SemaphoreType.DMA((row_count // PIECE + 1,)),
        ],
        cost_estimate=pl.CostEstimate(flops=2 * 10**9, bytes_accessed=0, transcendentals=0),
    )(*(pltpu.with_memory_space_constraint(value, pltpu.HBM) for value in (ids, tokens)))
    incoming = exchange(outgoing)
    acts = call(
        lambda *refs: lift(chips, *refs),
        "lift",
        jax.ShapeDtypeStruct((slot_count, 4 * hidden_count), jnp.float32),
    )(incoming, w_gate, w_up, across[0], across[1])
    crossed = lax.ppermute(acts, "core", SWAP)
    match, weight = call(
        lambda *refs: score(ep_count, *refs),
        "score",
        (
            jax.ShapeDtypeStruct((row_count, chips * slot_count), jnp.bfloat16),
            jax.ShapeDtypeStruct((row_count, 1), jnp.float32),
        ),
        in_specs=[vmem] * 2 + [anywhere],
    )(ids, scores, acts)
    partial_value = call(
        lambda _, *refs: finish(chips, *refs), "finish", half, in_specs=[anywhere] + [vmem] * 4
    )(weight, acts, crossed, w_down, across[2])
    returned = exchange(partial_value)
    return call(
        combine,
        "combine",
        jax.ShapeDtypeStruct((row_count, features), jnp.bfloat16),
        out_specs=hbm,
        scratch_shapes=[
            pltpu.VMEM((row_count, features), jnp.bfloat16),
            pltpu.SemaphoreType.DMA((row_count // PIECE,)),
        ],
    )(match, weight, returned)


def solution(mesh):
    groups, ep_count, tp_count = (mesh.shape[name] for name in ("groups", "ep", "tp"))
    split = jax.sharding.Mesh(
        mesh.devices.reshape(groups, ep_count, tp_count // 2, 2), ("groups", "ep", "chip", "core")
    )
    tp = ("chip", "core")
    placed = (
        P(("groups", "ep"), tp),
        P(("groups", "ep"), None),
        P(("groups", "ep"), None),
        P("ep", None, tp),
        P("ep", None, tp),
        P("ep", tp, None),
    )
    return jax.shard_map(
        shards, mesh=split, in_specs=placed, out_specs=P(("groups", "ep"), tp), check_vma=False
    )
```

```python
import jax
import jax.numpy as jnp
from jax import lax
from jax.experimental import pallas as pl
from jax.experimental.pallas import tpu as pltpu
from jax.sharding import PartitionSpec as P

CAP = 8
PIECE = 32
FAR = ("ep", "chip", "core")
SWAP = [(0, 1), (1, 0)]
LIMIT = pltpu.CompilerParams(vmem_limit_bytes=16 * 1024 * 1024)


def iota(shape, dim):
    return lax.broadcasted_iota(jnp.int32, shape, dim)


def to_column(row):
    size = row.shape[1]
    square = (size, size)
    return jnp.sum(jnp.where(iota(square, 0) == iota(square, 1), row, 0.0), axis=1, keepdims=True)


def slot_codes(ids, resident):
    row_count = ids.shape[1]
    expert = jnp.min(ids, axis=0, keepdims=True)
    onehot_shape = (-(-resident // 16) * 16, row_count)
    onehot = jnp.where(expert == iota(onehot_shape, 0).astype(jnp.float32), 1.0, 0.0)
    square = (row_count, row_count)
    earlier = jnp.where(iota(square, 0) < iota(square, 1), 1.0, 0.0).astype(jnp.bfloat16)
    counts = jnp.dot(onehot.astype(jnp.bfloat16), earlier, preferred_element_type=jnp.float32)
    return expert * CAP + jnp.sum(counts * onehot, axis=0, keepdims=True), expert


def row_codes(index, ep_count):
    index = lax.rem(index, ep_count * CAP)
    return ((index // (2 * CAP)) * CAP + lax.rem(index, CAP)).astype(jnp.float32)


def pack_pieces(chips, gate_hbm, up_hbm, down_hbm, pack_ref):
    features, width = down_hbm.shape[2] // (2 * chips), gate_hbm.shape[2]
    half = features // 2
    pieces = []
    for which, source in enumerate((gate_hbm, up_hbm)):
        for chip in range(chips):
            start = columns_of(chip, features, True)
            for at in (0, half):
                row = (which * chips + chip) * features + at
                rows = pl.ds(pl.multiple_of(start + at, half), half)
                pieces.append((source.at[0, rows, :], pack_ref.at[pl.ds(row, half), :]))
    for chip in range(chips):
        start = columns_of(chip, features, True)
        for at in range(0, features, width):
            row = (2 * chips + chip) * features + at
            columns = pl.ds(pl.multiple_of(start + at, width), width)
            pieces.append((down_hbm.at[0, :, columns], pack_ref.at[pl.ds(row, width), :]))
    return pieces


def route(ep_count, chips, ids_hbm, tokens_hbm, *refs):
    weights, (outgoing_ref, pack_ref) = refs[:3], refs[3:5]
    ids_ref, tokens_ref, sems, pack_sems = refs[5:]
    row_count = ids_ref.shape[1]
    parts = row_count // PIECE
    copies = [pltpu.make_async_copy(ids_hbm, ids_ref, sems.at[parts])] + [
        pltpu.make_async_copy(
            tokens_hbm.at[pl.ds(part * PIECE, PIECE), :],
            tokens_ref.at[pl.ds(part * PIECE, PIECE), :],
            sems.at[part],
        )
        for part in range(parts)
    ]
    pieces = [
        pltpu.make_async_copy(source, target, pack_sems.at[at])
        for at, (source, target) in enumerate(pack_pieces(chips, *weights, pack_ref))
    ]
    for copy in copies + pieces:
        copy.start()
    copies[0].wait()
    code, _ = slot_codes(ids_ref[...].astype(jnp.float32), ep_count // 2)
    wanted = row_codes(iota((outgoing_ref.shape[0], row_count), 0), ep_count)
    dispatch = jnp.where(code == wanted, 1.0, 0.0).astype(jnp.bfloat16)
    for copy in copies[1:]:
        copy.wait()
    outgoing_ref[...] = jnp.dot(
        dispatch, tokens_ref[...], preferred_element_type=jnp.float32
    ).astype(jnp.bfloat16)
    for piece in pieces:
        piece.wait()


def score(ep_count, ids_ref, scores_ref, _, match_ref, weight_ref):
    ids = ids_ref[...].astype(jnp.float32)
    code, expert = slot_codes(ids, ep_count // 2)
    wanted = row_codes(iota(match_ref.shape, 1), ep_count)
    match_ref[...] = jnp.where(to_column(code) == wanted, 1.0, 0.0).astype(jnp.bfloat16)
    squashed = jax.nn.sigmoid(scores_ref[...])
    chosen = jnp.sum(jnp.where(ids == expert, squashed, 0.0), axis=0, keepdims=True)
    weight_ref[...] = to_column(2.5 * chosen / jnp.sum(squashed, axis=0, keepdims=True))


def far_groups(ep_count, chips):
    return [
        [(z * chips + x) * 2 + (side + x) % 2 for x in range(chips) for z in range(ep_count)]
        for side in range(2)
    ]


def columns_of(chip, features, other=False):
    core = lax.rem(lax.axis_index("core") + lax.axis_index("chip") + chip + (1 if other else 0), 2)
    return pl.multiple_of((2 * chip + core) * features, features)


def lift(chips, rows_ref, gate_ref, up_ref, pack_ref, acts_ref):
    part_rows, features = rows_ref.shape[0] // chips, rows_ref.shape[1]
    width = 2 * gate_ref.shape[2]
    for across in range(2):
        acts = jnp.zeros((part_rows, width), jnp.float32)
        for chip in range(chips):
            rows = rows_ref[chip * part_rows : (chip + 1) * part_rows, :]
            if across:
                at = [(which * chips + chip) * features for which in range(2)]
                both = [pack_ref[start : start + features, :] for start in at]
            else:
                columns = pl.ds(columns_of(chip, features), features)
                both = [gate_ref[0, columns, :], up_ref[0, columns, :]]
            acts += jnp.dot(
                rows, jnp.concatenate(both, axis=1), preferred_element_type=jnp.float32
            )
        acts_ref[:, across * width : (across + 1) * width] = acts


def finish(chips, acts_ref, across_ref, down_ref, pack_ref, out_ref):
    part_rows, features = out_ref.shape[0] // chips, out_ref.shape[1]
    width = acts_ref.shape[1] // 4
    hidden = []
    for pair in range(2):
        gate_act, up_act = (
            acts_ref[:, (2 * pair + which) * width : (2 * pair + which + 1) * width]
            + across_ref[:, (2 - 2 * pair + which) * width : (3 - 2 * pair + which) * width]
            for which in range(2)
        )
        hidden.append((gate_act / (1.0 + jnp.exp(-gate_act)) * up_act).astype(jnp.bfloat16))
    for chip in range(chips):
        columns = pl.ds(columns_of(chip, features), features)
        summed = jnp.dot(hidden[0], down_ref[0, :, columns], preferred_element_type=jnp.float32)
        first = (2 * chips + chip) * features
        tiles = [pack_ref[first + at : first + at + width, :] for at in range(0, features, width)]
        summed += jnp.dot(
            hidden[1], jnp.concatenate(tiles, axis=1), preferred_element_type=jnp.float32
        )
        out_ref[chip * part_rows : (chip + 1) * part_rows, :] = summed.astype(jnp.bfloat16)


def combine(match_ref, weight_ref, returned_ref, out_hbm, out_ref, sems):
    copies = []
    for part in range(out_ref.shape[0] // PIECE):
        rows = pl.ds(part * PIECE, PIECE)
        summed = jnp.dot(match_ref[rows, :], returned_ref[...], preferred_element_type=jnp.float32)
        out_ref[rows, :] = (weight_ref[rows, :] * summed).astype(jnp.bfloat16)
        copies.append(pltpu.make_async_copy(out_ref.at[rows, :], out_hbm.at[rows, :], sems.at[part]))
        copies[-1].start()
    for copy in copies:
        copy.wait()


def shards(tokens, expert_ids, route_scores, w_gate, w_up, w_down):
    row_count, features = tokens.shape
    top_count, hidden_count = expert_ids.shape[1], w_gate.shape[2]
    ep_count, chips = lax.axis_size("ep"), lax.axis_size("chip")
    slot_count = ep_count * CAP
    half = jax.ShapeDtypeStruct((chips * slot_count, features), jnp.bfloat16)
    ids, scores = expert_ids.T, route_scores.T
    hbm, vmem = (pl.BlockSpec(memory_space=space) for space in (pltpu.HBM, pltpu.VMEM))
    anywhere = pl.BlockSpec(memory_space=pl.ANY)

    def exchange(rows):
        groups = far_groups(ep_count, chips)
        return lax.all_to_all(rows, FAR, 0, 0, axis_index_groups=groups, tiled=True)

    def call(kernel, name, out_shape, **rest):
        return pl.pallas_call(kernel, out_shape=out_shape, name=name, compiler_params=LIMIT, **rest)

    pack_shape = jax.ShapeDtypeStruct((3 * chips * features, hidden_count), jnp.bfloat16)
    inputs = (ids, tokens, w_gate, w_up, w_down)
    outgoing, pack = call(
        lambda *refs: route(ep_count, chips, *refs),
        "route",
        (half, pack_shape),
        in_specs=[hbm] * 5,
        scratch_shapes=[
            pltpu.VMEM((top_count, row_count), jnp.int32),
            pltpu.VMEM((row_count, features), jnp.bfloat16),
            pltpu.SemaphoreType.DMA((row_count // PIECE + 1,)),
            pltpu.SemaphoreType.DMA((chips * (4 + features // hidden_count),)),
        ],
        cost_estimate=pl.CostEstimate(flops=2 * 10**9, bytes_accessed=0, transcendentals=0),
    )(*(pltpu.with_memory_space_constraint(value, pltpu.HBM) for value in inputs))
    across = lax.ppermute(pack, "core", SWAP)
    incoming = exchange(outgoing)
    acts = call(
        lambda *refs: lift(chips, *refs),
        "lift",
        jax.ShapeDtypeStruct((slot_count, 4 * hidden_count), jnp.float32),
    )(incoming, w_gate, w_up, across)
    crossed = lax.ppermute(acts, "core", SWAP)
    match, weight = call(
        lambda *refs: score(ep_count, *refs),
        "score",
        (
            jax.ShapeDtypeStruct((row_count, chips * slot_count), jnp.bfloat16),
            jax.ShapeDtypeStruct((row_count, 1), jnp.float32),
        ),
        in_specs=[vmem] * 2 + [anywhere],
    )(ids, scores, acts)
    partial_value = call(
        lambda _, *refs: finish(chips, *refs), "finish", half, in_specs=[anywhere] + [vmem] * 4
    )(weight, acts, crossed, w_down, across)
    returned = exchange(partial_value)
    return call(
        combine,
        "combine",
        jax.ShapeDtypeStruct((row_count, features), jnp.bfloat16),
        out_specs=hbm,
        scratch_shapes=[
            pltpu.VMEM((row_count, features), jnp.bfloat16),
            pltpu.SemaphoreType.DMA((row_count // PIECE,)),
        ],
    )(match, weight, returned)


def solution(mesh):
    groups, ep_count, tp_count = (mesh.shape[name] for name in ("groups", "ep", "tp"))
    split = jax.sharding.Mesh(
        mesh.devices.reshape(groups, ep_count, tp_count // 2, 2), ("groups", "ep", "chip", "core")
    )
    tp = ("chip", "core")
    placed = (
        P(("groups", "ep"), tp),
        P(("groups", "ep"), None),
        P(("groups", "ep"), None),
        P("ep", None, tp),
        P("ep", None, tp),
        P("ep", tp, None),
    )
    return jax.shard_map(
        shards, mesh=split, in_specs=placed, out_specs=P(("groups", "ep"), tp), check_vma=False
    )
```

```python
import jax
import jax.numpy as jnp
from jax import lax
from jax.experimental import pallas as pl
from jax.experimental.pallas import tpu as pltpu
from jax.sharding import PartitionSpec as P

CAP = 8
PIECE = 32
FAR = ("ep", "chip", "core")
SWAP = [(0, 1), (1, 0)]
LIMIT = pltpu.CompilerParams(vmem_limit_bytes=16 * 1024 * 1024)


def iota(shape, dim):
    return lax.broadcasted_iota(jnp.int32, shape, dim)


def to_column(row):
    size = row.shape[1]
    square = (size, size)
    return jnp.sum(jnp.where(iota(square, 0) == iota(square, 1), row, 0.0), axis=1, keepdims=True)


def slot_codes(ids, resident):
    row_count = ids.shape[1]
    expert = jnp.min(ids, axis=0, keepdims=True)
    onehot_shape = (-(-resident // 16) * 16, row_count)
    onehot = jnp.where(expert == iota(onehot_shape, 0).astype(jnp.float32), 1.0, 0.0)
    square = (row_count, row_count)
    earlier = jnp.where(iota(square, 0) < iota(square, 1), 1.0, 0.0).astype(jnp.bfloat16)
    counts = jnp.dot(onehot.astype(jnp.bfloat16), earlier, preferred_element_type=jnp.float32)
    return expert * CAP + jnp.sum(counts * onehot, axis=0, keepdims=True), expert


def row_codes(index, ep_count):
    expert = (ep_count - 1 - lax.rem(index // CAP, ep_count)) // 2
    return (expert * CAP + lax.rem(index, CAP)).astype(jnp.float32)


def route(ep_count, ids_hbm, tokens_hbm, outgoing_ref, ids_ref, tokens_ref, sems):
    row_count = ids_ref.shape[1]
    parts = row_count // PIECE
    copies = [pltpu.make_async_copy(ids_hbm, ids_ref, sems.at[parts])] + [
        pltpu.make_async_copy(
            tokens_hbm.at[pl.ds(part * PIECE, PIECE), :],
            tokens_ref.at[pl.ds(part * PIECE, PIECE), :],
            sems.at[part],
        )
        for part in range(parts)
    ]
    for copy in copies:
        copy.start()
    copies[0].wait()
    code, _ = slot_codes(ids_ref[...].astype(jnp.float32), ep_count // 2)
    wanted = row_codes(iota((outgoing_ref.shape[0], row_count), 0), ep_count)
    dispatch = jnp.where(code == wanted, 1.0, 0.0).astype(jnp.bfloat16)
    for copy in copies[1:]:
        copy.wait()
    outgoing_ref[...] = jnp.dot(
        dispatch, tokens_ref[...], preferred_element_type=jnp.float32
    ).astype(jnp.bfloat16)


def score(ep_count, ids_ref, scores_ref, _, match_ref, weight_ref):
    ids = ids_ref[...].astype(jnp.float32)
    code, expert = slot_codes(ids, ep_count // 2)
    wanted = row_codes(iota(match_ref.shape, 1), ep_count)
    match_ref[...] = jnp.where(to_column(code) == wanted, 1.0, 0.0).astype(jnp.bfloat16)
    squashed = jax.nn.sigmoid(scores_ref[...])
    chosen = jnp.sum(jnp.where(ids == expert, squashed, 0.0), axis=0, keepdims=True)
    weight_ref[...] = to_column(2.5 * chosen / jnp.sum(squashed, axis=0, keepdims=True))


def far_groups(ep_count, chips):
    return [
        [(z * chips + x) * 2 + (side + x) % 2 for x in range(chips) for z in reversed(range(ep_count))]
        for side in range(2)
    ]


def columns_of(chip, own, features):
    core = lax.rem(lax.axis_index("core") + lax.axis_index("chip") + chip + (0 if own else 1), 2)
    return pl.ds(pl.multiple_of((2 * chip + core) * features, features), features)


def lift(chips, own, rows_ref, gate_ref, up_ref):
    part_rows, features = rows_ref.shape[0] // chips, rows_ref.shape[1]
    gate_act = jnp.zeros((part_rows, gate_ref.shape[2]), jnp.float32)
    up_act = jnp.zeros((part_rows, up_ref.shape[2]), jnp.float32)
    for chip in range(chips):
        rows = rows_ref[chip * part_rows : (chip + 1) * part_rows, :]
        columns = columns_of(chip, own, features)
        gate_act += jnp.dot(rows, gate_ref[0, columns, :], preferred_element_type=jnp.float32)
        up_act += jnp.dot(rows, up_ref[0, columns, :], preferred_element_type=jnp.float32)
    return gate_act, up_act


def lower(chips, own, hidden, down_ref, out_ref):
    part_rows, features = out_ref.shape[0] // chips, out_ref.shape[1]
    for chip in range(chips):
        columns = columns_of(chip, own, features)
        out_ref[chip * part_rows : (chip + 1) * part_rows, :] = jnp.dot(
            hidden, down_ref[0, :, columns], preferred_element_type=jnp.float32
        ).astype(jnp.bfloat16)


def begin(chips, rows_ref, gate_ref, up_ref, gate_act_ref, up_act_ref):
    gate_act_ref[...], up_act_ref[...] = lift(chips, True, rows_ref, gate_ref, up_ref)


def theirs(chips, *refs):
    rows_ref, gate_act_ref, up_act_ref, gate_ref, up_ref, down_ref, hidden_ref, other_ref = refs
    gate_act, up_act = lift(chips, False, rows_ref, gate_ref, up_ref)
    gate_act += gate_act_ref[...]
    up_act += up_act_ref[...]
    hidden = (gate_act / (1.0 + jnp.exp(-gate_act)) * up_act).astype(jnp.bfloat16)
    hidden_ref[...] = hidden
    lower(chips, False, hidden, down_ref, other_ref)


def ours(chips, hidden_ref, down_ref, mine_ref):
    lower(chips, True, hidden_ref[...], down_ref, mine_ref)


def add(mine_ref, other_ref, _, out_ref):
    total = mine_ref[...].astype(jnp.float32) + other_ref[...].astype(jnp.float32)
    out_ref[...] = total.astype(jnp.bfloat16)


def combine(match_ref, weight_ref, returned_ref, out_hbm, out_ref, sems):
    copies = []
    for part in range(out_ref.shape[0] // PIECE):
        rows = pl.ds(part * PIECE, PIECE)
        summed = jnp.dot(match_ref[rows, :], returned_ref[...], preferred_element_type=jnp.float32)
        out_ref[rows, :] = (weight_ref[rows, :] * summed).astype(jnp.bfloat16)
        copies.append(pltpu.make_async_copy(out_ref.at[rows, :], out_hbm.at[rows, :], sems.at[part]))
        copies[-1].start()
    for copy in copies:
        copy.wait()


def shards(tokens, expert_ids, route_scores, w_gate, w_up, w_down):
    row_count, features = tokens.shape
    top_count, hidden_count = expert_ids.shape[1], w_gate.shape[2]
    ep_count, chips = lax.axis_size("ep"), lax.axis_size("chip")
    slot_count = ep_count * CAP
    half = jax.ShapeDtypeStruct((chips * slot_count, features), jnp.bfloat16)
    ids, scores = expert_ids.T, route_scores.T
    hbm, vmem = (pl.BlockSpec(memory_space=space) for space in (pltpu.HBM, pltpu.VMEM))
    anywhere = pl.BlockSpec(memory_space=pl.ANY)

    def exchange(rows):
        groups = far_groups(ep_count, chips)
        return lax.all_to_all(rows, FAR, 0, 0, axis_index_groups=groups, tiled=True)

    def call(kernel, name, out_shape, **rest):
        return pl.pallas_call(kernel, out_shape=out_shape, name=name, compiler_params=LIMIT, **rest)

    outgoing = call(
        lambda *refs: route(ep_count, *refs),
        "route",
        half,
        in_specs=[hbm] * 2,
        scratch_shapes=[
            pltpu.VMEM((top_count, row_count), jnp.int32),
            pltpu.VMEM((row_count, features), jnp.bfloat16),
            pltpu.SemaphoreType.DMA((row_count // PIECE + 1,)),
        ],
        cost_estimate=pl.CostEstimate(flops=2 * 10**9, bytes_accessed=0, transcendentals=0),
    )(*(pltpu.with_memory_space_constraint(value, pltpu.HBM) for value in (ids, tokens)))
    incoming = exchange(outgoing)
    across = lax.ppermute(incoming, "core", SWAP)
    acts = (jax.ShapeDtypeStruct((slot_count, hidden_count), jnp.float32),) * 2
    begun = call(lambda *refs: begin(chips, *refs), "begin", acts)(incoming, w_gate, w_up)
    hidden_shape = jax.ShapeDtypeStruct((slot_count, hidden_count), jnp.bfloat16)
    hidden, other = call(lambda *refs: theirs(chips, *refs), "theirs", (hidden_shape, half))(
        across, *begun, w_gate, w_up, w_down
    )
    crossed = lax.ppermute(other, "core", SWAP)
    mine = call(lambda *refs: ours(chips, *refs), "ours", half)(hidden, w_down)
    match, weight = call(
        lambda *refs: score(ep_count, *refs),
        "score",
        (
            jax.ShapeDtypeStruct((row_count, chips * slot_count), jnp.bfloat16),
            jax.ShapeDtypeStruct((row_count, 1), jnp.float32),
        ),
        in_specs=[vmem] * 2 + [anywhere],
    )(ids, scores, other)
    summed = call(add, "add", half, in_specs=[vmem] * 2 + [anywhere])(mine, crossed, weight)
    returned = exchange(summed)
    return call(
        combine,
        "combine",
        jax.ShapeDtypeStruct((row_count, features), jnp.bfloat16),
        out_specs=hbm,
        scratch_shapes=[
            pltpu.VMEM((row_count, features), jnp.bfloat16),
            pltpu.SemaphoreType.DMA((row_count // PIECE,)),
        ],
    )(match, weight, returned)


def solution(mesh):
    groups, ep_count, tp_count = (mesh.shape[name] for name in ("groups", "ep", "tp"))
    split = jax.sharding.Mesh(
        mesh.devices.reshape(groups, ep_count, tp_count // 2, 2), ("groups", "ep", "chip", "core")
    )
    tp = ("chip", "core")
    placed = (
        P(("groups", "ep"), tp),
        P(("groups", "ep"), None),
        P(("groups", "ep"), None),
        P("ep", None, tp),
        P("ep", None, tp),
        P("ep", tp, None),
    )
    return jax.shard_map(
        shards, mesh=split, in_specs=placed, out_specs=P(("groups", "ep"), tp), check_vma=False
    )
```

```python
import jax
import jax.numpy as jnp
from jax import lax
from jax.experimental import pallas as pl
from jax.experimental.pallas import tpu as pltpu
from jax.sharding import PartitionSpec as P

CAP = 8
PIECE = 32
FAR = ("ep", "chip", "core")
SWAP = [(0, 1), (1, 0)]
LIMIT = pltpu.CompilerParams(vmem_limit_bytes=16 * 1024 * 1024)


def iota(shape, dim):
    return lax.broadcasted_iota(jnp.int32, shape, dim)


def to_column(row):
    size = row.shape[1]
    square = (size, size)
    return jnp.sum(jnp.where(iota(square, 0) == iota(square, 1), row, 0.0), axis=1, keepdims=True)


def slot_codes(ids, resident):
    row_count = ids.shape[1]
    expert = jnp.min(ids, axis=0, keepdims=True)
    onehot_shape = (-(-resident // 16) * 16, row_count)
    onehot = jnp.where(expert == iota(onehot_shape, 0).astype(jnp.float32), 1.0, 0.0)
    square = (row_count, row_count)
    earlier = jnp.where(iota(square, 0) < iota(square, 1), 1.0, 0.0).astype(jnp.bfloat16)
    counts = jnp.dot(onehot.astype(jnp.bfloat16), earlier, preferred_element_type=jnp.float32)
    return expert * CAP + jnp.sum(counts * onehot, axis=0, keepdims=True), expert


def row_codes(index, ep_count, chips):
    expert = (ep_count - 1 - index // (CAP * chips)) // 2
    return (expert * CAP + lax.rem(index, CAP)).astype(jnp.float32)


def route(ep_count, chips, ids_hbm, tokens_hbm, outgoing_ref, ids_ref, tokens_ref, sems):
    row_count = ids_ref.shape[1]
    parts = row_count // PIECE
    copies = [pltpu.make_async_copy(ids_hbm, ids_ref, sems.at[parts])] + [
        pltpu.make_async_copy(
            tokens_hbm.at[pl.ds(part * PIECE, PIECE), :],
            tokens_ref.at[pl.ds(part * PIECE, PIECE), :],
            sems.at[part],
        )
        for part in range(parts)
    ]
    for copy in copies:
        copy.start()
    copies[0].wait()
    code, _ = slot_codes(ids_ref[...].astype(jnp.float32), ep_count // 2)
    wanted = row_codes(iota((outgoing_ref.shape[0], row_count), 0), ep_count, chips)
    dispatch = jnp.where(code == wanted, 1.0, 0.0).astype(jnp.bfloat16)
    for copy in copies[1:]:
        copy.wait()
    outgoing_ref[...] = jnp.dot(
        dispatch, tokens_ref[...], preferred_element_type=jnp.float32
    ).astype(jnp.bfloat16)


def score(ep_count, chips, ids_ref, scores_ref, _, match_ref, weight_ref):
    ids = ids_ref[...].astype(jnp.float32)
    code, expert = slot_codes(ids, ep_count // 2)
    wanted = row_codes(iota(match_ref.shape, 1), ep_count, chips)
    match_ref[...] = jnp.where(to_column(code) == wanted, 1.0, 0.0).astype(jnp.bfloat16)
    squashed = jax.nn.sigmoid(scores_ref[...])
    chosen = jnp.sum(jnp.where(ids == expert, squashed, 0.0), axis=0, keepdims=True)
    weight_ref[...] = to_column(2.5 * chosen / jnp.sum(squashed, axis=0, keepdims=True))


def far_groups(ep_count, chips):
    return [
        [
            (z * chips + x) * 2 + (side + x) % 2
            for z in reversed(range(ep_count))
            for x in reversed(range(chips))
        ]
        for side in range(2)
    ]


def columns_of(chip, own, features):
    core = lax.rem(lax.axis_index("core") + lax.axis_index("chip") + chip + (0 if own else 1), 2)
    return pl.ds(pl.multiple_of((2 * chip + core) * features, features), features)


def lift(chips, own, rows_ref, gate_ref, up_ref):
    rows, features = rows_ref[...], rows_ref.shape[1]
    totals = []
    for ref in (gate_ref, up_ref):
        total = 0.0
        for chip in range(chips):
            weight = ref[0, columns_of(chip, own, features), :]
            acts = jnp.dot(rows, weight, preferred_element_type=jnp.float32)
            acts = acts.reshape(-1, chips, CAP, acts.shape[1])
            total += acts[:, chips - 1 - chip].reshape(-1, acts.shape[3])
        totals.append(total)
    return totals


def lower(chips, own, hidden, down_ref, out_ref):
    features = out_ref.shape[3]
    for chip in range(chips):
        values = jnp.dot(
            hidden,
            down_ref[0, :, columns_of(chip, own, features)],
            preferred_element_type=jnp.float32,
        )
        out_ref[:, chips - 1 - chip] = values.reshape(-1, CAP, features).astype(jnp.bfloat16)


def begin(chips, rows_ref, gate_ref, up_ref, gate_act_ref, up_act_ref):
    gate_act_ref[...], up_act_ref[...] = lift(chips, True, rows_ref, gate_ref, up_ref)


def theirs(chips, *refs):
    rows_ref, gate_act_ref, up_act_ref, gate_ref, up_ref, down_ref, hidden_ref, other_ref = refs
    gate_act, up_act = lift(chips, False, rows_ref, gate_ref, up_ref)
    gate_act += gate_act_ref[...]
    up_act += up_act_ref[...]
    hidden = (gate_act / (1.0 + jnp.exp(-gate_act)) * up_act).astype(jnp.bfloat16)
    hidden_ref[...] = hidden
    lower(chips, False, hidden, down_ref, other_ref)


def ours(chips, hidden_ref, down_ref, mine_ref):
    lower(chips, True, hidden_ref[...], down_ref, mine_ref)


def add(mine_ref, other_ref, _, out_ref):
    total = mine_ref[...].astype(jnp.float32) + other_ref[...].astype(jnp.float32)
    out_ref[...] = total.astype(jnp.bfloat16)


def combine(match_ref, weight_ref, returned_ref, out_hbm, out_ref, sems):
    copies = []
    for part in range(out_ref.shape[0] // PIECE):
        rows = pl.ds(part * PIECE, PIECE)
        summed = jnp.dot(match_ref[rows, :], returned_ref[...], preferred_element_type=jnp.float32)
        out_ref[rows, :] = (weight_ref[rows, :] * summed).astype(jnp.bfloat16)
        copies.append(pltpu.make_async_copy(out_ref.at[rows, :], out_hbm.at[rows, :], sems.at[part]))
        copies[-1].start()
    for copy in copies:
        copy.wait()


def shards(tokens, expert_ids, route_scores, w_gate, w_up, w_down):
    row_count, features = tokens.shape
    top_count, hidden_count = expert_ids.shape[1], w_gate.shape[2]
    ep_count, chips = lax.axis_size("ep"), lax.axis_size("chip")
    slot_count = ep_count * CAP
    half = jax.ShapeDtypeStruct((chips * slot_count, features), jnp.bfloat16)
    split = jax.ShapeDtypeStruct((ep_count, chips, CAP, features), jnp.bfloat16)
    ids, scores = expert_ids.T, route_scores.T
    hbm, vmem = (pl.BlockSpec(memory_space=space) for space in (pltpu.HBM, pltpu.VMEM))
    anywhere = pl.BlockSpec(memory_space=pl.ANY)

    def exchange(rows):
        groups = far_groups(ep_count, chips)
        return lax.all_to_all(rows, FAR, 0, 0, axis_index_groups=groups, tiled=True)

    def call(kernel, name, out_shape, **rest):
        return pl.pallas_call(kernel, out_shape=out_shape, name=name, compiler_params=LIMIT, **rest)

    outgoing = call(
        lambda *refs: route(ep_count, chips, *refs),
        "route",
        half,
        in_specs=[hbm] * 2,
        scratch_shapes=[
            pltpu.VMEM((top_count, row_count), jnp.int32),
            pltpu.VMEM((row_count, features), jnp.bfloat16),
            pltpu.SemaphoreType.DMA((row_count // PIECE + 1,)),
        ],
        cost_estimate=pl.CostEstimate(flops=2 * 10**9, bytes_accessed=0, transcendentals=0),
    )(*(pltpu.with_memory_space_constraint(value, pltpu.HBM) for value in (ids, tokens)))
    incoming = exchange(outgoing)
    across = lax.ppermute(incoming, "core", SWAP)
    acts = (jax.ShapeDtypeStruct((slot_count, hidden_count), jnp.float32),) * 2
    begun = call(lambda *refs: begin(chips, *refs), "begin", acts)(incoming, w_gate, w_up)
    hidden_shape = jax.ShapeDtypeStruct((slot_count, hidden_count), jnp.bfloat16)
    hidden, other = call(lambda *refs: theirs(chips, *refs), "theirs", (hidden_shape, split))(
        across, *begun, w_gate, w_up, w_down
    )
    crossed = lax.ppermute(other, "core", SWAP)
    mine = call(lambda *refs: ours(chips, *refs), "ours", split)(hidden, w_down)
    match, weight = call(
        lambda *refs: score(ep_count, chips, *refs),
        "score",
        (
            jax.ShapeDtypeStruct((row_count, chips * slot_count), jnp.bfloat16),
            jax.ShapeDtypeStruct((row_count, 1), jnp.float32),
        ),
        in_specs=[vmem] * 2 + [anywhere],
    )(ids, scores, other)
    summed = call(add, "add", split, in_specs=[vmem] * 2 + [anywhere])(mine, crossed, weight)
    returned = exchange(summed.reshape(half.shape))
    return call(
        combine,
        "combine",
        jax.ShapeDtypeStruct((row_count, features), jnp.bfloat16),
        out_specs=hbm,
        scratch_shapes=[
            pltpu.VMEM((row_count, features), jnp.bfloat16),
            pltpu.SemaphoreType.DMA((row_count // PIECE,)),
        ],
    )(match, weight, returned)


def solution(mesh):
    groups, ep_count, tp_count = (mesh.shape[name] for name in ("groups", "ep", "tp"))
    split = jax.sharding.Mesh(
        mesh.devices.reshape(groups, ep_count, tp_count // 2, 2), ("groups", "ep", "chip", "core")
    )
    tp = ("chip", "core")
    placed = (
        P(("groups", "ep"), tp),
        P(("groups", "ep"), None),
        P(("groups", "ep"), None),
        P("ep", None, tp),
        P("ep", None, tp),
        P("ep", tp, None),
    )
    return jax.shard_map(
        shards, mesh=split, in_specs=placed, out_specs=P(("groups", "ep"), tp), check_vma=False
    )
```

```python
import jax
import jax.numpy as jnp
from jax import lax
from jax.experimental import pallas as pl
from jax.experimental.pallas import tpu as pltpu
from jax.sharding import PartitionSpec as P

CAP = 8
PIECE = 32
FAR = ("ep", "chip", "core")
SWAP = [(0, 1), (1, 0)]
LIMIT = pltpu.CompilerParams(vmem_limit_bytes=16 * 1024 * 1024)


def iota(shape, dim):
    return lax.broadcasted_iota(jnp.int32, shape, dim)


def to_column(row):
    size = row.shape[1]
    square = (size, size)
    return jnp.sum(jnp.where(iota(square, 0) == iota(square, 1), row, 0.0), axis=1, keepdims=True)


def slot_codes(ids, resident):
    row_count = ids.shape[1]
    expert = jnp.min(ids, axis=0, keepdims=True)
    onehot_shape = (-(-resident // 16) * 16, row_count)
    onehot = jnp.where(expert == iota(onehot_shape, 0).astype(jnp.float32), 1.0, 0.0)
    square = (row_count, row_count)
    earlier = jnp.where(iota(square, 0) < iota(square, 1), 1.0, 0.0).astype(jnp.bfloat16)
    counts = jnp.dot(onehot.astype(jnp.bfloat16), earlier, preferred_element_type=jnp.float32)
    return expert * CAP + jnp.sum(counts * onehot, axis=0, keepdims=True), expert


def first_order(ep_count):
    return [z ^ 2 for z in range(ep_count)]


def second_order(ep_count):
    return list(reversed(range(ep_count)))


def row_codes(index, order):
    listed = lax.rem(index // CAP, len(order))
    expert = sum(jnp.where(listed == at, z // 2, 0) for at, z in enumerate(order))
    return (expert * CAP + lax.rem(index, CAP)).astype(jnp.float32)


def route(ep_count, ids_hbm, tokens_hbm, outgoing_ref, ids_ref, tokens_ref, sems):
    row_count = ids_ref.shape[1]
    parts = row_count // PIECE
    copies = [pltpu.make_async_copy(ids_hbm, ids_ref, sems.at[parts])] + [
        pltpu.make_async_copy(
            tokens_hbm.at[pl.ds(part * PIECE, PIECE), :],
            tokens_ref.at[pl.ds(part * PIECE, PIECE), :],
            sems.at[part],
        )
        for part in range(parts)
    ]
    for copy in copies:
        copy.start()
    wanted = row_codes(iota((outgoing_ref.shape[0], row_count), 0), first_order(ep_count))
    copies[0].wait()
    code, _ = slot_codes(ids_ref[...].astype(jnp.float32), ep_count // 2)
    dispatch = jnp.where(code == wanted, 1.0, 0.0).astype(jnp.bfloat16)
    for copy in copies[1:]:
        copy.wait()
    outgoing_ref[...] = jnp.dot(
        dispatch, tokens_ref[...], preferred_element_type=jnp.float32
    ).astype(jnp.bfloat16)


def score(ep_count, ids_ref, scores_ref, _, match_ref, weight_ref):
    ids = ids_ref[...].astype(jnp.float32)
    code, expert = slot_codes(ids, ep_count // 2)
    wanted = row_codes(iota(match_ref.shape, 1), second_order(ep_count))
    match_ref[...] = jnp.where(to_column(code) == wanted, 1.0, 0.0).astype(jnp.bfloat16)
    squashed = jax.nn.sigmoid(scores_ref[...])
    chosen = jnp.sum(jnp.where(ids == expert, squashed, 0.0), axis=0, keepdims=True)
    weight_ref[...] = to_column(2.5 * chosen / jnp.sum(squashed, axis=0, keepdims=True))


def far_groups(order, chips):
    return [
        [(z * chips + x) * 2 + (side + x) % 2 for x in range(chips) for z in order]
        for side in range(2)
    ]


def columns_of(chip, own, features):
    core = lax.rem(lax.axis_index("core") + lax.axis_index("chip") + chip + (0 if own else 1), 2)
    return pl.ds(pl.multiple_of((2 * chip + core) * features, features), features)


def lift(chips, own, rows_ref, gate_ref, up_ref):
    part_rows, features = rows_ref.shape[0] // chips, rows_ref.shape[1]
    gate_act = jnp.zeros((part_rows, gate_ref.shape[2]), jnp.float32)
    up_act = jnp.zeros((part_rows, up_ref.shape[2]), jnp.float32)
    for chip in range(chips):
        rows = rows_ref[chip * part_rows : (chip + 1) * part_rows, :]
        columns = columns_of(chip, own, features)
        gate_act += jnp.dot(rows, gate_ref[0, columns, :], preferred_element_type=jnp.float32)
        up_act += jnp.dot(rows, up_ref[0, columns, :], preferred_element_type=jnp.float32)
    return gate_act, up_act


def lower(chips, own, hidden, down_ref, out_ref):
    part_rows, features = out_ref.shape[0] // chips, out_ref.shape[1]
    first = first_order(part_rows // CAP)
    moves = [first.index(z) for z in second_order(part_rows // CAP)]
    for chip in range(chips):
        columns = columns_of(chip, own, features)
        values = jnp.dot(hidden, down_ref[0, :, columns], preferred_element_type=jnp.float32)
        blocks = [values[at * CAP : (at + 1) * CAP, :] for at in moves]
        out_ref[chip * part_rows : (chip + 1) * part_rows, :] = jnp.concatenate(
            blocks, axis=0
        ).astype(jnp.bfloat16)


def begin(chips, rows_ref, gate_ref, up_ref, gate_act_ref, up_act_ref):
    gate_act_ref[...], up_act_ref[...] = lift(chips, True, rows_ref, gate_ref, up_ref)


def theirs(chips, *refs):
    rows_ref, gate_act_ref, up_act_ref, gate_ref, up_ref, down_ref, hidden_ref, other_ref = refs
    gate_act, up_act = lift(chips, False, rows_ref, gate_ref, up_ref)
    gate_act += gate_act_ref[...]
    up_act += up_act_ref[...]
    hidden = (gate_act / (1.0 + jnp.exp(-gate_act)) * up_act).astype(jnp.bfloat16)
    hidden_ref[...] = hidden
    lower(chips, False, hidden, down_ref, other_ref)


def ours(chips, hidden_ref, down_ref, mine_ref):
    lower(chips, True, hidden_ref[...], down_ref, mine_ref)


def add(mine_ref, other_ref, _, out_ref):
    total = mine_ref[...].astype(jnp.float32) + other_ref[...].astype(jnp.float32)
    out_ref[...] = total.astype(jnp.bfloat16)


def combine(match_ref, weight_ref, returned_ref, out_hbm, out_ref, sems):
    copies = []
    for part in range(out_ref.shape[0] // PIECE):
        rows = pl.ds(part * PIECE, PIECE)
        summed = jnp.dot(match_ref[rows, :], returned_ref[...], preferred_element_type=jnp.float32)
        out_ref[rows, :] = (weight_ref[rows, :] * summed).astype(jnp.bfloat16)
        copies.append(pltpu.make_async_copy(out_ref.at[rows, :], out_hbm.at[rows, :], sems.at[part]))
        copies[-1].start()
    for copy in copies:
        copy.wait()


def shards(tokens, expert_ids, route_scores, w_gate, w_up, w_down):
    row_count, features = tokens.shape
    top_count, hidden_count = expert_ids.shape[1], w_gate.shape[2]
    ep_count, chips = lax.axis_size("ep"), lax.axis_size("chip")
    slot_count = ep_count * CAP
    half = jax.ShapeDtypeStruct((chips * slot_count, features), jnp.bfloat16)
    ids, scores = expert_ids.T, route_scores.T
    hbm, vmem = (pl.BlockSpec(memory_space=space) for space in (pltpu.HBM, pltpu.VMEM))
    anywhere = pl.BlockSpec(memory_space=pl.ANY)

    def exchange(rows, order):
        groups = far_groups(order(ep_count), chips)
        return lax.all_to_all(rows, FAR, 0, 0, axis_index_groups=groups, tiled=True)

    def call(kernel, name, out_shape, **rest):
        return pl.pallas_call(kernel, out_shape=out_shape, name=name, compiler_params=LIMIT, **rest)

    outgoing = call(
        lambda *refs: route(ep_count, *refs),
        "route",
        half,
        in_specs=[hbm] * 2,
        scratch_shapes=[
            pltpu.VMEM((top_count, row_count), jnp.int32),
            pltpu.VMEM((row_count, features), jnp.bfloat16),
            pltpu.SemaphoreType.DMA((row_count // PIECE + 1,)),
        ],
        cost_estimate=pl.CostEstimate(flops=2 * 10**9, bytes_accessed=0, transcendentals=0),
    )(*(pltpu.with_memory_space_constraint(value, pltpu.HBM) for value in (ids, tokens)))
    incoming = exchange(outgoing, first_order)
    across = lax.ppermute(incoming, "core", SWAP)
    acts = (jax.ShapeDtypeStruct((slot_count, hidden_count), jnp.float32),) * 2
    begun = call(lambda *refs: begin(chips, *refs), "begin", acts)(incoming, w_gate, w_up)
    hidden_shape = jax.ShapeDtypeStruct((slot_count, hidden_count), jnp.bfloat16)
    hidden, other = call(lambda *refs: theirs(chips, *refs), "theirs", (hidden_shape, half))(
        across, *begun, w_gate, w_up, w_down
    )
    crossed = lax.ppermute(other, "core", SWAP)
    mine = call(lambda *refs: ours(chips, *refs), "ours", half)(hidden, w_down)
    match, weight = call(
        lambda *refs: score(ep_count, *refs),
        "score",
        (
            jax.ShapeDtypeStruct((row_count, chips * slot_count), jnp.bfloat16),
            jax.ShapeDtypeStruct((row_count, 1), jnp.float32),
        ),
        in_specs=[vmem] * 2 + [anywhere],
    )(ids, scores, other)
    summed = call(add, "add", half, in_specs=[vmem] * 2 + [anywhere])(mine, crossed, weight)
    returned = exchange(summed, second_order)
    return call(
        combine,
        "combine",
        jax.ShapeDtypeStruct((row_count, features), jnp.bfloat16),
        out_specs=hbm,
        scratch_shapes=[
            pltpu.VMEM((row_count, features), jnp.bfloat16),
            pltpu.SemaphoreType.DMA((row_count // PIECE,)),
        ],
    )(match, weight, returned)


def solution(mesh):
    groups, ep_count, tp_count = (mesh.shape[name] for name in ("groups", "ep", "tp"))
    split = jax.sharding.Mesh(
        mesh.devices.reshape(groups, ep_count, tp_count // 2, 2), ("groups", "ep", "chip", "core")
    )
    tp = ("chip", "core")
    placed = (
        P(("groups", "ep"), tp),
        P(("groups", "ep"), None),
        P(("groups", "ep"), None),
        P("ep", None, tp),
        P("ep", None, tp),
        P("ep", tp, None),
    )
    return jax.shard_map(
        shards, mesh=split, in_specs=placed, out_specs=P(("groups", "ep"), tp), check_vma=False
    )
```

```python
import jax
import jax.numpy as jnp
from jax import lax
from jax.experimental import pallas as pl
from jax.experimental.pallas import tpu as pltpu
from jax.sharding import PartitionSpec as P

CAP = 8
PIECE = 32
FAR = ("ep", "chip", "core")
SWAP = [(0, 1), (1, 0)]
LIMIT = pltpu.CompilerParams(vmem_limit_bytes=16 * 1024 * 1024)


def iota(shape, dim):
    return lax.broadcasted_iota(jnp.int32, shape, dim)


def to_column(row):
    size = row.shape[1]
    square = (size, size)
    return jnp.sum(jnp.where(iota(square, 0) == iota(square, 1), row, 0.0), axis=1, keepdims=True)


def slot_codes(ids, resident):
    row_count = ids.shape[1]
    expert = jnp.min(ids, axis=0, keepdims=True)
    onehot_shape = (-(-resident // 16) * 16, row_count)
    onehot = jnp.where(expert == iota(onehot_shape, 0).astype(jnp.float32), 1.0, 0.0)
    square = (row_count, row_count)
    earlier = jnp.where(iota(square, 0) < iota(square, 1), 1.0, 0.0).astype(jnp.bfloat16)
    counts = jnp.dot(onehot.astype(jnp.bfloat16), earlier, preferred_element_type=jnp.float32)
    return expert * CAP + jnp.sum(counts * onehot, axis=0, keepdims=True), expert


def first_order(ep_count):
    return [z ^ 2 for z in range(ep_count)]


def second_order(ep_count):
    return [z // 4 * 4 + (3, 1, 2, 0)[z % 4] for z in range(ep_count)]


def row_codes(index, order):
    listed = lax.rem(index // CAP, len(order))
    expert = sum(jnp.where(listed == at, z // 2, 0) for at, z in enumerate(order))
    return (expert * CAP + lax.rem(index, CAP)).astype(jnp.float32)


def route(ep_count, ids_hbm, tokens_hbm, outgoing_ref, ids_ref, tokens_ref, sems):
    row_count = ids_ref.shape[1]
    parts = row_count // PIECE
    copies = [pltpu.make_async_copy(ids_hbm, ids_ref, sems.at[parts])] + [
        pltpu.make_async_copy(
            tokens_hbm.at[pl.ds(part * PIECE, PIECE), :],
            tokens_ref.at[pl.ds(part * PIECE, PIECE), :],
            sems.at[part],
        )
        for part in range(parts)
    ]
    for copy in copies:
        copy.start()
    wanted = row_codes(iota((outgoing_ref.shape[0], row_count), 0), first_order(ep_count))
    copies[0].wait()
    code, _ = slot_codes(ids_ref[...].astype(jnp.float32), ep_count // 2)
    dispatch = jnp.where(code == wanted, 1.0, 0.0).astype(jnp.bfloat16)
    for copy in copies[1:]:
        copy.wait()
    outgoing_ref[...] = jnp.dot(
        dispatch, tokens_ref[...], preferred_element_type=jnp.float32
    ).astype(jnp.bfloat16)


def score(ep_count, ids_ref, scores_ref, _, match_ref, weight_ref):
    ids = ids_ref[...].astype(jnp.float32)
    code, expert = slot_codes(ids, ep_count // 2)
    wanted = row_codes(iota(match_ref.shape, 1), second_order(ep_count))
    match_ref[...] = jnp.where(to_column(code) == wanted, 1.0, 0.0).astype(jnp.bfloat16)
    squashed = jax.nn.sigmoid(scores_ref[...])
    chosen = jnp.sum(jnp.where(ids == expert, squashed, 0.0), axis=0, keepdims=True)
    weight_ref[...] = to_column(2.5 * chosen / jnp.sum(squashed, axis=0, keepdims=True))


def far_groups(order, chips):
    return [
        [(z * chips + x) * 2 + (side + x) % 2 for x in range(chips) for z in order]
        for side in range(2)
    ]


def columns_of(chip, own, features):
    core = lax.rem(lax.axis_index("core") + lax.axis_index("chip") + chip + (0 if own else 1), 2)
    return pl.ds(pl.multiple_of((2 * chip + core) * features, features), features)


def lift(chips, own, rows_ref, gate_ref, up_ref):
    part_rows, features = rows_ref.shape[0] // chips, rows_ref.shape[1]
    gate_act = jnp.zeros((part_rows, gate_ref.shape[2]), jnp.float32)
    up_act = jnp.zeros((part_rows, up_ref.shape[2]), jnp.float32)
    for chip in range(chips):
        rows = rows_ref[chip * part_rows : (chip + 1) * part_rows, :]
        columns = columns_of(chip, own, features)
        gate_act += jnp.dot(rows, gate_ref[0, columns, :], preferred_element_type=jnp.float32)
        up_act += jnp.dot(rows, up_ref[0, columns, :], preferred_element_type=jnp.float32)
    return gate_act, up_act


def lower(chips, own, hidden, down_ref, out_ref):
    part_rows, features = out_ref.shape[0] // chips, out_ref.shape[1]
    first = first_order(part_rows // CAP)
    moves = [first.index(z) for z in second_order(part_rows // CAP)]
    for chip in range(chips):
        columns = columns_of(chip, own, features)
        values = jnp.dot(hidden, down_ref[0, :, columns], preferred_element_type=jnp.float32)
        blocks = [values[at * CAP : (at + 1) * CAP, :] for at in moves]
        out_ref[chip * part_rows : (chip + 1) * part_rows, :] = jnp.concatenate(
            blocks, axis=0
        ).astype(jnp.bfloat16)


def begin(chips, rows_ref, gate_ref, up_ref, gate_act_ref, up_act_ref):
    gate_act_ref[...], up_act_ref[...] = lift(chips, True, rows_ref, gate_ref, up_ref)


def theirs(chips, *refs):
    rows_ref, gate_act_ref, up_act_ref, gate_ref, up_ref, down_ref, hidden_ref, other_ref = refs
    gate_act, up_act = lift(chips, False, rows_ref, gate_ref, up_ref)
    gate_act += gate_act_ref[...]
    up_act += up_act_ref[...]
    hidden = (gate_act / (1.0 + jnp.exp(-gate_act)) * up_act).astype(jnp.bfloat16)
    hidden_ref[...] = hidden
    lower(chips, False, hidden, down_ref, other_ref)


def ours(chips, hidden_ref, down_ref, mine_ref):
    lower(chips, True, hidden_ref[...], down_ref, mine_ref)


def add(mine_ref, other_ref, _, out_ref):
    total = mine_ref[...].astype(jnp.float32) + other_ref[...].astype(jnp.float32)
    out_ref[...] = total.astype(jnp.bfloat16)


def combine(match_ref, weight_ref, returned_ref, out_hbm, out_ref, sems):
    copies = []
    for part in range(out_ref.shape[0] // PIECE):
        rows = pl.ds(part * PIECE, PIECE)
        summed = jnp.dot(match_ref[rows, :], returned_ref[...], preferred_element_type=jnp.float32)
        out_ref[rows, :] = (weight_ref[rows, :] * summed).astype(jnp.bfloat16)
        copies.append(pltpu.make_async_copy(out_ref.at[rows, :], out_hbm.at[rows, :], sems.at[part]))
        copies[-1].start()
    for copy in copies:
        copy.wait()


def shards(tokens, expert_ids, route_scores, w_gate, w_up, w_down):
    row_count, features = tokens.shape
    top_count, hidden_count = expert_ids.shape[1], w_gate.shape[2]
    ep_count, chips = lax.axis_size("ep"), lax.axis_size("chip")
    slot_count = ep_count * CAP
    half = jax.ShapeDtypeStruct((chips * slot_count, features), jnp.bfloat16)
    ids, scores = expert_ids.T, route_scores.T
    hbm, vmem = (pl.BlockSpec(memory_space=space) for space in (pltpu.HBM, pltpu.VMEM))
    anywhere = pl.BlockSpec(memory_space=pl.ANY)

    def exchange(rows, order):
        groups = far_groups(order(ep_count), chips)
        return lax.all_to_all(rows, FAR, 0, 0, axis_index_groups=groups, tiled=True)

    def call(kernel, name, out_shape, **rest):
        return pl.pallas_call(kernel, out_shape=out_shape, name=name, compiler_params=LIMIT, **rest)

    outgoing = call(
        lambda *refs: route(ep_count, *refs),
        "route",
        half,
        in_specs=[hbm] * 2,
        scratch_shapes=[
            pltpu.VMEM((top_count, row_count), jnp.int32),
            pltpu.VMEM((row_count, features), jnp.bfloat16),
            pltpu.SemaphoreType.DMA((row_count // PIECE + 1,)),
        ],
        cost_estimate=pl.CostEstimate(flops=2 * 10**9, bytes_accessed=0, transcendentals=0),
    )(*(pltpu.with_memory_space_constraint(value, pltpu.HBM) for value in (ids, tokens)))
    incoming = exchange(outgoing, first_order)
    across = lax.ppermute(incoming, "core", SWAP)
    acts = (jax.ShapeDtypeStruct((slot_count, hidden_count), jnp.float32),) * 2
    begun = call(lambda *refs: begin(chips, *refs), "begin", acts)(incoming, w_gate, w_up)
    hidden_shape = jax.ShapeDtypeStruct((slot_count, hidden_count), jnp.bfloat16)
    hidden, other = call(lambda *refs: theirs(chips, *refs), "theirs", (hidden_shape, half))(
        across, *begun, w_gate, w_up, w_down
    )
    crossed = lax.ppermute(other, "core", SWAP)
    mine = call(lambda *refs: ours(chips, *refs), "ours", half)(hidden, w_down)
    match, weight = call(
        lambda *refs: score(ep_count, *refs),
        "score",
        (
            jax.ShapeDtypeStruct((row_count, chips * slot_count), jnp.bfloat16),
            jax.ShapeDtypeStruct((row_count, 1), jnp.float32),
        ),
        in_specs=[vmem] * 2 + [anywhere],
    )(ids, scores, other)
    summed = call(add, "add", half, in_specs=[vmem] * 2 + [anywhere])(mine, crossed, weight)
    returned = exchange(summed, second_order)
    return call(
        combine,
        "combine",
        jax.ShapeDtypeStruct((row_count, features), jnp.bfloat16),
        out_specs=hbm,
        scratch_shapes=[
            pltpu.VMEM((row_count, features), jnp.bfloat16),
            pltpu.SemaphoreType.DMA((row_count // PIECE,)),
        ],
    )(match, weight, returned)


def solution(mesh):
    groups, ep_count, tp_count = (mesh.shape[name] for name in ("groups", "ep", "tp"))
    split = jax.sharding.Mesh(
        mesh.devices.reshape(groups, ep_count, tp_count // 2, 2), ("groups", "ep", "chip", "core")
    )
    tp = ("chip", "core")
    placed = (
        P(("groups", "ep"), tp),
        P(("groups", "ep"), None),
        P(("groups", "ep"), None),
        P("ep", None, tp),
        P("ep", None, tp),
        P("ep", tp, None),
    )
    return jax.shard_map(
        shards, mesh=split, in_specs=placed, out_specs=P(("groups", "ep"), tp), check_vma=False
    )
```

```python
import jax
import jax.numpy as jnp
from jax import lax
from jax.experimental import pallas as pl
from jax.experimental.pallas import tpu as pltpu
from jax.sharding import PartitionSpec as P

CAP = 8
PIECE = 32
FAR = ("ep", "chip", "core")
SWAP = [(0, 1), (1, 0)]
LIMIT = pltpu.CompilerParams(vmem_limit_bytes=16 * 1024 * 1024)


def iota(shape, dim):
    return lax.broadcasted_iota(jnp.int32, shape, dim)


def to_column(row):
    size = row.shape[1]
    square = (size, size)
    return jnp.sum(jnp.where(iota(square, 0) == iota(square, 1), row, 0.0), axis=1, keepdims=True)


def slot_codes(ids, resident):
    row_count = ids.shape[1]
    expert = jnp.min(ids, axis=0, keepdims=True)
    onehot_shape = (-(-resident // 16) * 16, row_count)
    onehot = jnp.where(expert == iota(onehot_shape, 0).astype(jnp.float32), 1.0, 0.0)
    square = (row_count, row_count)
    earlier = jnp.where(iota(square, 0) < iota(square, 1), 1.0, 0.0).astype(jnp.bfloat16)
    counts = jnp.dot(onehot.astype(jnp.bfloat16), earlier, preferred_element_type=jnp.float32)
    return expert * CAP + jnp.sum(counts * onehot, axis=0, keepdims=True), expert


def first_order(ep_count):
    return [z ^ 2 for z in range(ep_count)]


def second_order(ep_count):
    return list(reversed(range(ep_count)))


def flip(chip, z):
    return (z >> 1) & 1


def row_codes(index, order):
    listed = lax.rem(index // CAP, len(order))
    expert = sum(jnp.where(listed == at, z // 2, 0) for at, z in enumerate(order))
    return (expert * CAP + lax.rem(index, CAP)).astype(jnp.float32)


def route(ep_count, ids_hbm, tokens_hbm, outgoing_ref, ids_ref, tokens_ref, sems):
    row_count = ids_ref.shape[1]
    parts = row_count // PIECE
    copies = [pltpu.make_async_copy(ids_hbm, ids_ref, sems.at[parts])] + [
        pltpu.make_async_copy(
            tokens_hbm.at[pl.ds(part * PIECE, PIECE), :],
            tokens_ref.at[pl.ds(part * PIECE, PIECE), :],
            sems.at[part],
        )
        for part in range(parts)
    ]
    for copy in copies:
        copy.start()
    wanted = row_codes(iota((outgoing_ref.shape[0], row_count), 0), first_order(ep_count))
    copies[0].wait()
    code, _ = slot_codes(ids_ref[...].astype(jnp.float32), ep_count // 2)
    dispatch = jnp.where(code == wanted, 1.0, 0.0).astype(jnp.bfloat16)
    for copy in copies[1:]:
        copy.wait()
    outgoing_ref[...] = jnp.dot(
        dispatch, tokens_ref[...], preferred_element_type=jnp.float32
    ).astype(jnp.bfloat16)


def score(ep_count, ids_ref, scores_ref, _, match_ref, weight_ref):
    ids = ids_ref[...].astype(jnp.float32)
    code, expert = slot_codes(ids, ep_count // 2)
    wanted = row_codes(iota(match_ref.shape, 1), second_order(ep_count))
    match_ref[...] = jnp.where(to_column(code) == wanted, 1.0, 0.0).astype(jnp.bfloat16)
    squashed = jax.nn.sigmoid(scores_ref[...])
    chosen = jnp.sum(jnp.where(ids == expert, squashed, 0.0), axis=0, keepdims=True)
    weight_ref[...] = to_column(2.5 * chosen / jnp.sum(squashed, axis=0, keepdims=True))


def far_groups(order, chips):
    return [
        [(z * chips + x) * 2 + (side + flip(x, z)) % 2 for x in range(chips) for z in order]
        for side in range(2)
    ]


def turned(chip, z):
    side = lax.axis_index("core") ^ flip(lax.axis_index("chip"), lax.axis_index("ep"))
    return (side ^ flip(chip, z)) == 1


def theirs(chips, own_ref, across_ref, gate_ref, up_ref, down_ref, mine_ref, other_ref):
    part_rows, features = own_ref.shape[0] // chips, own_ref.shape[1]
    first, second = first_order(part_rows // CAP), second_order(part_rows // CAP)
    width = gate_ref.shape[2]
    acts = jnp.zeros((part_rows, 2 * width), jnp.float32)
    for chip in range(chips):
        sides = [[], []]
        at = 0
        while at < len(first):
            end = at + 1
            while end < len(first) and flip(chip, first[end]) == flip(chip, first[at]):
                end += 1
            rows = slice(chip * part_rows + at * CAP, chip * part_rows + end * CAP)
            own, across = own_ref[rows, :], across_ref[rows, :]
            second_core = turned(chip, first[at])
            sides[0].append(jnp.where(second_core, across, own))
            sides[1].append(jnp.where(second_core, own, across))
            at = end
        for core in range(2):
            columns = slice((2 * chip + core) * features, (2 * chip + core + 1) * features)
            both = jnp.concatenate([gate_ref[0, columns, :], up_ref[0, columns, :]], axis=1)
            rows = jnp.concatenate(sides[core], axis=0)
            acts += jnp.dot(rows, both, preferred_element_type=jnp.float32)
    gate_act, up_act = acts[:, :width], acts[:, width:]
    hidden = (gate_act / (1.0 + jnp.exp(-gate_act)) * up_act).astype(jnp.bfloat16)
    for chip in range(chips):
        values = []
        for core in range(2):
            columns = slice((2 * chip + core) * features, (2 * chip + core + 1) * features)
            values.append(
                jnp.dot(hidden, down_ref[0, :, columns], preferred_element_type=jnp.float32)
            )
        mine, other = [], []
        for z in second:
            rows = slice(first.index(z) * CAP, (first.index(z) + 1) * CAP)
            second_core = turned(chip, z)
            mine.append(jnp.where(second_core, values[1][rows, :], values[0][rows, :]))
            other.append(jnp.where(second_core, values[0][rows, :], values[1][rows, :]))
        rows = slice(chip * part_rows, (chip + 1) * part_rows)
        mine_ref[rows, :] = jnp.concatenate(mine, axis=0).astype(jnp.bfloat16)
        other_ref[rows, :] = jnp.concatenate(other, axis=0).astype(jnp.bfloat16)


def add(mine_ref, other_ref, _, out_ref):
    total = mine_ref[...].astype(jnp.float32) + other_ref[...].astype(jnp.float32)
    out_ref[...] = total.astype(jnp.bfloat16)


def combine(match_ref, weight_ref, returned_ref, out_hbm, out_ref, sems):
    copies = []
    for part in range(out_ref.shape[0] // PIECE):
        rows = pl.ds(part * PIECE, PIECE)
        summed = jnp.dot(match_ref[rows, :], returned_ref[...], preferred_element_type=jnp.float32)
        out_ref[rows, :] = (weight_ref[rows, :] * summed).astype(jnp.bfloat16)
        copies.append(pltpu.make_async_copy(out_ref.at[rows, :], out_hbm.at[rows, :], sems.at[part]))
        copies[-1].start()
    for copy in copies:
        copy.wait()


def shards(tokens, expert_ids, route_scores, w_gate, w_up, w_down):
    row_count, features = tokens.shape
    top_count = expert_ids.shape[1]
    ep_count, chips = lax.axis_size("ep"), lax.axis_size("chip")
    slot_count = ep_count * CAP
    half = jax.ShapeDtypeStruct((chips * slot_count, features), jnp.bfloat16)
    ids, scores = expert_ids.T, route_scores.T
    hbm, vmem = (pl.BlockSpec(memory_space=space) for space in (pltpu.HBM, pltpu.VMEM))
    anywhere = pl.BlockSpec(memory_space=pl.ANY)

    def exchange(rows, order):
        groups = far_groups(order(ep_count), chips)
        return lax.all_to_all(rows, FAR, 0, 0, axis_index_groups=groups, tiled=True)

    def call(kernel, name, out_shape, **rest):
        return pl.pallas_call(kernel, out_shape=out_shape, name=name, compiler_params=LIMIT, **rest)

    outgoing = call(
        lambda *refs: route(ep_count, *refs),
        "route",
        half,
        in_specs=[hbm] * 2,
        scratch_shapes=[
            pltpu.VMEM((top_count, row_count), jnp.int32),
            pltpu.VMEM((row_count, features), jnp.bfloat16),
            pltpu.SemaphoreType.DMA((row_count // PIECE + 1,)),
        ],
        cost_estimate=pl.CostEstimate(flops=2 * 10**9, bytes_accessed=0, transcendentals=0),
    )(*(pltpu.with_memory_space_constraint(value, pltpu.HBM) for value in (ids, tokens)))
    incoming = exchange(outgoing, first_order)
    across = lax.ppermute(incoming, "core", SWAP)
    mine, other = call(lambda *refs: theirs(chips, *refs), "theirs", (half, half))(
        incoming, across, w_gate, w_up, w_down
    )
    crossed = lax.ppermute(other, "core", SWAP)
    match, weight = call(
        lambda *refs: score(ep_count, *refs),
        "score",
        (
            jax.ShapeDtypeStruct((row_count, chips * slot_count), jnp.bfloat16),
            jax.ShapeDtypeStruct((row_count, 1), jnp.float32),
        ),
        in_specs=[vmem] * 2 + [anywhere],
    )(ids, scores, incoming)
    summed = call(add, "add", half, in_specs=[vmem] * 2 + [anywhere])(mine, crossed, weight)
    returned = exchange(summed, second_order)
    return call(
        combine,
        "combine",
        jax.ShapeDtypeStruct((row_count, features), jnp.bfloat16),
        out_specs=hbm,
        scratch_shapes=[
            pltpu.VMEM((row_count, features), jnp.bfloat16),
            pltpu.SemaphoreType.DMA((row_count // PIECE,)),
        ],
    )(match, weight, returned)


def solution(mesh):
    groups, ep_count, tp_count = (mesh.shape[name] for name in ("groups", "ep", "tp"))
    split = jax.sharding.Mesh(
        mesh.devices.reshape(groups, ep_count, tp_count // 2, 2), ("groups", "ep", "chip", "core")
    )
    tp = ("chip", "core")
    placed = (
        P(("groups", "ep"), tp),
        P(("groups", "ep"), None),
        P(("groups", "ep"), None),
        P("ep", None, tp),
        P("ep", None, tp),
        P("ep", tp, None),
    )
    return jax.shard_map(
        shards, mesh=split, in_specs=placed, out_specs=P(("groups", "ep"), tp), check_vma=False
    )
```

```python
import jax
import jax.numpy as jnp
from jax import lax
from jax.experimental import pallas as pl
from jax.experimental.pallas import tpu as pltpu
from jax.sharding import PartitionSpec as P

CAP = 8
PIECE = 32
FAR = ("ep", "chip", "core")
SWAP = [(0, 1), (1, 0)]
LIMIT = pltpu.CompilerParams(vmem_limit_bytes=16 * 1024 * 1024)


def iota(shape, dim):
    return lax.broadcasted_iota(jnp.int32, shape, dim)


def to_column(row):
    size = row.shape[1]
    square = (size, size)
    return jnp.sum(jnp.where(iota(square, 0) == iota(square, 1), row, 0.0), axis=1, keepdims=True)


def slot_codes(ids, resident):
    row_count = ids.shape[1]
    expert = jnp.min(ids, axis=0, keepdims=True)
    onehot_shape = (-(-resident // 16) * 16, row_count)
    onehot = jnp.where(expert == iota(onehot_shape, 0).astype(jnp.float32), 1.0, 0.0)
    square = (row_count, row_count)
    earlier = jnp.where(iota(square, 0) < iota(square, 1), 1.0, 0.0).astype(jnp.bfloat16)
    counts = jnp.dot(onehot.astype(jnp.bfloat16), earlier, preferred_element_type=jnp.float32)
    return expert * CAP + jnp.sum(counts * onehot, axis=0, keepdims=True), expert


def first_order(ep_count):
    return [z ^ 2 for z in range(ep_count)]


def second_order(ep_count):
    return list(reversed(range(ep_count)))


def first_flip(chip, z):
    return chip & 1


def second_flip(chip, z):
    return (z >> 1) & 1


def row_codes(index, order):
    listed = lax.rem(index // CAP, len(order))
    expert = sum(jnp.where(listed == at, z // 2, 0) for at, z in enumerate(order))
    return (expert * CAP + lax.rem(index, CAP)).astype(jnp.float32)


def route(ep_count, ids_hbm, tokens_hbm, outgoing_ref, ids_ref, tokens_ref, sems):
    row_count = ids_ref.shape[1]
    parts = row_count // PIECE
    copies = [pltpu.make_async_copy(ids_hbm, ids_ref, sems.at[parts])] + [
        pltpu.make_async_copy(
            tokens_hbm.at[pl.ds(part * PIECE, PIECE), :],
            tokens_ref.at[pl.ds(part * PIECE, PIECE), :],
            sems.at[part],
        )
        for part in range(parts)
    ]
    for copy in copies:
        copy.start()
    wanted = row_codes(iota((outgoing_ref.shape[0], row_count), 0), first_order(ep_count))
    copies[0].wait()
    code, _ = slot_codes(ids_ref[...].astype(jnp.float32), ep_count // 2)
    dispatch = jnp.where(code == wanted, 1.0, 0.0).astype(jnp.bfloat16)
    for copy in copies[1:]:
        copy.wait()
    outgoing_ref[...] = jnp.dot(
        dispatch, tokens_ref[...], preferred_element_type=jnp.float32
    ).astype(jnp.bfloat16)


def score(ep_count, ids_ref, scores_ref, _, match_ref, weight_ref):
    ids = ids_ref[...].astype(jnp.float32)
    code, expert = slot_codes(ids, ep_count // 2)
    wanted = row_codes(iota(match_ref.shape, 1), second_order(ep_count))
    match_ref[...] = jnp.where(to_column(code) == wanted, 1.0, 0.0).astype(jnp.bfloat16)
    squashed = jax.nn.sigmoid(scores_ref[...])
    chosen = jnp.sum(jnp.where(ids == expert, squashed, 0.0), axis=0, keepdims=True)
    weight_ref[...] = to_column(2.5 * chosen / jnp.sum(squashed, axis=0, keepdims=True))


def far_groups(order, flip, chips):
    return [
        [(z * chips + x) * 2 + (side + flip(x, z)) % 2 for x in range(chips) for z in order]
        for side in range(2)
    ]


def core_there(flip, chip, z):
    here = flip(lax.axis_index("chip"), lax.axis_index("ep"))
    return lax.axis_index("core") ^ here ^ flip(chip, z)


def lift(chips, own, rows_ref, gate_ref, up_ref):
    part_rows, features = rows_ref.shape[0] // chips, rows_ref.shape[1]
    acts = jnp.zeros((part_rows, 2 * gate_ref.shape[2]), jnp.float32)
    for chip in range(chips):
        rows = rows_ref[chip * part_rows : (chip + 1) * part_rows, :]
        core = core_there(first_flip, chip, 0)
        core = core if own else 1 - core
        columns = pl.ds(pl.multiple_of((2 * chip + core) * features, features), features)
        both = jnp.concatenate([gate_ref[0, columns, :], up_ref[0, columns, :]], axis=1)
        acts += jnp.dot(rows, both, preferred_element_type=jnp.float32)
    return acts


def begin(chips, rows_ref, gate_ref, up_ref, acts_ref):
    acts_ref[...] = lift(chips, True, rows_ref, gate_ref, up_ref)


def theirs(chips, rows_ref, acts_ref, gate_ref, up_ref, down_ref, mine_ref, other_ref):
    part_rows, features = mine_ref.shape[0] // chips, mine_ref.shape[1]
    first, second = first_order(part_rows // CAP), second_order(part_rows // CAP)
    width = gate_ref.shape[2]
    acts = acts_ref[...] + lift(chips, False, rows_ref, gate_ref, up_ref)
    gate_act, up_act = acts[:, :width], acts[:, width:]
    hidden = (gate_act / (1.0 + jnp.exp(-gate_act)) * up_act).astype(jnp.bfloat16)
    for chip in range(chips):
        values = []
        for core in range(2):
            columns = slice((2 * chip + core) * features, (2 * chip + core + 1) * features)
            values.append(
                jnp.dot(hidden, down_ref[0, :, columns], preferred_element_type=jnp.float32)
            )
        mine, other = [], []
        for z in second:
            rows = slice(first.index(z) * CAP, (first.index(z) + 1) * CAP)
            second_core = core_there(second_flip, chip, z) == 1
            mine.append(jnp.where(second_core, values[1][rows, :], values[0][rows, :]))
            other.append(jnp.where(second_core, values[0][rows, :], values[1][rows, :]))
        rows = slice(chip * part_rows, (chip + 1) * part_rows)
        mine_ref[rows, :] = jnp.concatenate(mine, axis=0).astype(jnp.bfloat16)
        other_ref[rows, :] = jnp.concatenate(other, axis=0).astype(jnp.bfloat16)


def add(mine_ref, other_ref, _, out_ref):
    total = mine_ref[...].astype(jnp.float32) + other_ref[...].astype(jnp.float32)
    out_ref[...] = total.astype(jnp.bfloat16)


def combine(match_ref, weight_ref, returned_ref, out_hbm, out_ref, sems):
    copies = []
    for part in range(out_ref.shape[0] // PIECE):
        rows = pl.ds(part * PIECE, PIECE)
        summed = jnp.dot(match_ref[rows, :], returned_ref[...], preferred_element_type=jnp.float32)
        out_ref[rows, :] = (weight_ref[rows, :] * summed).astype(jnp.bfloat16)
        copies.append(pltpu.make_async_copy(out_ref.at[rows, :], out_hbm.at[rows, :], sems.at[part]))
        copies[-1].start()
    for copy in copies:
        copy.wait()


def shards(tokens, expert_ids, route_scores, w_gate, w_up, w_down):
    row_count, features = tokens.shape
    top_count, hidden_count = expert_ids.shape[1], w_gate.shape[2]
    ep_count, chips = lax.axis_size("ep"), lax.axis_size("chip")
    slot_count = ep_count * CAP
    half = jax.ShapeDtypeStruct((chips * slot_count, features), jnp.bfloat16)
    ids, scores = expert_ids.T, route_scores.T
    hbm, vmem = (pl.BlockSpec(memory_space=space) for space in (pltpu.HBM, pltpu.VMEM))
    anywhere = pl.BlockSpec(memory_space=pl.ANY)

    def exchange(rows, order, flip):
        groups = far_groups(order(ep_count), flip, chips)
        return lax.all_to_all(rows, FAR, 0, 0, axis_index_groups=groups, tiled=True)

    def call(kernel, name, out_shape, **rest):
        return pl.pallas_call(kernel, out_shape=out_shape, name=name, compiler_params=LIMIT, **rest)

    outgoing = call(
        lambda *refs: route(ep_count, *refs),
        "route",
        half,
        in_specs=[hbm] * 2,
        scratch_shapes=[
            pltpu.VMEM((top_count, row_count), jnp.int32),
            pltpu.VMEM((row_count, features), jnp.bfloat16),
            pltpu.SemaphoreType.DMA((row_count // PIECE + 1,)),
        ],
        cost_estimate=pl.CostEstimate(flops=2 * 10**9, bytes_accessed=0, transcendentals=0),
    )(*(pltpu.with_memory_space_constraint(value, pltpu.HBM) for value in (ids, tokens)))
    incoming = exchange(outgoing, first_order, first_flip)
    across = lax.ppermute(incoming, "core", SWAP)
    acts = jax.ShapeDtypeStruct((slot_count, 2 * hidden_count), jnp.float32)
    begun = call(lambda *refs: begin(chips, *refs), "begin", acts)(incoming, w_gate, w_up)
    mine, other = call(lambda *refs: theirs(chips, *refs), "theirs", (half, half))(
        across, begun, w_gate, w_up, w_down
    )
    crossed = lax.ppermute(other, "core", SWAP)
    match, weight = call(
        lambda *refs: score(ep_count, *refs),
        "score",
        (
            jax.ShapeDtypeStruct((row_count, chips * slot_count), jnp.bfloat16),
            jax.ShapeDtypeStruct((row_count, 1), jnp.float32),
        ),
        in_specs=[vmem] * 2 + [anywhere],
    )(ids, scores, other)
    summed = call(add, "add", half, in_specs=[vmem] * 2 + [anywhere])(mine, crossed, weight)
    returned = exchange(summed, second_order, second_flip)
    return call(
        combine,
        "combine",
        jax.ShapeDtypeStruct((row_count, features), jnp.bfloat16),
        out_specs=hbm,
        scratch_shapes=[
            pltpu.VMEM((row_count, features), jnp.bfloat16),
            pltpu.SemaphoreType.DMA((row_count // PIECE,)),
        ],
    )(match, weight, returned)


def solution(mesh):
    groups, ep_count, tp_count = (mesh.shape[name] for name in ("groups", "ep", "tp"))
    split = jax.sharding.Mesh(
        mesh.devices.reshape(groups, ep_count, tp_count // 2, 2), ("groups", "ep", "chip", "core")
    )
    tp = ("chip", "core")
    placed = (
        P(("groups", "ep"), tp),
        P(("groups", "ep"), None),
        P(("groups", "ep"), None),
        P("ep", None, tp),
        P("ep", None, tp),
        P("ep", tp, None),
    )
    return jax.shard_map(
        shards, mesh=split, in_specs=placed, out_specs=P(("groups", "ep"), tp), check_vma=False
    )
```

```python
import jax
import jax.numpy as jnp
from jax import lax
from jax.experimental import pallas as pl
from jax.experimental.pallas import tpu as pltpu
from jax.sharding import PartitionSpec as P

CAP = 8
PIECE = 32
FAR = ("ep", "chip", "core")
SWAP = [(0, 1), (1, 0)]
LIMIT = pltpu.CompilerParams(vmem_limit_bytes=16 * 1024 * 1024)


def iota(shape, dim):
    return lax.broadcasted_iota(jnp.int32, shape, dim)


def to_column(row):
    size = row.shape[1]
    square = (size, size)
    return jnp.sum(jnp.where(iota(square, 0) == iota(square, 1), row, 0.0), axis=1, keepdims=True)


def slot_codes(ids, resident):
    row_count = ids.shape[1]
    expert = jnp.min(ids, axis=0, keepdims=True)
    onehot_shape = (-(-resident // 16) * 16, row_count)
    onehot = jnp.where(expert == iota(onehot_shape, 0).astype(jnp.float32), 1.0, 0.0)
    square = (row_count, row_count)
    earlier = jnp.where(iota(square, 0) < iota(square, 1), 1.0, 0.0).astype(jnp.bfloat16)
    counts = jnp.dot(onehot.astype(jnp.bfloat16), earlier, preferred_element_type=jnp.float32)
    return expert * CAP + jnp.sum(counts * onehot, axis=0, keepdims=True), expert


def first_order(ep_count, chip):
    return [z ^ 2 for z in range(ep_count)] if chip % 2 == 0 else list(reversed(range(ep_count)))


def second_order(ep_count, chip):
    return list(reversed(range(ep_count)))


def row_codes(index, order, ep_count, chips):
    listed = [z for chip in range(chips) for z in order(ep_count, chip)]
    expert = sum(jnp.where(index // CAP == at, z // 2, 0) for at, z in enumerate(listed))
    return (expert * CAP + lax.rem(index, CAP)).astype(jnp.float32)


def route(ep_count, chips, ids_hbm, tokens_hbm, outgoing_ref, ids_ref, tokens_ref, sems):
    row_count = ids_ref.shape[1]
    parts = row_count // PIECE
    copies = [pltpu.make_async_copy(ids_hbm, ids_ref, sems.at[parts])] + [
        pltpu.make_async_copy(
            tokens_hbm.at[pl.ds(part * PIECE, PIECE), :],
            tokens_ref.at[pl.ds(part * PIECE, PIECE), :],
            sems.at[part],
        )
        for part in range(parts)
    ]
    for copy in copies:
        copy.start()
    wanted = row_codes(iota((outgoing_ref.shape[0], row_count), 0), first_order, ep_count, chips)
    copies[0].wait()
    code, _ = slot_codes(ids_ref[...].astype(jnp.float32), ep_count // 2)
    dispatch = jnp.where(code == wanted, 1.0, 0.0).astype(jnp.bfloat16)
    for copy in copies[1:]:
        copy.wait()
    outgoing_ref[...] = jnp.dot(
        dispatch, tokens_ref[...], preferred_element_type=jnp.float32
    ).astype(jnp.bfloat16)


def score(ep_count, chips, ids_ref, scores_ref, _, match_ref, weight_ref):
    ids = ids_ref[...].astype(jnp.float32)
    code, expert = slot_codes(ids, ep_count // 2)
    wanted = row_codes(iota(match_ref.shape, 1), second_order, ep_count, chips)
    match_ref[...] = jnp.where(to_column(code) == wanted, 1.0, 0.0).astype(jnp.bfloat16)
    squashed = jax.nn.sigmoid(scores_ref[...])
    chosen = jnp.sum(jnp.where(ids == expert, squashed, 0.0), axis=0, keepdims=True)
    weight_ref[...] = to_column(2.5 * chosen / jnp.sum(squashed, axis=0, keepdims=True))


def far_groups(order, ep_count, chips):
    return [
        [(z * chips + x) * 2 + (side + x) % 2 for x in range(chips) for z in order(ep_count, x)]
        for side in range(2)
    ]


def columns_of(chip, own, features):
    core = lax.rem(lax.axis_index("core") + lax.axis_index("chip") + chip + (0 if own else 1), 2)
    return pl.ds(pl.multiple_of((2 * chip + core) * features, features), features)


def in_order(values, held, wanted):
    if held == wanted:
        return values
    blocks = [values[held.index(z) * CAP : (held.index(z) + 1) * CAP, :] for z in wanted]
    return jnp.concatenate(blocks, axis=0)


def lift(chips, own, rows_ref, gate_ref, up_ref):
    part_rows, features = rows_ref.shape[0] // chips, rows_ref.shape[1]
    ep_count = part_rows // CAP
    total = jnp.zeros((part_rows, 2 * gate_ref.shape[2]), jnp.float32)
    for chip in range(chips):
        rows = rows_ref[chip * part_rows : (chip + 1) * part_rows, :]
        columns = columns_of(chip, own, features)
        both = jnp.concatenate([gate_ref[0, columns, :], up_ref[0, columns, :]], axis=1)
        acts = jnp.dot(rows, both, preferred_element_type=jnp.float32)
        total += in_order(acts, first_order(ep_count, chip), first_order(ep_count, 0))
    return total


def lower(chips, own, hidden, down_ref, out_ref):
    part_rows, features = out_ref.shape[0] // chips, out_ref.shape[1]
    ep_count = part_rows // CAP
    for chip in range(chips):
        columns = columns_of(chip, own, features)
        values = jnp.dot(hidden, down_ref[0, :, columns], preferred_element_type=jnp.float32)
        values = in_order(values, first_order(ep_count, 0), second_order(ep_count, chip))
        out_ref[chip * part_rows : (chip + 1) * part_rows, :] = values.astype(jnp.bfloat16)


def begin(chips, rows_ref, gate_ref, up_ref, acts_ref):
    acts_ref[...] = lift(chips, True, rows_ref, gate_ref, up_ref)


def theirs(chips, rows_ref, acts_ref, gate_ref, up_ref, down_ref, hidden_ref, other_ref):
    width = gate_ref.shape[2]
    acts = acts_ref[...] + lift(chips, False, rows_ref, gate_ref, up_ref)
    gate_act, up_act = acts[:, :width], acts[:, width:]
    hidden = (gate_act / (1.0 + jnp.exp(-gate_act)) * up_act).astype(jnp.bfloat16)
    hidden_ref[...] = hidden
    lower(chips, False, hidden, down_ref, other_ref)


def ours(chips, hidden_ref, down_ref, mine_ref):
    lower(chips, True, hidden_ref[...], down_ref, mine_ref)


def add(mine_ref, other_ref, _, out_ref):
    total = mine_ref[...].astype(jnp.float32) + other_ref[...].astype(jnp.float32)
    out_ref[...] = total.astype(jnp.bfloat16)


def combine(match_ref, weight_ref, returned_ref, out_hbm, out_ref, sems):
    copies = []
    for part in range(out_ref.shape[0] // PIECE):
        rows = pl.ds(part * PIECE, PIECE)
        summed = jnp.dot(match_ref[rows, :], returned_ref[...], preferred_element_type=jnp.float32)
        out_ref[rows, :] = (weight_ref[rows, :] * summed).astype(jnp.bfloat16)
        copies.append(pltpu.make_async_copy(out_ref.at[rows, :], out_hbm.at[rows, :], sems.at[part]))
        copies[-1].start()
    for copy in copies:
        copy.wait()


def shards(tokens, expert_ids, route_scores, w_gate, w_up, w_down):
    row_count, features = tokens.shape
    top_count, hidden_count = expert_ids.shape[1], w_gate.shape[2]
    ep_count, chips = lax.axis_size("ep"), lax.axis_size("chip")
    slot_count = ep_count * CAP
    half = jax.ShapeDtypeStruct((chips * slot_count, features), jnp.bfloat16)
    ids, scores = expert_ids.T, route_scores.T
    hbm, vmem = (pl.BlockSpec(memory_space=space) for space in (pltpu.HBM, pltpu.VMEM))
    anywhere = pl.BlockSpec(memory_space=pl.ANY)

    def exchange(rows, order):
        groups = far_groups(order, ep_count, chips)
        return lax.all_to_all(rows, FAR, 0, 0, axis_index_groups=groups, tiled=True)

    def call(kernel, name, out_shape, **rest):
        return pl.pallas_call(kernel, out_shape=out_shape, name=name, compiler_params=LIMIT, **rest)

    outgoing = call(
        lambda *refs: route(ep_count, chips, *refs),
        "route",
        half,
        in_specs=[hbm] * 2,
        scratch_shapes=[
            pltpu.VMEM((top_count, row_count), jnp.int32),
            pltpu.VMEM((row_count, features), jnp.bfloat16),
            pltpu.SemaphoreType.DMA((row_count // PIECE + 1,)),
        ],
        cost_estimate=pl.CostEstimate(flops=2 * 10**9, bytes_accessed=0, transcendentals=0),
    )(*(pltpu.with_memory_space_constraint(value, pltpu.HBM) for value in (ids, tokens)))
    incoming = exchange(outgoing, first_order)
    across = lax.ppermute(incoming, "core", SWAP)
    acts = jax.ShapeDtypeStruct((slot_count, 2 * hidden_count), jnp.float32)
    begun = call(lambda *refs: begin(chips, *refs), "begin", acts)(incoming, w_gate, w_up)
    hidden_shape = jax.ShapeDtypeStruct((slot_count, hidden_count), jnp.bfloat16)
    hidden, other = call(lambda *refs: theirs(chips, *refs), "theirs", (hidden_shape, half))(
        across, begun, w_gate, w_up, w_down
    )
    crossed = lax.ppermute(other, "core", SWAP)
    mine = call(lambda *refs: ours(chips, *refs), "ours", half)(hidden, w_down)
    match, weight = call(
        lambda *refs: score(ep_count, chips, *refs),
        "score",
        (
            jax.ShapeDtypeStruct((row_count, chips * slot_count), jnp.bfloat16),
            jax.ShapeDtypeStruct((row_count, 1), jnp.float32),
        ),
        in_specs=[vmem] * 2 + [anywhere],
    )(ids, scores, other)
    summed = call(add, "add", half, in_specs=[vmem] * 2 + [anywhere])(mine, crossed, weight)
    returned = exchange(summed, second_order)
    return call(
        combine,
        "combine",
        jax.ShapeDtypeStruct((row_count, features), jnp.bfloat16),
        out_specs=hbm,
        scratch_shapes=[
            pltpu.VMEM((row_count, features), jnp.bfloat16),
            pltpu.SemaphoreType.DMA((row_count // PIECE,)),
        ],
    )(match, weight, returned)


def solution(mesh):
    groups, ep_count, tp_count = (mesh.shape[name] for name in ("groups", "ep", "tp"))
    split = jax.sharding.Mesh(
        mesh.devices.reshape(groups, ep_count, tp_count // 2, 2), ("groups", "ep", "chip", "core")
    )
    tp = ("chip", "core")
    placed = (
        P(("groups", "ep"), tp),
        P(("groups", "ep"), None),
        P(("groups", "ep"), None),
        P("ep", None, tp),
        P("ep", None, tp),
        P("ep", tp, None),
    )
    return jax.shard_map(
        shards, mesh=split, in_specs=placed, out_specs=P(("groups", "ep"), tp), check_vma=False
    )
```

```python
import jax
import jax.numpy as jnp
from jax import lax
from jax.experimental import pallas as pl
from jax.experimental.pallas import tpu as pltpu
from jax.sharding import PartitionSpec as P

CAP = 8
PIECE = 32
FAR = ("ep", "chip", "core")
SWAP = [(0, 1), (1, 0)]
LIMIT = pltpu.CompilerParams(vmem_limit_bytes=16 * 1024 * 1024)


def iota(shape, dim):
    return lax.broadcasted_iota(jnp.int32, shape, dim)


def to_column(row):
    size = row.shape[1]
    square = (size, size)
    return jnp.sum(jnp.where(iota(square, 0) == iota(square, 1), row, 0.0), axis=1, keepdims=True)


def slot_codes(ids, resident):
    row_count = ids.shape[1]
    expert = jnp.min(ids, axis=0, keepdims=True)
    onehot_shape = (-(-resident // 16) * 16, row_count)
    onehot = jnp.where(expert == iota(onehot_shape, 0).astype(jnp.float32), 1.0, 0.0)
    square = (row_count, row_count)
    earlier = jnp.where(iota(square, 0) < iota(square, 1), 1.0, 0.0).astype(jnp.bfloat16)
    counts = jnp.dot(onehot.astype(jnp.bfloat16), earlier, preferred_element_type=jnp.float32)
    return expert * CAP + jnp.sum(counts * onehot, axis=0, keepdims=True), expert


def first_order(ep_count, chip):
    listed = ((1, 0, 2, 3), (3, 1, 2, 0))[chip % 2]
    return [z // 4 * 4 + listed[z % 4] for z in range(ep_count)]


def second_order(ep_count, chip):
    listed = ((2, 1, 0, 3), (3, 0, 2, 1))[chip % 2]
    return [z // 4 * 4 + listed[z % 4] for z in range(ep_count)]


def row_codes(index, order, ep_count, chips):
    listed = [z for chip in range(chips) for z in order(ep_count, chip)]
    expert = sum(jnp.where(index // CAP == at, z // 2, 0) for at, z in enumerate(listed))
    return (expert * CAP + lax.rem(index, CAP)).astype(jnp.float32)


def route(ep_count, chips, ids_hbm, tokens_hbm, outgoing_ref, ids_ref, tokens_ref, sems):
    row_count = ids_ref.shape[1]
    parts = row_count // PIECE
    copies = [pltpu.make_async_copy(ids_hbm, ids_ref, sems.at[parts])] + [
        pltpu.make_async_copy(
            tokens_hbm.at[pl.ds(part * PIECE, PIECE), :],
            tokens_ref.at[pl.ds(part * PIECE, PIECE), :],
            sems.at[part],
        )
        for part in range(parts)
    ]
    for copy in copies:
        copy.start()
    wanted = row_codes(iota((outgoing_ref.shape[0], row_count), 0), first_order, ep_count, chips)
    copies[0].wait()
    code, _ = slot_codes(ids_ref[...].astype(jnp.float32), ep_count // 2)
    dispatch = jnp.where(code == wanted, 1.0, 0.0).astype(jnp.bfloat16)
    for copy in copies[1:]:
        copy.wait()
    outgoing_ref[...] = jnp.dot(
        dispatch, tokens_ref[...], preferred_element_type=jnp.float32
    ).astype(jnp.bfloat16)


def score(ep_count, chips, ids_ref, scores_ref, _, match_ref, weight_ref):
    ids = ids_ref[...].astype(jnp.float32)
    code, expert = slot_codes(ids, ep_count // 2)
    wanted = row_codes(iota(match_ref.shape, 1), second_order, ep_count, chips)
    match_ref[...] = jnp.where(to_column(code) == wanted, 1.0, 0.0).astype(jnp.bfloat16)
    squashed = jax.nn.sigmoid(scores_ref[...])
    chosen = jnp.sum(jnp.where(ids == expert, squashed, 0.0), axis=0, keepdims=True)
    weight_ref[...] = to_column(2.5 * chosen / jnp.sum(squashed, axis=0, keepdims=True))


def far_groups(order, ep_count, chips):
    return [
        [(z * chips + x) * 2 + (side + x) % 2 for x in range(chips) for z in order(ep_count, x)]
        for side in range(2)
    ]


def columns_of(chip, own, features):
    core = lax.rem(lax.axis_index("core") + lax.axis_index("chip") + chip + (0 if own else 1), 2)
    return pl.ds(pl.multiple_of((2 * chip + core) * features, features), features)


def in_order(values, held, wanted):
    if held == wanted:
        return values
    blocks = [values[held.index(z) * CAP : (held.index(z) + 1) * CAP, :] for z in wanted]
    return jnp.concatenate(blocks, axis=0)


def lift(chips, own, rows_ref, gate_ref, up_ref):
    part_rows, features = rows_ref.shape[0] // chips, rows_ref.shape[1]
    ep_count = part_rows // CAP
    total = jnp.zeros((part_rows, 2 * gate_ref.shape[2]), jnp.float32)
    for chip in range(chips):
        rows = rows_ref[chip * part_rows : (chip + 1) * part_rows, :]
        columns = columns_of(chip, own, features)
        both = jnp.concatenate([gate_ref[0, columns, :], up_ref[0, columns, :]], axis=1)
        acts = jnp.dot(rows, both, preferred_element_type=jnp.float32)
        total += in_order(acts, first_order(ep_count, chip), first_order(ep_count, 0))
    return total


def lower(chips, own, hidden, down_ref, out_ref):
    part_rows, features = out_ref.shape[0] // chips, out_ref.shape[1]
    ep_count = part_rows // CAP
    for chip in range(chips):
        columns = columns_of(chip, own, features)
        values = jnp.dot(hidden, down_ref[0, :, columns], preferred_element_type=jnp.float32)
        values = in_order(values, first_order(ep_count, 0), second_order(ep_count, chip))
        out_ref[chip * part_rows : (chip + 1) * part_rows, :] = values.astype(jnp.bfloat16)


def begin(chips, rows_ref, gate_ref, up_ref, acts_ref):
    acts_ref[...] = lift(chips, True, rows_ref, gate_ref, up_ref)


def theirs(chips, rows_ref, acts_ref, gate_ref, up_ref, down_ref, hidden_ref, other_ref):
    width = gate_ref.shape[2]
    acts = acts_ref[...] + lift(chips, False, rows_ref, gate_ref, up_ref)
    gate_act, up_act = acts[:, :width], acts[:, width:]
    hidden = (gate_act / (1.0 + jnp.exp(-gate_act)) * up_act).astype(jnp.bfloat16)
    hidden_ref[...] = hidden
    lower(chips, False, hidden, down_ref, other_ref)


def ours(chips, hidden_ref, down_ref, mine_ref):
    lower(chips, True, hidden_ref[...], down_ref, mine_ref)


def add(mine_ref, other_ref, _, out_ref):
    total = mine_ref[...].astype(jnp.float32) + other_ref[...].astype(jnp.float32)
    out_ref[...] = total.astype(jnp.bfloat16)


def combine(match_ref, weight_ref, returned_ref, out_hbm, out_ref, sems):
    copies = []
    for part in range(out_ref.shape[0] // PIECE):
        rows = pl.ds(part * PIECE, PIECE)
        summed = jnp.dot(match_ref[rows, :], returned_ref[...], preferred_element_type=jnp.float32)
        out_ref[rows, :] = (weight_ref[rows, :] * summed).astype(jnp.bfloat16)
        copies.append(pltpu.make_async_copy(out_ref.at[rows, :], out_hbm.at[rows, :], sems.at[part]))
        copies[-1].start()
    for copy in copies:
        copy.wait()


def shards(tokens, expert_ids, route_scores, w_gate, w_up, w_down):
    row_count, features = tokens.shape
    top_count, hidden_count = expert_ids.shape[1], w_gate.shape[2]
    ep_count, chips = lax.axis_size("ep"), lax.axis_size("chip")
    slot_count = ep_count * CAP
    half = jax.ShapeDtypeStruct((chips * slot_count, features), jnp.bfloat16)
    ids, scores = expert_ids.T, route_scores.T
    hbm, vmem = (pl.BlockSpec(memory_space=space) for space in (pltpu.HBM, pltpu.VMEM))
    anywhere = pl.BlockSpec(memory_space=pl.ANY)

    def exchange(rows, order):
        groups = far_groups(order, ep_count, chips)
        return lax.all_to_all(rows, FAR, 0, 0, axis_index_groups=groups, tiled=True)

    def call(kernel, name, out_shape, **rest):
        return pl.pallas_call(kernel, out_shape=out_shape, name=name, compiler_params=LIMIT, **rest)

    outgoing = call(
        lambda *refs: route(ep_count, chips, *refs),
        "route",
        half,
        in_specs=[hbm] * 2,
        scratch_shapes=[
            pltpu.VMEM((top_count, row_count), jnp.int32),
            pltpu.VMEM((row_count, features), jnp.bfloat16),
            pltpu.SemaphoreType.DMA((row_count // PIECE + 1,)),
        ],
        cost_estimate=pl.CostEstimate(flops=2 * 10**9, bytes_accessed=0, transcendentals=0),
    )(*(pltpu.with_memory_space_constraint(value, pltpu.HBM) for value in (ids, tokens)))
    incoming = exchange(outgoing, first_order)
    across = lax.ppermute(incoming, "core", SWAP)
    acts = jax.ShapeDtypeStruct((slot_count, 2 * hidden_count), jnp.float32)
    begun = call(lambda *refs: begin(chips, *refs), "begin", acts)(incoming, w_gate, w_up)
    hidden_shape = jax.ShapeDtypeStruct((slot_count, hidden_count), jnp.bfloat16)
    hidden, other = call(lambda *refs: theirs(chips, *refs), "theirs", (hidden_shape, half))(
        across, begun, w_gate, w_up, w_down
    )
    crossed = lax.ppermute(other, "core", SWAP)
    mine = call(lambda *refs: ours(chips, *refs), "ours", half)(hidden, w_down)
    match, weight = call(
        lambda *refs: score(ep_count, chips, *refs),
        "score",
        (
            jax.ShapeDtypeStruct((row_count, chips * slot_count), jnp.bfloat16),
            jax.ShapeDtypeStruct((row_count, 1), jnp.float32),
        ),
        in_specs=[vmem] * 2 + [anywhere],
    )(ids, scores, other)
    summed = call(add, "add", half, in_specs=[vmem] * 2 + [anywhere])(mine, crossed, weight)
    returned = exchange(summed, second_order)
    return call(
        combine,
        "combine",
        jax.ShapeDtypeStruct((row_count, features), jnp.bfloat16),
        out_specs=hbm,
        scratch_shapes=[
            pltpu.VMEM((row_count, features), jnp.bfloat16),
            pltpu.SemaphoreType.DMA((row_count // PIECE,)),
        ],
    )(match, weight, returned)


def solution(mesh):
    groups, ep_count, tp_count = (mesh.shape[name] for name in ("groups", "ep", "tp"))
    split = jax.sharding.Mesh(
        mesh.devices.reshape(groups, ep_count, tp_count // 2, 2), ("groups", "ep", "chip", "core")
    )
    tp = ("chip", "core")
    placed = (
        P(("groups", "ep"), tp),
        P(("groups", "ep"), None),
        P(("groups", "ep"), None),
        P("ep", None, tp),
        P("ep", None, tp),
        P("ep", tp, None),
    )
    return jax.shard_map(
        shards, mesh=split, in_specs=placed, out_specs=P(("groups", "ep"), tp), check_vma=False
    )
```

```python
import jax
import jax.numpy as jnp
from jax import lax
from jax.experimental import pallas as pl
from jax.experimental.pallas import tpu as pltpu
from jax.sharding import PartitionSpec as P

CAP = 8
PIECE = 32
FAR = ("ep", "chip", "core")
SWAP = [(0, 1), (1, 0)]
LIMIT = pltpu.CompilerParams(vmem_limit_bytes=16 * 1024 * 1024)


def iota(shape, dim):
    return lax.broadcasted_iota(jnp.int32, shape, dim)


def to_column(row):
    size = row.shape[1]
    square = (size, size)
    return jnp.sum(jnp.where(iota(square, 0) == iota(square, 1), row, 0.0), axis=1, keepdims=True)


def slot_codes(ids, resident):
    row_count = ids.shape[1]
    expert = jnp.min(ids, axis=0, keepdims=True)
    onehot_shape = (-(-resident // 16) * 16, row_count)
    onehot = jnp.where(expert == iota(onehot_shape, 0).astype(jnp.float32), 1.0, 0.0)
    square = (row_count, row_count)
    earlier = jnp.where(iota(square, 0) < iota(square, 1), 1.0, 0.0).astype(jnp.bfloat16)
    counts = jnp.dot(onehot.astype(jnp.bfloat16), earlier, preferred_element_type=jnp.float32)
    return expert * CAP + jnp.sum(counts * onehot, axis=0, keepdims=True), expert


def first_order(ep_count, chip):
    listed = ((2, 3, 0, 1), (3, 2, 1, 0))[chip % 2]
    return [z // 4 * 4 + listed[z % 4] for z in range(ep_count)]


def second_order(ep_count, chip):
    listed = ((2, 1, 0, 3), (3, 0, 2, 1))[chip % 2]
    return [z // 4 * 4 + listed[z % 4] for z in range(ep_count)]


def row_codes(index, order, ep_count, chips):
    listed = [z for chip in range(chips) for z in order(ep_count, chip)]
    expert = sum(jnp.where(index // CAP == at, z // 2, 0) for at, z in enumerate(listed))
    return (expert * CAP + lax.rem(index, CAP)).astype(jnp.float32)


def route(ep_count, chips, ids_hbm, tokens_hbm, outgoing_ref, ids_ref, tokens_ref, sems):
    row_count = ids_ref.shape[1]
    parts = row_count // PIECE
    copies = [pltpu.make_async_copy(ids_hbm, ids_ref, sems.at[parts])] + [
        pltpu.make_async_copy(
            tokens_hbm.at[pl.ds(part * PIECE, PIECE), :],
            tokens_ref.at[pl.ds(part * PIECE, PIECE), :],
            sems.at[part],
        )
        for part in range(parts)
    ]
    for copy in copies:
        copy.start()
    wanted = row_codes(iota((outgoing_ref.shape[0], row_count), 0), first_order, ep_count, chips)
    copies[0].wait()
    code, _ = slot_codes(ids_ref[...].astype(jnp.float32), ep_count // 2)
    dispatch = jnp.where(code == wanted, 1.0, 0.0).astype(jnp.bfloat16)
    for copy in copies[1:]:
        copy.wait()
    outgoing_ref[...] = jnp.dot(
        dispatch, tokens_ref[...], preferred_element_type=jnp.float32
    ).astype(jnp.bfloat16)


def score(ep_count, chips, ids_ref, scores_ref, _, match_ref, weight_ref):
    ids = ids_ref[...].astype(jnp.float32)
    code, expert = slot_codes(ids, ep_count // 2)
    wanted = row_codes(iota(match_ref.shape, 1), second_order, ep_count, chips)
    match_ref[...] = jnp.where(to_column(code) == wanted, 1.0, 0.0).astype(jnp.bfloat16)
    squashed = jax.nn.sigmoid(scores_ref[...])
    chosen = jnp.sum(jnp.where(ids == expert, squashed, 0.0), axis=0, keepdims=True)
    weight_ref[...] = to_column(2.5 * chosen / jnp.sum(squashed, axis=0, keepdims=True))


def far_groups(order, ep_count, chips):
    return [
        [(z * chips + x) * 2 + (side + x) % 2 for x in range(chips) for z in order(ep_count, x)]
        for side in range(2)
    ]


def columns_of(chip, own, features):
    core = lax.rem(lax.axis_index("core") + lax.axis_index("chip") + chip + (0 if own else 1), 2)
    return pl.ds(pl.multiple_of((2 * chip + core) * features, features), features)


def in_order(values, held, wanted):
    if held == wanted:
        return values
    blocks = [values[held.index(z) * CAP : (held.index(z) + 1) * CAP, :] for z in wanted]
    return jnp.concatenate(blocks, axis=0)


def lift(chips, own, rows_ref, gate_ref, up_ref):
    part_rows, features = rows_ref.shape[0] // chips, rows_ref.shape[1]
    ep_count = part_rows // CAP
    total = jnp.zeros((part_rows, 2 * gate_ref.shape[2]), jnp.float32)
    for chip in range(chips):
        rows = rows_ref[chip * part_rows : (chip + 1) * part_rows, :]
        columns = columns_of(chip, own, features)
        both = jnp.concatenate([gate_ref[0, columns, :], up_ref[0, columns, :]], axis=1)
        acts = jnp.dot(rows, both, preferred_element_type=jnp.float32)
        total += in_order(acts, first_order(ep_count, chip), first_order(ep_count, 0))
    return total


def lower(chips, own, hidden, down_ref, out_ref):
    part_rows, features = out_ref.shape[0] // chips, out_ref.shape[1]
    ep_count = part_rows // CAP
    for chip in range(chips):
        columns = columns_of(chip, own, features)
        values = jnp.dot(hidden, down_ref[0, :, columns], preferred_element_type=jnp.float32)
        values = in_order(values, first_order(ep_count, 0), second_order(ep_count, chip))
        out_ref[chip * part_rows : (chip + 1) * part_rows, :] = values.astype(jnp.bfloat16)


def begin(chips, rows_ref, gate_ref, up_ref, acts_ref):
    acts_ref[...] = lift(chips, True, rows_ref, gate_ref, up_ref)


def theirs(chips, rows_ref, acts_ref, gate_ref, up_ref, down_ref, hidden_ref, other_ref):
    width = gate_ref.shape[2]
    acts = acts_ref[...] + lift(chips, False, rows_ref, gate_ref, up_ref)
    gate_act, up_act = acts[:, :width], acts[:, width:]
    hidden = (gate_act / (1.0 + jnp.exp(-gate_act)) * up_act).astype(jnp.bfloat16)
    hidden_ref[...] = hidden
    lower(chips, False, hidden, down_ref, other_ref)


def ours(chips, hidden_ref, down_ref, mine_ref):
    lower(chips, True, hidden_ref[...], down_ref, mine_ref)


def add(mine_ref, other_ref, _, out_ref):
    total = mine_ref[...].astype(jnp.float32) + other_ref[...].astype(jnp.float32)
    out_ref[...] = total.astype(jnp.bfloat16)


def combine(match_ref, weight_ref, returned_ref, out_hbm, out_ref, sems):
    copies = []
    for part in range(out_ref.shape[0] // PIECE):
        rows = pl.ds(part * PIECE, PIECE)
        summed = jnp.dot(match_ref[rows, :], returned_ref[...], preferred_element_type=jnp.float32)
        out_ref[rows, :] = (weight_ref[rows, :] * summed).astype(jnp.bfloat16)
        copies.append(pltpu.make_async_copy(out_ref.at[rows, :], out_hbm.at[rows, :], sems.at[part]))
        copies[-1].start()
    for copy in copies:
        copy.wait()


def shards(tokens, expert_ids, route_scores, w_gate, w_up, w_down):
    row_count, features = tokens.shape
    top_count, hidden_count = expert_ids.shape[1], w_gate.shape[2]
    ep_count, chips = lax.axis_size("ep"), lax.axis_size("chip")
    slot_count = ep_count * CAP
    half = jax.ShapeDtypeStruct((chips * slot_count, features), jnp.bfloat16)
    ids, scores = expert_ids.T, route_scores.T
    hbm, vmem = (pl.BlockSpec(memory_space=space) for space in (pltpu.HBM, pltpu.VMEM))
    anywhere = pl.BlockSpec(memory_space=pl.ANY)

    def exchange(rows, order):
        groups = far_groups(order, ep_count, chips)
        return lax.all_to_all(rows, FAR, 0, 0, axis_index_groups=groups, tiled=True)

    def call(kernel, name, out_shape, **rest):
        return pl.pallas_call(kernel, out_shape=out_shape, name=name, compiler_params=LIMIT, **rest)

    outgoing = call(
        lambda *refs: route(ep_count, chips, *refs),
        "route",
        half,
        in_specs=[hbm] * 2,
        scratch_shapes=[
            pltpu.VMEM((top_count, row_count), jnp.int32),
            pltpu.VMEM((row_count, features), jnp.bfloat16),
            pltpu.SemaphoreType.DMA((row_count // PIECE + 1,)),
        ],
        cost_estimate=pl.CostEstimate(flops=2 * 10**9, bytes_accessed=0, transcendentals=0),
    )(*(pltpu.with_memory_space_constraint(value, pltpu.HBM) for value in (ids, tokens)))
    incoming = exchange(outgoing, first_order)
    across = lax.ppermute(incoming, "core", SWAP)
    acts = jax.ShapeDtypeStruct((slot_count, 2 * hidden_count), jnp.float32)
    begun = call(lambda *refs: begin(chips, *refs), "begin", acts)(incoming, w_gate, w_up)
    hidden_shape = jax.ShapeDtypeStruct((slot_count, hidden_count), jnp.bfloat16)
    hidden, other = call(lambda *refs: theirs(chips, *refs), "theirs", (hidden_shape, half))(
        across, begun, w_gate, w_up, w_down
    )
    crossed = lax.ppermute(other, "core", SWAP)
    mine = call(lambda *refs: ours(chips, *refs), "ours", half)(hidden, w_down)
    match, weight = call(
        lambda *refs: score(ep_count, chips, *refs),
        "score",
        (
            jax.ShapeDtypeStruct((row_count, chips * slot_count), jnp.bfloat16),
            jax.ShapeDtypeStruct((row_count, 1), jnp.float32),
        ),
        in_specs=[vmem] * 2 + [anywhere],
    )(ids, scores, other)
    summed = call(add, "add", half, in_specs=[vmem] * 2 + [anywhere])(mine, crossed, weight)
    returned = exchange(summed, second_order)
    return call(
        combine,
        "combine",
        jax.ShapeDtypeStruct((row_count, features), jnp.bfloat16),
        out_specs=hbm,
        scratch_shapes=[
            pltpu.VMEM((row_count, features), jnp.bfloat16),
            pltpu.SemaphoreType.DMA((row_count // PIECE,)),
        ],
    )(match, weight, returned)


def solution(mesh):
    groups, ep_count, tp_count = (mesh.shape[name] for name in ("groups", "ep", "tp"))
    split = jax.sharding.Mesh(
        mesh.devices.reshape(groups, ep_count, tp_count // 2, 2), ("groups", "ep", "chip", "core")
    )
    tp = ("chip", "core")
    placed = (
        P(("groups", "ep"), tp),
        P(("groups", "ep"), None),
        P(("groups", "ep"), None),
        P("ep", None, tp),
        P("ep", None, tp),
        P("ep", tp, None),
    )
    return jax.shard_map(
        shards, mesh=split, in_specs=placed, out_specs=P(("groups", "ep"), tp), check_vma=False
    )
```

```python
import jax
import jax.numpy as jnp
from jax import lax
from jax.experimental import pallas as pl
from jax.experimental.pallas import tpu as pltpu
from jax.sharding import PartitionSpec as P

CAP = 8
PIECE = 32
FAR = ("ep", "chip", "core")
SWAP = [(0, 1), (1, 0)]
LIMIT = pltpu.CompilerParams(vmem_limit_bytes=16 * 1024 * 1024)


def iota(shape, dim):
    return lax.broadcasted_iota(jnp.int32, shape, dim)


def to_column(row):
    size = row.shape[1]
    square = (size, size)
    return jnp.sum(jnp.where(iota(square, 0) == iota(square, 1), row, 0.0), axis=1, keepdims=True)


def slot_codes(ids, resident):
    row_count = ids.shape[1]
    expert = jnp.min(ids, axis=0, keepdims=True)
    onehot_shape = (-(-resident // 16) * 16, row_count)
    onehot = jnp.where(expert == iota(onehot_shape, 0).astype(jnp.float32), 1.0, 0.0)
    square = (row_count, row_count)
    earlier = jnp.where(iota(square, 0) < iota(square, 1), 1.0, 0.0).astype(jnp.bfloat16)
    counts = jnp.dot(onehot.astype(jnp.bfloat16), earlier, preferred_element_type=jnp.float32)
    return expert * CAP + jnp.sum(counts * onehot, axis=0, keepdims=True), expert


def first_order(ep_count, chip):
    listed = ((2, 1, 0, 3), (3, 0, 2, 1))[chip % 2]
    return [z // 4 * 4 + listed[z % 4] for z in range(ep_count)]


def second_order(ep_count, chip):
    listed = ((2, 1, 0, 3), (3, 0, 2, 1))[chip % 2]
    return [z // 4 * 4 + listed[z % 4] for z in range(ep_count)]


def row_codes(index, order, ep_count, chips):
    listed = [z for chip in range(chips) for z in order(ep_count, chip)]
    expert = sum(jnp.where(index // CAP == at, z // 2, 0) for at, z in enumerate(listed))
    return (expert * CAP + lax.rem(index, CAP)).astype(jnp.float32)


def route(ep_count, chips, ids_hbm, tokens_hbm, outgoing_ref, ids_ref, tokens_ref, sems):
    row_count = ids_ref.shape[1]
    parts = row_count // PIECE
    copies = [pltpu.make_async_copy(ids_hbm, ids_ref, sems.at[parts])] + [
        pltpu.make_async_copy(
            tokens_hbm.at[pl.ds(part * PIECE, PIECE), :],
            tokens_ref.at[pl.ds(part * PIECE, PIECE), :],
            sems.at[part],
        )
        for part in range(parts)
    ]
    for copy in copies:
        copy.start()
    wanted = row_codes(iota((outgoing_ref.shape[0], row_count), 0), first_order, ep_count, chips)
    copies[0].wait()
    code, _ = slot_codes(ids_ref[...].astype(jnp.float32), ep_count // 2)
    dispatch = jnp.where(code == wanted, 1.0, 0.0).astype(jnp.bfloat16)
    for copy in copies[1:]:
        copy.wait()
    outgoing_ref[...] = jnp.dot(
        dispatch, tokens_ref[...], preferred_element_type=jnp.float32
    ).astype(jnp.bfloat16)


def score(ep_count, chips, ids_ref, scores_ref, _, match_ref, weight_ref):
    ids = ids_ref[...].astype(jnp.float32)
    code, expert = slot_codes(ids, ep_count // 2)
    wanted = row_codes(iota(match_ref.shape, 1), second_order, ep_count, chips)
    match_ref[...] = jnp.where(to_column(code) == wanted, 1.0, 0.0).astype(jnp.bfloat16)
    squashed = jax.nn.sigmoid(scores_ref[...])
    chosen = jnp.sum(jnp.where(ids == expert, squashed, 0.0), axis=0, keepdims=True)
    weight_ref[...] = to_column(2.5 * chosen / jnp.sum(squashed, axis=0, keepdims=True))


def far_groups(order, ep_count, chips):
    return [
        [(z * chips + x) * 2 + (side + x) % 2 for x in range(chips) for z in order(ep_count, x)]
        for side in range(2)
    ]


def columns_of(chip, own, features):
    core = lax.rem(lax.axis_index("core") + lax.axis_index("chip") + chip + (0 if own else 1), 2)
    return pl.ds(pl.multiple_of((2 * chip + core) * features, features), features)


def in_order(values, held, wanted):
    if held == wanted:
        return values
    blocks = [values[held.index(z) * CAP : (held.index(z) + 1) * CAP, :] for z in wanted]
    return jnp.concatenate(blocks, axis=0)


def lift(chips, own, rows_ref, gate_ref, up_ref):
    part_rows, features = rows_ref.shape[0] // chips, rows_ref.shape[1]
    ep_count = part_rows // CAP
    total = jnp.zeros((part_rows, 2 * gate_ref.shape[2]), jnp.float32)
    for chip in range(chips):
        rows = rows_ref[chip * part_rows : (chip + 1) * part_rows, :]
        columns = columns_of(chip, own, features)
        both = jnp.concatenate([gate_ref[0, columns, :], up_ref[0, columns, :]], axis=1)
        acts = jnp.dot(rows, both, preferred_element_type=jnp.float32)
        total += in_order(acts, first_order(ep_count, chip), first_order(ep_count, 0))
    return total


def lower(chips, own, hidden, down_ref, out_ref):
    part_rows, features = out_ref.shape[0] // chips, out_ref.shape[1]
    ep_count = part_rows // CAP
    for chip in range(chips):
        columns = columns_of(chip, own, features)
        values = jnp.dot(hidden, down_ref[0, :, columns], preferred_element_type=jnp.float32)
        values = in_order(values, first_order(ep_count, 0), second_order(ep_count, chip))
        out_ref[chip * part_rows : (chip + 1) * part_rows, :] = values.astype(jnp.bfloat16)


def begin(chips, rows_ref, gate_ref, up_ref, acts_ref):
    acts_ref[...] = lift(chips, True, rows_ref, gate_ref, up_ref)


def theirs(chips, rows_ref, acts_ref, gate_ref, up_ref, down_ref, hidden_ref, other_ref):
    width = gate_ref.shape[2]
    acts = acts_ref[...] + lift(chips, False, rows_ref, gate_ref, up_ref)
    gate_act, up_act = acts[:, :width], acts[:, width:]
    hidden = (gate_act / (1.0 + jnp.exp(-gate_act)) * up_act).astype(jnp.bfloat16)
    hidden_ref[...] = hidden
    lower(chips, False, hidden, down_ref, other_ref)


def ours(chips, hidden_ref, down_ref, mine_ref):
    lower(chips, True, hidden_ref[...], down_ref, mine_ref)


def add(mine_ref, other_ref, _, out_ref):
    total = mine_ref[...].astype(jnp.float32) + other_ref[...].astype(jnp.float32)
    out_ref[...] = total.astype(jnp.bfloat16)


def combine(match_ref, weight_ref, returned_ref, out_hbm, out_ref, sems):
    copies = []
    for part in range(out_ref.shape[0] // PIECE):
        rows = pl.ds(part * PIECE, PIECE)
        summed = jnp.dot(match_ref[rows, :], returned_ref[...], preferred_element_type=jnp.float32)
        out_ref[rows, :] = (weight_ref[rows, :] * summed).astype(jnp.bfloat16)
        copies.append(pltpu.make_async_copy(out_ref.at[rows, :], out_hbm.at[rows, :], sems.at[part]))
        copies[-1].start()
    for copy in copies:
        copy.wait()


def shards(tokens, expert_ids, route_scores, w_gate, w_up, w_down):
    row_count, features = tokens.shape
    top_count, hidden_count = expert_ids.shape[1], w_gate.shape[2]
    ep_count, chips = lax.axis_size("ep"), lax.axis_size("chip")
    slot_count = ep_count * CAP
    half = jax.ShapeDtypeStruct((chips * slot_count, features), jnp.bfloat16)
    ids, scores = expert_ids.T, route_scores.T
    hbm, vmem = (pl.BlockSpec(memory_space=space) for space in (pltpu.HBM, pltpu.VMEM))
    anywhere = pl.BlockSpec(memory_space=pl.ANY)

    def exchange(rows, order):
        groups = far_groups(order, ep_count, chips)
        return lax.all_to_all(rows, FAR, 0, 0, axis_index_groups=groups, tiled=True)

    def call(kernel, name, out_shape, **rest):
        return pl.pallas_call(kernel, out_shape=out_shape, name=name, compiler_params=LIMIT, **rest)

    outgoing = call(
        lambda *refs: route(ep_count, chips, *refs),
        "route",
        half,
        in_specs=[hbm] * 2,
        scratch_shapes=[
            pltpu.VMEM((top_count, row_count), jnp.int32),
            pltpu.VMEM((row_count, features), jnp.bfloat16),
            pltpu.SemaphoreType.DMA((row_count // PIECE + 1,)),
        ],
        cost_estimate=pl.CostEstimate(flops=2 * 10**9, bytes_accessed=0, transcendentals=0),
    )(*(pltpu.with_memory_space_constraint(value, pltpu.HBM) for value in (ids, tokens)))
    incoming = exchange(outgoing, first_order)
    across = lax.ppermute(incoming, "core", SWAP)
    acts = jax.ShapeDtypeStruct((slot_count, 2 * hidden_count), jnp.float32)
    begun = call(lambda *refs: begin(chips, *refs), "begin", acts)(incoming, w_gate, w_up)
    hidden_shape = jax.ShapeDtypeStruct((slot_count, hidden_count), jnp.bfloat16)
    hidden, other = call(lambda *refs: theirs(chips, *refs), "theirs", (hidden_shape, half))(
        across, begun, w_gate, w_up, w_down
    )
    crossed = lax.ppermute(other, "core", SWAP)
    mine = call(lambda *refs: ours(chips, *refs), "ours", half)(hidden, w_down)
    match, weight = call(
        lambda *refs: score(ep_count, chips, *refs),
        "score",
        (
            jax.ShapeDtypeStruct((row_count, chips * slot_count), jnp.bfloat16),
            jax.ShapeDtypeStruct((row_count, 1), jnp.float32),
        ),
        in_specs=[vmem] * 2 + [anywhere],
    )(ids, scores, other)
    summed = call(add, "add", half, in_specs=[vmem] * 2 + [anywhere])(mine, crossed, weight)
    returned = exchange(summed, second_order)
    return call(
        combine,
        "combine",
        jax.ShapeDtypeStruct((row_count, features), jnp.bfloat16),
        out_specs=hbm,
        scratch_shapes=[
            pltpu.VMEM((row_count, features), jnp.bfloat16),
            pltpu.SemaphoreType.DMA((row_count // PIECE,)),
        ],
    )(match, weight, returned)


def solution(mesh):
    groups, ep_count, tp_count = (mesh.shape[name] for name in ("groups", "ep", "tp"))
    split = jax.sharding.Mesh(
        mesh.devices.reshape(groups, ep_count, tp_count // 2, 2), ("groups", "ep", "chip", "core")
    )
    tp = ("chip", "core")
    placed = (
        P(("groups", "ep"), tp),
        P(("groups", "ep"), None),
        P(("groups", "ep"), None),
        P("ep", None, tp),
        P("ep", None, tp),
        P("ep", tp, None),
    )
    return jax.shard_map(
        shards, mesh=split, in_specs=placed, out_specs=P(("groups", "ep"), tp), check_vma=False
    )
```

```python
import jax
import jax.numpy as jnp
from jax import lax
from jax.experimental import pallas as pl
from jax.experimental.pallas import tpu as pltpu
from jax.sharding import PartitionSpec as P

CAP = 8
PIECE = 32
FAR = ("ep", "chip", "core")
SWAP = [(0, 1), (1, 0)]
LIMIT = pltpu.CompilerParams(vmem_limit_bytes=16 * 1024 * 1024)


def iota(shape, dim):
    return lax.broadcasted_iota(jnp.int32, shape, dim)


def to_column(row):
    size = row.shape[1]
    square = (size, size)
    return jnp.sum(jnp.where(iota(square, 0) == iota(square, 1), row, 0.0), axis=1, keepdims=True)


def slot_codes(ids, resident):
    row_count = ids.shape[1]
    expert = jnp.min(ids, axis=0, keepdims=True)
    onehot_shape = (-(-resident // 16) * 16, row_count)
    onehot = jnp.where(expert == iota(onehot_shape, 0).astype(jnp.float32), 1.0, 0.0)
    square = (row_count, row_count)
    earlier = jnp.where(iota(square, 0) < iota(square, 1), 1.0, 0.0).astype(jnp.bfloat16)
    counts = jnp.dot(onehot.astype(jnp.bfloat16), earlier, preferred_element_type=jnp.float32)
    return expert * CAP + jnp.sum(counts * onehot, axis=0, keepdims=True), expert


def first_order(ep_count, chip):
    listed = ((2, 3, 0, 1), (3, 2, 1, 0))[chip % 2]
    return [z // 4 * 4 + listed[z % 4] for z in range(ep_count)]


def second_order(ep_count, chip):
    listed = ((2, 1, 0, 3), (3, 2, 0, 1))[chip % 2]
    return [z // 4 * 4 + listed[z % 4] for z in range(ep_count)]


def row_codes(index, order, ep_count, chips):
    listed = [z for chip in range(chips) for z in order(ep_count, chip)]
    expert = sum(jnp.where(index // CAP == at, z // 2, 0) for at, z in enumerate(listed))
    return (expert * CAP + lax.rem(index, CAP)).astype(jnp.float32)


def route(ep_count, chips, ids_hbm, tokens_hbm, outgoing_ref, ids_ref, tokens_ref, sems):
    row_count = ids_ref.shape[1]
    parts = row_count // PIECE
    copies = [pltpu.make_async_copy(ids_hbm, ids_ref, sems.at[parts])] + [
        pltpu.make_async_copy(
            tokens_hbm.at[pl.ds(part * PIECE, PIECE), :],
            tokens_ref.at[pl.ds(part * PIECE, PIECE), :],
            sems.at[part],
        )
        for part in range(parts)
    ]
    for copy in copies:
        copy.start()
    wanted = row_codes(iota((outgoing_ref.shape[0], row_count), 0), first_order, ep_count, chips)
    copies[0].wait()
    code, _ = slot_codes(ids_ref[...].astype(jnp.float32), ep_count // 2)
    dispatch = jnp.where(code == wanted, 1.0, 0.0).astype(jnp.bfloat16)
    for copy in copies[1:]:
        copy.wait()
    outgoing_ref[...] = jnp.dot(
        dispatch, tokens_ref[...], preferred_element_type=jnp.float32
    ).astype(jnp.bfloat16)


def score(ep_count, chips, ids_ref, scores_ref, _, match_ref, weight_ref):
    ids = ids_ref[...].astype(jnp.float32)
    code, expert = slot_codes(ids, ep_count // 2)
    wanted = row_codes(iota(match_ref.shape, 1), second_order, ep_count, chips)
    match_ref[...] = jnp.where(to_column(code) == wanted, 1.0, 0.0).astype(jnp.bfloat16)
    squashed = jax.nn.sigmoid(scores_ref[...])
    chosen = jnp.sum(jnp.where(ids == expert, squashed, 0.0), axis=0, keepdims=True)
    weight_ref[...] = to_column(2.5 * chosen / jnp.sum(squashed, axis=0, keepdims=True))


def far_groups(order, ep_count, chips):
    return [
        [(z * chips + x) * 2 + (side + x) % 2 for x in range(chips) for z in order(ep_count, x)]
        for side in range(2)
    ]


def columns_of(chip, own, features):
    core = lax.rem(lax.axis_index("core") + lax.axis_index("chip") + chip + (0 if own else 1), 2)
    return pl.ds(pl.multiple_of((2 * chip + core) * features, features), features)


def in_order(values, held, wanted):
    if held == wanted:
        return values
    blocks = [values[held.index(z) * CAP : (held.index(z) + 1) * CAP, :] for z in wanted]
    return jnp.concatenate(blocks, axis=0)


def lift(chips, own, rows_ref, gate_ref, up_ref):
    part_rows, features = rows_ref.shape[0] // chips, rows_ref.shape[1]
    ep_count = part_rows // CAP
    total = jnp.zeros((part_rows, 2 * gate_ref.shape[2]), jnp.float32)
    for chip in range(chips):
        rows = rows_ref[chip * part_rows : (chip + 1) * part_rows, :]
        columns = columns_of(chip, own, features)
        both = jnp.concatenate([gate_ref[0, columns, :], up_ref[0, columns, :]], axis=1)
        acts = jnp.dot(rows, both, preferred_element_type=jnp.float32)
        total += in_order(acts, first_order(ep_count, chip), first_order(ep_count, 0))
    return total


def lower(chips, own, hidden, down_ref, out_ref):
    part_rows, features = out_ref.shape[0] // chips, out_ref.shape[1]
    ep_count = part_rows // CAP
    for chip in range(chips):
        columns = columns_of(chip, own, features)
        values = jnp.dot(hidden, down_ref[0, :, columns], preferred_element_type=jnp.float32)
        values = in_order(values, first_order(ep_count, 0), second_order(ep_count, chip))
        out_ref[chip * part_rows : (chip + 1) * part_rows, :] = values.astype(jnp.bfloat16)


def begin(chips, rows_ref, gate_ref, up_ref, acts_ref):
    acts_ref[...] = lift(chips, True, rows_ref, gate_ref, up_ref)


def theirs(chips, rows_ref, acts_ref, gate_ref, up_ref, down_ref, hidden_ref, other_ref):
    width = gate_ref.shape[2]
    acts = acts_ref[...] + lift(chips, False, rows_ref, gate_ref, up_ref)
    gate_act, up_act = acts[:, :width], acts[:, width:]
    hidden = (gate_act / (1.0 + jnp.exp(-gate_act)) * up_act).astype(jnp.bfloat16)
    hidden_ref[...] = hidden
    lower(chips, False, hidden, down_ref, other_ref)


def ours(chips, hidden_ref, down_ref, mine_ref):
    lower(chips, True, hidden_ref[...], down_ref, mine_ref)


def add(mine_ref, other_ref, _, out_ref):
    total = mine_ref[...].astype(jnp.float32) + other_ref[...].astype(jnp.float32)
    out_ref[...] = total.astype(jnp.bfloat16)


def combine(match_ref, weight_ref, returned_ref, out_hbm, out_ref, sems):
    copies = []
    for part in range(out_ref.shape[0] // PIECE):
        rows = pl.ds(part * PIECE, PIECE)
        summed = jnp.dot(match_ref[rows, :], returned_ref[...], preferred_element_type=jnp.float32)
        out_ref[rows, :] = (weight_ref[rows, :] * summed).astype(jnp.bfloat16)
        copies.append(pltpu.make_async_copy(out_ref.at[rows, :], out_hbm.at[rows, :], sems.at[part]))
        copies[-1].start()
    for copy in copies:
        copy.wait()


def shards(tokens, expert_ids, route_scores, w_gate, w_up, w_down):
    row_count, features = tokens.shape
    top_count, hidden_count = expert_ids.shape[1], w_gate.shape[2]
    ep_count, chips = lax.axis_size("ep"), lax.axis_size("chip")
    slot_count = ep_count * CAP
    half = jax.ShapeDtypeStruct((chips * slot_count, features), jnp.bfloat16)
    ids, scores = expert_ids.T, route_scores.T
    hbm, vmem = (pl.BlockSpec(memory_space=space) for space in (pltpu.HBM, pltpu.VMEM))
    anywhere = pl.BlockSpec(memory_space=pl.ANY)

    def exchange(rows, order):
        groups = far_groups(order, ep_count, chips)
        return lax.all_to_all(rows, FAR, 0, 0, axis_index_groups=groups, tiled=True)

    def call(kernel, name, out_shape, **rest):
        return pl.pallas_call(kernel, out_shape=out_shape, name=name, compiler_params=LIMIT, **rest)

    outgoing = call(
        lambda *refs: route(ep_count, chips, *refs),
        "route",
        half,
        in_specs=[hbm] * 2,
        scratch_shapes=[
            pltpu.VMEM((top_count, row_count), jnp.int32),
            pltpu.VMEM((row_count, features), jnp.bfloat16),
            pltpu.SemaphoreType.DMA((row_count // PIECE + 1,)),
        ],
        cost_estimate=pl.CostEstimate(flops=2 * 10**9, bytes_accessed=0, transcendentals=0),
    )(*(pltpu.with_memory_space_constraint(value, pltpu.HBM) for value in (ids, tokens)))
    incoming = exchange(outgoing, first_order)
    across = lax.ppermute(incoming, "core", SWAP)
    acts = jax.ShapeDtypeStruct((slot_count, 2 * hidden_count), jnp.float32)
    begun = call(lambda *refs: begin(chips, *refs), "begin", acts)(incoming, w_gate, w_up)
    hidden_shape = jax.ShapeDtypeStruct((slot_count, hidden_count), jnp.bfloat16)
    hidden, other = call(lambda *refs: theirs(chips, *refs), "theirs", (hidden_shape, half))(
        across, begun, w_gate, w_up, w_down
    )
    crossed = lax.ppermute(other, "core", SWAP)
    mine = call(lambda *refs: ours(chips, *refs), "ours", half)(hidden, w_down)
    match, weight = call(
        lambda *refs: score(ep_count, chips, *refs),
        "score",
        (
            jax.ShapeDtypeStruct((row_count, chips * slot_count), jnp.bfloat16),
            jax.ShapeDtypeStruct((row_count, 1), jnp.float32),
        ),
        in_specs=[vmem] * 2 + [anywhere],
    )(ids, scores, other)
    summed = call(add, "add", half, in_specs=[vmem] * 2 + [anywhere])(mine, crossed, weight)
    returned = exchange(summed, second_order)
    return call(
        combine,
        "combine",
        jax.ShapeDtypeStruct((row_count, features), jnp.bfloat16),
        out_specs=hbm,
        scratch_shapes=[
            pltpu.VMEM((row_count, features), jnp.bfloat16),
            pltpu.SemaphoreType.DMA((row_count // PIECE,)),
        ],
    )(match, weight, returned)


def solution(mesh):
    groups, ep_count, tp_count = (mesh.shape[name] for name in ("groups", "ep", "tp"))
    split = jax.sharding.Mesh(
        mesh.devices.reshape(groups, ep_count, tp_count // 2, 2), ("groups", "ep", "chip", "core")
    )
    tp = ("chip", "core")
    placed = (
        P(("groups", "ep"), tp),
        P(("groups", "ep"), None),
        P(("groups", "ep"), None),
        P("ep", None, tp),
        P("ep", None, tp),
        P("ep", tp, None),
    )
    return jax.shard_map(
        shards, mesh=split, in_specs=placed, out_specs=P(("groups", "ep"), tp), check_vma=False
    )
```

```python
import jax
import jax.numpy as jnp
from jax import lax
from jax.experimental import pallas as pl
from jax.experimental.pallas import tpu as pltpu
from jax.sharding import PartitionSpec as P

CAP = 8
PIECE = 32
FAR = ("ep", "chip", "core")
SWAP = [(0, 1), (1, 0)]
LIMIT = pltpu.CompilerParams(vmem_limit_bytes=16 * 1024 * 1024)


def iota(shape, dim):
    return lax.broadcasted_iota(jnp.int32, shape, dim)


def to_column(row):
    size = row.shape[1]
    square = (size, size)
    return jnp.sum(jnp.where(iota(square, 0) == iota(square, 1), row, 0.0), axis=1, keepdims=True)


def slot_codes(ids, resident):
    row_count = ids.shape[1]
    expert = jnp.min(ids, axis=0, keepdims=True)
    onehot_shape = (-(-resident // 16) * 16, row_count)
    onehot = jnp.where(expert == iota(onehot_shape, 0).astype(jnp.float32), 1.0, 0.0)
    square = (row_count, row_count)
    earlier = jnp.where(iota(square, 0) < iota(square, 1), 1.0, 0.0).astype(jnp.bfloat16)
    counts = jnp.dot(onehot.astype(jnp.bfloat16), earlier, preferred_element_type=jnp.float32)
    return expert * CAP + jnp.sum(counts * onehot, axis=0, keepdims=True), expert


def first_order(ep_count, chip):
    listed = ((2, 3, 0, 1), (3, 1, 2, 0))[chip % 2]
    return [z // 4 * 4 + listed[z % 4] for z in range(ep_count)]


def second_order(ep_count, chip):
    listed = ((2, 1, 0, 3), (3, 2, 0, 1))[chip % 2]
    return [z // 4 * 4 + listed[z % 4] for z in range(ep_count)]


def row_codes(index, order, ep_count, chips):
    listed = [z for chip in range(chips) for z in order(ep_count, chip)]
    expert = sum(jnp.where(index // CAP == at, z // 2, 0) for at, z in enumerate(listed))
    return (expert * CAP + lax.rem(index, CAP)).astype(jnp.float32)


def route(ep_count, chips, ids_hbm, tokens_hbm, outgoing_ref, ids_ref, tokens_ref, sems):
    row_count = ids_ref.shape[1]
    parts = row_count // PIECE
    copies = [pltpu.make_async_copy(ids_hbm, ids_ref, sems.at[parts])] + [
        pltpu.make_async_copy(
            tokens_hbm.at[pl.ds(part * PIECE, PIECE), :],
            tokens_ref.at[pl.ds(part * PIECE, PIECE), :],
            sems.at[part],
        )
        for part in range(parts)
    ]
    for copy in copies:
        copy.start()
    wanted = row_codes(iota((outgoing_ref.shape[0], row_count), 0), first_order, ep_count, chips)
    copies[0].wait()
    code, _ = slot_codes(ids_ref[...].astype(jnp.float32), ep_count // 2)
    dispatch = jnp.where(code == wanted, 1.0, 0.0).astype(jnp.bfloat16)
    for copy in copies[1:]:
        copy.wait()
    outgoing_ref[...] = jnp.dot(
        dispatch, tokens_ref[...], preferred_element_type=jnp.float32
    ).astype(jnp.bfloat16)


def score(ep_count, chips, ids_ref, scores_ref, _, match_ref, weight_ref):
    ids = ids_ref[...].astype(jnp.float32)
    code, expert = slot_codes(ids, ep_count // 2)
    wanted = row_codes(iota(match_ref.shape, 1), second_order, ep_count, chips)
    match_ref[...] = jnp.where(to_column(code) == wanted, 1.0, 0.0).astype(jnp.bfloat16)
    squashed = jax.nn.sigmoid(scores_ref[...])
    chosen = jnp.sum(jnp.where(ids == expert, squashed, 0.0), axis=0, keepdims=True)
    weight_ref[...] = to_column(2.5 * chosen / jnp.sum(squashed, axis=0, keepdims=True))


def far_groups(order, ep_count, chips):
    return [
        [(z * chips + x) * 2 + (side + x) % 2 for x in range(chips) for z in order(ep_count, x)]
        for side in range(2)
    ]


def columns_of(chip, own, features):
    core = lax.rem(lax.axis_index("core") + lax.axis_index("chip") + chip + (0 if own else 1), 2)
    return pl.ds(pl.multiple_of((2 * chip + core) * features, features), features)


def in_order(values, held, wanted):
    if held == wanted:
        return values
    blocks = [values[held.index(z) * CAP : (held.index(z) + 1) * CAP, :] for z in wanted]
    return jnp.concatenate(blocks, axis=0)


def lift(chips, own, rows_ref, gate_ref, up_ref):
    part_rows, features = rows_ref.shape[0] // chips, rows_ref.shape[1]
    ep_count = part_rows // CAP
    total = jnp.zeros((part_rows, 2 * gate_ref.shape[2]), jnp.float32)
    for chip in range(chips):
        rows = rows_ref[chip * part_rows : (chip + 1) * part_rows, :]
        columns = columns_of(chip, own, features)
        both = jnp.concatenate([gate_ref[0, columns, :], up_ref[0, columns, :]], axis=1)
        acts = jnp.dot(rows, both, preferred_element_type=jnp.float32)
        total += in_order(acts, first_order(ep_count, chip), first_order(ep_count, 0))
    return total


def lower(chips, own, hidden, down_ref, out_ref):
    part_rows, features = out_ref.shape[0] // chips, out_ref.shape[1]
    ep_count = part_rows // CAP
    for chip in range(chips):
        columns = columns_of(chip, own, features)
        values = jnp.dot(hidden, down_ref[0, :, columns], preferred_element_type=jnp.float32)
        values = in_order(values, first_order(ep_count, 0), second_order(ep_count, chip))
        out_ref[chip * part_rows : (chip + 1) * part_rows, :] = values.astype(jnp.bfloat16)


def begin(chips, rows_ref, gate_ref, up_ref, acts_ref):
    acts_ref[...] = lift(chips, True, rows_ref, gate_ref, up_ref)


def theirs(chips, rows_ref, acts_ref, gate_ref, up_ref, down_ref, hidden_ref, other_ref):
    width = gate_ref.shape[2]
    acts = acts_ref[...] + lift(chips, False, rows_ref, gate_ref, up_ref)
    gate_act, up_act = acts[:, :width], acts[:, width:]
    hidden = (gate_act / (1.0 + jnp.exp(-gate_act)) * up_act).astype(jnp.bfloat16)
    hidden_ref[...] = hidden
    lower(chips, False, hidden, down_ref, other_ref)


def ours(chips, hidden_ref, down_ref, mine_ref):
    lower(chips, True, hidden_ref[...], down_ref, mine_ref)


def add(mine_ref, other_ref, _, out_ref):
    total = mine_ref[...].astype(jnp.float32) + other_ref[...].astype(jnp.float32)
    out_ref[...] = total.astype(jnp.bfloat16)


def combine(match_ref, weight_ref, returned_ref, out_hbm, out_ref, sems):
    copies = []
    for part in range(out_ref.shape[0] // PIECE):
        rows = pl.ds(part * PIECE, PIECE)
        summed = jnp.dot(match_ref[rows, :], returned_ref[...], preferred_element_type=jnp.float32)
        out_ref[rows, :] = (weight_ref[rows, :] * summed).astype(jnp.bfloat16)
        copies.append(pltpu.make_async_copy(out_ref.at[rows, :], out_hbm.at[rows, :], sems.at[part]))
        copies[-1].start()
    for copy in copies:
        copy.wait()


def shards(tokens, expert_ids, route_scores, w_gate, w_up, w_down):
    row_count, features = tokens.shape
    top_count, hidden_count = expert_ids.shape[1], w_gate.shape[2]
    ep_count, chips = lax.axis_size("ep"), lax.axis_size("chip")
    slot_count = ep_count * CAP
    half = jax.ShapeDtypeStruct((chips * slot_count, features), jnp.bfloat16)
    ids, scores = expert_ids.T, route_scores.T
    hbm, vmem = (pl.BlockSpec(memory_space=space) for space in (pltpu.HBM, pltpu.VMEM))
    anywhere = pl.BlockSpec(memory_space=pl.ANY)

    def exchange(rows, order):
        groups = far_groups(order, ep_count, chips)
        return lax.all_to_all(rows, FAR, 0, 0, axis_index_groups=groups, tiled=True)

    def call(kernel, name, out_shape, **rest):
        return pl.pallas_call(kernel, out_shape=out_shape, name=name, compiler_params=LIMIT, **rest)

    outgoing = call(
        lambda *refs: route(ep_count, chips, *refs),
        "route",
        half,
        in_specs=[hbm] * 2,
        scratch_shapes=[
            pltpu.VMEM((top_count, row_count), jnp.int32),
            pltpu.VMEM((row_count, features), jnp.bfloat16),
            pltpu.SemaphoreType.DMA((row_count // PIECE + 1,)),
        ],
        cost_estimate=pl.CostEstimate(flops=2 * 10**9, bytes_accessed=0, transcendentals=0),
    )(*(pltpu.with_memory_space_constraint(value, pltpu.HBM) for value in (ids, tokens)))
    incoming = exchange(outgoing, first_order)
    across = lax.ppermute(incoming, "core", SWAP)
    acts = jax.ShapeDtypeStruct((slot_count, 2 * hidden_count), jnp.float32)
    begun = call(lambda *refs: begin(chips, *refs), "begin", acts)(incoming, w_gate, w_up)
    hidden_shape = jax.ShapeDtypeStruct((slot_count, hidden_count), jnp.bfloat16)
    hidden, other = call(lambda *refs: theirs(chips, *refs), "theirs", (hidden_shape, half))(
        across, begun, w_gate, w_up, w_down
    )
    crossed = lax.ppermute(other, "core", SWAP)
    mine = call(lambda *refs: ours(chips, *refs), "ours", half)(hidden, w_down)
    match, weight = call(
        lambda *refs: score(ep_count, chips, *refs),
        "score",
        (
            jax.ShapeDtypeStruct((row_count, chips * slot_count), jnp.bfloat16),
            jax.ShapeDtypeStruct((row_count, 1), jnp.float32),
        ),
        in_specs=[vmem] * 2 + [anywhere],
    )(ids, scores, other)
    summed = call(add, "add", half, in_specs=[vmem] * 2 + [anywhere])(mine, crossed, weight)
    returned = exchange(summed, second_order)
    return call(
        combine,
        "combine",
        jax.ShapeDtypeStruct((row_count, features), jnp.bfloat16),
        out_specs=hbm,
        scratch_shapes=[
            pltpu.VMEM((row_count, features), jnp.bfloat16),
            pltpu.SemaphoreType.DMA((row_count // PIECE,)),
        ],
    )(match, weight, returned)


def solution(mesh):
    groups, ep_count, tp_count = (mesh.shape[name] for name in ("groups", "ep", "tp"))
    split = jax.sharding.Mesh(
        mesh.devices.reshape(groups, ep_count, tp_count // 2, 2), ("groups", "ep", "chip", "core")
    )
    tp = ("chip", "core")
    placed = (
        P(("groups", "ep"), tp),
        P(("groups", "ep"), None),
        P(("groups", "ep"), None),
        P("ep", None, tp),
        P("ep", None, tp),
        P("ep", tp, None),
    )
    return jax.shard_map(
        shards, mesh=split, in_specs=placed, out_specs=P(("groups", "ep"), tp), check_vma=False
    )
```

```python
import jax
import jax.numpy as jnp
from jax import lax
from jax.experimental import pallas as pl
from jax.experimental.pallas import tpu as pltpu
from jax.sharding import PartitionSpec as P

CAP = 8
PIECE = 32
FETCH = 16
FAR = ("ep", "chip", "core")
SWAP = [(0, 1), (1, 0)]
LIMIT = pltpu.CompilerParams(vmem_limit_bytes=16 * 1024 * 1024)


def iota(shape, dim):
    return lax.broadcasted_iota(jnp.int32, shape, dim)


def to_column(row):
    size = row.shape[1]
    square = (size, size)
    return jnp.sum(jnp.where(iota(square, 0) == iota(square, 1), row, 0.0), axis=1, keepdims=True)


def slot_codes(ids, resident):
    row_count = ids.shape[1]
    expert = jnp.min(ids, axis=0, keepdims=True)
    onehot_shape = (-(-resident // 16) * 16, row_count)
    onehot = jnp.where(expert == iota(onehot_shape, 0).astype(jnp.float32), 1.0, 0.0)
    square = (row_count, row_count)
    earlier = jnp.where(iota(square, 0) < iota(square, 1), 1.0, 0.0).astype(jnp.bfloat16)
    counts = jnp.dot(onehot.astype(jnp.bfloat16), earlier, preferred_element_type=jnp.float32)
    return expert * CAP + jnp.sum(counts * onehot, axis=0, keepdims=True), expert


def first_order(ep_count, chip):
    listed = ((2, 3, 0, 1), (3, 2, 1, 0))[chip % 2]
    return [z // 4 * 4 + listed[z % 4] for z in range(ep_count)]


def second_order(ep_count, chip):
    listed = ((2, 1, 0, 3), (3, 2, 0, 1))[chip % 2]
    return [z // 4 * 4 + listed[z % 4] for z in range(ep_count)]


def row_codes(index, order, ep_count, chips):
    listed = [z for chip in range(chips) for z in order(ep_count, chip)]
    expert = sum(jnp.where(index // CAP == at, z // 2, 0) for at, z in enumerate(listed))
    return (expert * CAP + lax.rem(index, CAP)).astype(jnp.float32)


def route(ep_count, chips, ids_hbm, tokens_hbm, outgoing_ref, ids_ref, tokens_ref, sems):
    row_count = ids_ref.shape[1]
    parts = row_count // FETCH
    copies = [pltpu.make_async_copy(ids_hbm, ids_ref, sems.at[parts])] + [
        pltpu.make_async_copy(
            tokens_hbm.at[pl.ds(part * FETCH, FETCH), :],
            tokens_ref.at[pl.ds(part * FETCH, FETCH), :],
            sems.at[part],
        )
        for part in range(parts)
    ]
    for copy in copies:
        copy.start()
    wanted = row_codes(iota((outgoing_ref.shape[0], row_count), 0), first_order, ep_count, chips)
    copies[0].wait()
    code, _ = slot_codes(ids_ref[...].astype(jnp.float32), ep_count // 2)
    dispatch = jnp.where(code == wanted, 1.0, 0.0).astype(jnp.bfloat16)
    for copy in copies[1:]:
        copy.wait()
    outgoing_ref[...] = jnp.dot(
        dispatch, tokens_ref[...], preferred_element_type=jnp.float32
    ).astype(jnp.bfloat16)


def score(ep_count, chips, ids_ref, scores_ref, _, match_ref, weight_ref):
    ids = ids_ref[...].astype(jnp.float32)
    code, expert = slot_codes(ids, ep_count // 2)
    wanted = row_codes(iota(match_ref.shape, 1), second_order, ep_count, chips)
    match_ref[...] = jnp.where(to_column(code) == wanted, 1.0, 0.0).astype(jnp.bfloat16)
    squashed = jax.nn.sigmoid(scores_ref[...])
    chosen = jnp.sum(jnp.where(ids == expert, squashed, 0.0), axis=0, keepdims=True)
    weight_ref[...] = to_column(2.5 * chosen / jnp.sum(squashed, axis=0, keepdims=True))


def far_groups(order, ep_count, chips):
    return [
        [(z * chips + x) * 2 + (side + x) % 2 for x in range(chips) for z in order(ep_count, x)]
        for side in range(2)
    ]


def columns_of(chip, own, features):
    core = lax.rem(lax.axis_index("core") + lax.axis_index("chip") + chip + (0 if own else 1), 2)
    return pl.ds(pl.multiple_of((2 * chip + core) * features, features), features)


def in_order(values, held, wanted):
    if held == wanted:
        return values
    blocks = [values[held.index(z) * CAP : (held.index(z) + 1) * CAP, :] for z in wanted]
    return jnp.concatenate(blocks, axis=0)


def lift(chips, own, rows_ref, gate_ref, up_ref):
    part_rows, features = rows_ref.shape[0] // chips, rows_ref.shape[1]
    ep_count = part_rows // CAP
    total = jnp.zeros((part_rows, 2 * gate_ref.shape[2]), jnp.float32)
    for chip in range(chips):
        rows = rows_ref[chip * part_rows : (chip + 1) * part_rows, :]
        columns = columns_of(chip, own, features)
        both = jnp.concatenate([gate_ref[0, columns, :], up_ref[0, columns, :]], axis=1)
        acts = jnp.dot(rows, both, preferred_element_type=jnp.float32)
        total += in_order(acts, first_order(ep_count, chip), first_order(ep_count, 0))
    return total


def lower(chips, own, hidden, down_ref, out_ref):
    part_rows, features = out_ref.shape[0] // chips, out_ref.shape[1]
    ep_count = part_rows // CAP
    for chip in range(chips):
        columns = columns_of(chip, own, features)
        values = jnp.dot(hidden, down_ref[0, :, columns], preferred_element_type=jnp.float32)
        values = in_order(values, first_order(ep_count, 0), second_order(ep_count, chip))
        out_ref[chip * part_rows : (chip + 1) * part_rows, :] = values.astype(jnp.bfloat16)


def begin(chips, rows_ref, gate_ref, up_ref, acts_ref):
    acts_ref[...] = lift(chips, True, rows_ref, gate_ref, up_ref)


def theirs(chips, rows_ref, acts_ref, gate_ref, up_ref, down_ref, hidden_ref, other_ref):
    width = gate_ref.shape[2]
    acts = acts_ref[...] + lift(chips, False, rows_ref, gate_ref, up_ref)
    gate_act, up_act = acts[:, :width], acts[:, width:]
    hidden = (gate_act / (1.0 + jnp.exp(-gate_act)) * up_act).astype(jnp.bfloat16)
    hidden_ref[...] = hidden
    lower(chips, False, hidden, down_ref, other_ref)


def ours(chips, hidden_ref, down_ref, mine_ref):
    lower(chips, True, hidden_ref[...], down_ref, mine_ref)


def add(mine_ref, other_ref, _, out_ref):
    total = mine_ref[...].astype(jnp.float32) + other_ref[...].astype(jnp.float32)
    out_ref[...] = total.astype(jnp.bfloat16)


def combine(match_ref, weight_ref, returned_ref, out_hbm, out_ref, sems):
    copies = []
    for part in range(out_ref.shape[0] // PIECE):
        rows = pl.ds(part * PIECE, PIECE)
        summed = jnp.dot(match_ref[rows, :], returned_ref[...], preferred_element_type=jnp.float32)
        out_ref[rows, :] = (weight_ref[rows, :] * summed).astype(jnp.bfloat16)
        copies.append(pltpu.make_async_copy(out_ref.at[rows, :], out_hbm.at[rows, :], sems.at[part]))
        copies[-1].start()
    for copy in copies:
        copy.wait()


def shards(tokens, expert_ids, route_scores, w_gate, w_up, w_down):
    row_count, features = tokens.shape
    top_count, hidden_count = expert_ids.shape[1], w_gate.shape[2]
    ep_count, chips = lax.axis_size("ep"), lax.axis_size("chip")
    slot_count = ep_count * CAP
    half = jax.ShapeDtypeStruct((chips * slot_count, features), jnp.bfloat16)
    ids, scores = expert_ids.T, route_scores.T
    hbm, vmem = (pl.BlockSpec(memory_space=space) for space in (pltpu.HBM, pltpu.VMEM))
    anywhere = pl.BlockSpec(memory_space=pl.ANY)

    def exchange(rows, order):
        groups = far_groups(order, ep_count, chips)
        return lax.all_to_all(rows, FAR, 0, 0, axis_index_groups=groups, tiled=True)

    def call(kernel, name, out_shape, **rest):
        return pl.pallas_call(kernel, out_shape=out_shape, name=name, compiler_params=LIMIT, **rest)

    outgoing = call(
        lambda *refs: route(ep_count, chips, *refs),
        "route",
        half,
        in_specs=[hbm] * 2,
        scratch_shapes=[
            pltpu.VMEM((top_count, row_count), jnp.int32),
            pltpu.VMEM((row_count, features), jnp.bfloat16),
            pltpu.SemaphoreType.DMA((row_count // FETCH + 1,)),
        ],
        cost_estimate=pl.CostEstimate(flops=2 * 10**9, bytes_accessed=0, transcendentals=0),
    )(*(pltpu.with_memory_space_constraint(value, pltpu.HBM) for value in (ids, tokens)))
    incoming = exchange(outgoing, first_order)
    across = lax.ppermute(incoming, "core", SWAP)
    acts = jax.ShapeDtypeStruct((slot_count, 2 * hidden_count), jnp.float32)
    begun = call(lambda *refs: begin(chips, *refs), "begin", acts)(incoming, w_gate, w_up)
    hidden_shape = jax.ShapeDtypeStruct((slot_count, hidden_count), jnp.bfloat16)
    hidden, other = call(lambda *refs: theirs(chips, *refs), "theirs", (hidden_shape, half))(
        across, begun, w_gate, w_up, w_down
    )
    crossed = lax.ppermute(other, "core", SWAP)
    mine = call(lambda *refs: ours(chips, *refs), "ours", half)(hidden, w_down)
    match, weight = call(
        lambda *refs: score(ep_count, chips, *refs),
        "score",
        (
            jax.ShapeDtypeStruct((row_count, chips * slot_count), jnp.bfloat16),
            jax.ShapeDtypeStruct((row_count, 1), jnp.float32),
        ),
        in_specs=[vmem] * 2 + [anywhere],
    )(ids, scores, other)
    summed = call(add, "add", half, in_specs=[vmem] * 2 + [anywhere])(mine, crossed, weight)
    returned = exchange(summed, second_order)
    return call(
        combine,
        "combine",
        jax.ShapeDtypeStruct((row_count, features), jnp.bfloat16),
        out_specs=hbm,
        scratch_shapes=[
            pltpu.VMEM((row_count, features), jnp.bfloat16),
            pltpu.SemaphoreType.DMA((row_count // PIECE,)),
        ],
    )(match, weight, returned)


def solution(mesh):
    groups, ep_count, tp_count = (mesh.shape[name] for name in ("groups", "ep", "tp"))
    split = jax.sharding.Mesh(
        mesh.devices.reshape(groups, ep_count, tp_count // 2, 2), ("groups", "ep", "chip", "core")
    )
    tp = ("chip", "core")
    placed = (
        P(("groups", "ep"), tp),
        P(("groups", "ep"), None),
        P(("groups", "ep"), None),
        P("ep", None, tp),
        P("ep", None, tp),
        P("ep", tp, None),
    )
    return jax.shard_map(
        shards, mesh=split, in_specs=placed, out_specs=P(("groups", "ep"), tp), check_vma=False
    )
```

```python
import jax
import jax.numpy as jnp
from jax import lax
from jax.experimental import pallas as pl
from jax.experimental.pallas import tpu as pltpu
from jax.sharding import PartitionSpec as P

CAP = 8
PIECE = 32
FETCH = 16
FAR = ("ep", "chip", "core")
SWAP = [(0, 1), (1, 0)]
LIMIT = pltpu.CompilerParams(vmem_limit_bytes=16 * 1024 * 1024)


def iota(shape, dim):
    return lax.broadcasted_iota(jnp.int32, shape, dim)


def to_column(row):
    size = row.shape[1]
    square = (size, size)
    return jnp.sum(jnp.where(iota(square, 0) == iota(square, 1), row, 0.0), axis=1, keepdims=True)


def slot_codes(ids, resident):
    row_count = ids.shape[1]
    expert = jnp.min(ids, axis=0, keepdims=True)
    onehot_shape = (-(-resident // 16) * 16, row_count)
    onehot = jnp.where(expert == iota(onehot_shape, 0).astype(jnp.float32), 1.0, 0.0)
    square = (row_count, row_count)
    earlier = jnp.where(iota(square, 0) < iota(square, 1), 1.0, 0.0).astype(jnp.bfloat16)
    counts = jnp.dot(onehot.astype(jnp.bfloat16), earlier, preferred_element_type=jnp.float32)
    return expert * CAP + jnp.sum(counts * onehot, axis=0, keepdims=True), expert


def first_order(ep_count, chip):
    listed = ((0, 1, 3, 2), (3, 1, 2, 0))[chip % 2]
    return [z // 4 * 4 + listed[z % 4] for z in range(ep_count)]


def second_order(ep_count, chip):
    listed = ((2, 1, 0, 3), (3, 1, 2, 0))[chip % 2]
    return [z // 4 * 4 + listed[z % 4] for z in range(ep_count)]


def row_codes(index, order, ep_count, chips):
    listed = [z for chip in range(chips) for z in order(ep_count, chip)]
    expert = sum(jnp.where(index // CAP == at, z // 2, 0) for at, z in enumerate(listed))
    return (expert * CAP + lax.rem(index, CAP)).astype(jnp.float32)


def route(ep_count, chips, ids_hbm, tokens_hbm, outgoing_ref, ids_ref, tokens_ref, sems):
    row_count = ids_ref.shape[1]
    parts = row_count // FETCH
    copies = [pltpu.make_async_copy(ids_hbm, ids_ref, sems.at[parts])] + [
        pltpu.make_async_copy(
            tokens_hbm.at[pl.ds(part * FETCH, FETCH), :],
            tokens_ref.at[pl.ds(part * FETCH, FETCH), :],
            sems.at[part],
        )
        for part in range(parts)
    ]
    for copy in copies:
        copy.start()
    wanted = row_codes(iota((outgoing_ref.shape[0], row_count), 0), first_order, ep_count, chips)
    copies[0].wait()
    code, _ = slot_codes(ids_ref[...].astype(jnp.float32), ep_count // 2)
    dispatch = jnp.where(code == wanted, 1.0, 0.0).astype(jnp.bfloat16)
    for copy in copies[1:]:
        copy.wait()
    outgoing_ref[...] = jnp.dot(
        dispatch, tokens_ref[...], preferred_element_type=jnp.float32
    ).astype(jnp.bfloat16)


def score(ep_count, chips, ids_ref, scores_ref, _, match_ref, weight_ref):
    ids = ids_ref[...].astype(jnp.float32)
    code, expert = slot_codes(ids, ep_count // 2)
    wanted = row_codes(iota(match_ref.shape, 1), second_order, ep_count, chips)
    match_ref[...] = jnp.where(to_column(code) == wanted, 1.0, 0.0).astype(jnp.bfloat16)
    squashed = jax.nn.sigmoid(scores_ref[...])
    chosen = jnp.sum(jnp.where(ids == expert, squashed, 0.0), axis=0, keepdims=True)
    weight_ref[...] = to_column(2.5 * chosen / jnp.sum(squashed, axis=0, keepdims=True))


def far_groups(order, ep_count, chips):
    return [
        [(z * chips + x) * 2 + (side + x) % 2 for x in range(chips) for z in order(ep_count, x)]
        for side in range(2)
    ]


def columns_of(chip, own, features):
    core = lax.rem(lax.axis_index("core") + lax.axis_index("chip") + chip + (0 if own else 1), 2)
    return pl.ds(pl.multiple_of((2 * chip + core) * features, features), features)


def in_order(values, held, wanted):
    if held == wanted:
        return values
    blocks = [values[held.index(z) * CAP : (held.index(z) + 1) * CAP, :] for z in wanted]
    return jnp.concatenate(blocks, axis=0)


def lift(chips, own, rows_ref, gate_ref, up_ref):
    part_rows, features = rows_ref.shape[0] // chips, rows_ref.shape[1]
    ep_count = part_rows // CAP
    total = jnp.zeros((part_rows, 2 * gate_ref.shape[2]), jnp.float32)
    for chip in range(chips):
        rows = rows_ref[chip * part_rows : (chip + 1) * part_rows, :]
        columns = columns_of(chip, own, features)
        both = jnp.concatenate([gate_ref[0, columns, :], up_ref[0, columns, :]], axis=1)
        acts = jnp.dot(rows, both, preferred_element_type=jnp.float32)
        total += in_order(acts, first_order(ep_count, chip), first_order(ep_count, 0))
    return total


def lower(chips, own, hidden, down_ref, out_ref):
    part_rows, features = out_ref.shape[0] // chips, out_ref.shape[1]
    ep_count = part_rows // CAP
    for chip in range(chips):
        columns = columns_of(chip, own, features)
        values = jnp.dot(hidden, down_ref[0, :, columns], preferred_element_type=jnp.float32)
        values = in_order(values, first_order(ep_count, 0), second_order(ep_count, chip))
        out_ref[chip * part_rows : (chip + 1) * part_rows, :] = values.astype(jnp.bfloat16)


def begin(chips, rows_ref, gate_ref, up_ref, acts_ref):
    acts_ref[...] = lift(chips, True, rows_ref, gate_ref, up_ref)


def theirs(chips, rows_ref, acts_ref, gate_ref, up_ref, down_ref, hidden_ref, other_ref):
    width = gate_ref.shape[2]
    acts = acts_ref[...] + lift(chips, False, rows_ref, gate_ref, up_ref)
    gate_act, up_act = acts[:, :width], acts[:, width:]
    hidden = (gate_act / (1.0 + jnp.exp(-gate_act)) * up_act).astype(jnp.bfloat16)
    hidden_ref[...] = hidden
    lower(chips, False, hidden, down_ref, other_ref)


def ours(chips, hidden_ref, down_ref, mine_ref):
    lower(chips, True, hidden_ref[...], down_ref, mine_ref)


def add(mine_ref, other_ref, _, out_ref):
    total = mine_ref[...].astype(jnp.float32) + other_ref[...].astype(jnp.float32)
    out_ref[...] = total.astype(jnp.bfloat16)


def combine(match_ref, weight_ref, returned_ref, out_hbm, out_ref, sems):
    copies = []
    summed = jnp.dot(match_ref[...], returned_ref[...], preferred_element_type=jnp.float32)
    for part in range(out_ref.shape[0] // PIECE):
        rows = pl.ds(part * PIECE, PIECE)
        piece = summed[part * PIECE : (part + 1) * PIECE, :]
        out_ref[rows, :] = (weight_ref[rows, :] * piece).astype(jnp.bfloat16)
        copies.append(pltpu.make_async_copy(out_ref.at[rows, :], out_hbm.at[rows, :], sems.at[part]))
        copies[-1].start()
    for copy in copies:
        copy.wait()


def shards(tokens, expert_ids, route_scores, w_gate, w_up, w_down):
    row_count, features = tokens.shape
    top_count, hidden_count = expert_ids.shape[1], w_gate.shape[2]
    ep_count, chips = lax.axis_size("ep"), lax.axis_size("chip")
    slot_count = ep_count * CAP
    half = jax.ShapeDtypeStruct((chips * slot_count, features), jnp.bfloat16)
    ids, scores = expert_ids.T, route_scores.T
    hbm, vmem = (pl.BlockSpec(memory_space=space) for space in (pltpu.HBM, pltpu.VMEM))
    anywhere = pl.BlockSpec(memory_space=pl.ANY)

    def exchange(rows, order):
        groups = far_groups(order, ep_count, chips)
        return lax.all_to_all(rows, FAR, 0, 0, axis_index_groups=groups, tiled=True)

    def call(kernel, name, out_shape, **rest):
        return pl.pallas_call(kernel, out_shape=out_shape, name=name, compiler_params=LIMIT, **rest)

    outgoing = call(
        lambda *refs: route(ep_count, chips, *refs),
        "route",
        half,
        in_specs=[hbm] * 2,
        scratch_shapes=[
            pltpu.VMEM((top_count, row_count), jnp.int32),
            pltpu.VMEM((row_count, features), jnp.bfloat16),
            pltpu.SemaphoreType.DMA((row_count // FETCH + 1,)),
        ],
        cost_estimate=pl.CostEstimate(flops=2 * 10**9, bytes_accessed=0, transcendentals=0),
    )(*(pltpu.with_memory_space_constraint(value, pltpu.HBM) for value in (ids, tokens)))
    incoming = exchange(outgoing, first_order)
    across = lax.ppermute(incoming, "core", SWAP)
    acts = jax.ShapeDtypeStruct((slot_count, 2 * hidden_count), jnp.float32)
    begun = call(lambda *refs: begin(chips, *refs), "begin", acts)(incoming, w_gate, w_up)
    hidden_shape = jax.ShapeDtypeStruct((slot_count, hidden_count), jnp.bfloat16)
    hidden, other = call(lambda *refs: theirs(chips, *refs), "theirs", (hidden_shape, half))(
        across, begun, w_gate, w_up, w_down
    )
    crossed = lax.ppermute(other, "core", SWAP)
    mine = call(lambda *refs: ours(chips, *refs), "ours", half)(hidden, w_down)
    match, weight = call(
        lambda *refs: score(ep_count, chips, *refs),
        "score",
        (
            jax.ShapeDtypeStruct((row_count, chips * slot_count), jnp.bfloat16),
            jax.ShapeDtypeStruct((row_count, 1), jnp.float32),
        ),
        in_specs=[vmem] * 2 + [anywhere],
    )(ids, scores, other)
    summed = call(add, "add", half, in_specs=[vmem] * 2 + [anywhere])(mine, crossed, weight)
    returned = exchange(summed, second_order)
    return call(
        combine,
        "combine",
        jax.ShapeDtypeStruct((row_count, features), jnp.bfloat16),
        out_specs=hbm,
        scratch_shapes=[
            pltpu.VMEM((row_count, features), jnp.bfloat16),
            pltpu.SemaphoreType.DMA((row_count // PIECE,)),
        ],
    )(match, weight, returned)


def solution(mesh):
    groups, ep_count, tp_count = (mesh.shape[name] for name in ("groups", "ep", "tp"))
    split = jax.sharding.Mesh(
        mesh.devices.reshape(groups, ep_count, tp_count // 2, 2), ("groups", "ep", "chip", "core")
    )
    tp = ("chip", "core")
    placed = (
        P(("groups", "ep"), tp),
        P(("groups", "ep"), None),
        P(("groups", "ep"), None),
        P("ep", None, tp),
        P("ep", None, tp),
        P("ep", tp, None),
    )
    return jax.shard_map(
        shards, mesh=split, in_specs=placed, out_specs=P(("groups", "ep"), tp), check_vma=False
    )
```

```python
import jax
import jax.numpy as jnp
from jax import lax
from jax.experimental import pallas as pl
from jax.experimental.pallas import tpu as pltpu
from jax.sharding import PartitionSpec as P

CAP = 8
PIECE = 32
FETCH = 16
FAR = ("ep", "chip", "core")
SWAP = [(0, 1), (1, 0)]
LIMIT = pltpu.CompilerParams(vmem_limit_bytes=16 * 1024 * 1024)


def iota(shape, dim):
    return lax.broadcasted_iota(jnp.int32, shape, dim)


def to_column(row):
    size = row.shape[1]
    square = (size, size)
    return jnp.sum(jnp.where(iota(square, 0) == iota(square, 1), row, 0.0), axis=1, keepdims=True)


def slot_codes(ids, resident):
    row_count = ids.shape[1]
    expert = jnp.min(ids, axis=0, keepdims=True)
    onehot_shape = (-(-resident // 16) * 16, row_count)
    onehot = jnp.where(expert == iota(onehot_shape, 0).astype(jnp.float32), 1.0, 0.0)
    square = (row_count, row_count)
    earlier = jnp.where(iota(square, 0) < iota(square, 1), 1.0, 0.0).astype(jnp.bfloat16)
    counts = jnp.dot(onehot.astype(jnp.bfloat16), earlier, preferred_element_type=jnp.float32)
    return expert * CAP + jnp.sum(counts * onehot, axis=0, keepdims=True), expert


def first_order(ep_count, chip):
    listed = ((2, 3, 1, 0), (3, 2, 1, 0))[chip % 2]
    return [z // 4 * 4 + listed[z % 4] for z in range(ep_count)]


def second_order(ep_count, chip):
    listed = ((3, 1, 2, 0), (3, 0, 2, 1))[chip % 2]
    return [z // 4 * 4 + listed[z % 4] for z in range(ep_count)]


def row_codes(index, order, ep_count, chips):
    listed = [z for chip in range(chips) for z in order(ep_count, chip)]
    expert = sum(jnp.where(index // CAP == at, z // 2, 0) for at, z in enumerate(listed))
    return (expert * CAP + lax.rem(index, CAP)).astype(jnp.float32)


def route(ep_count, chips, ids_hbm, tokens_hbm, outgoing_ref, ids_ref, tokens_ref, sems):
    row_count = ids_ref.shape[1]
    parts = row_count // FETCH
    copies = [pltpu.make_async_copy(ids_hbm, ids_ref, sems.at[parts])] + [
        pltpu.make_async_copy(
            tokens_hbm.at[pl.ds(part * FETCH, FETCH), :],
            tokens_ref.at[pl.ds(part * FETCH, FETCH), :],
            sems.at[part],
        )
        for part in range(parts)
    ]
    for copy in copies:
        copy.start()
    wanted = row_codes(iota((outgoing_ref.shape[0], row_count), 0), first_order, ep_count, chips)
    copies[0].wait()
    code, _ = slot_codes(ids_ref[...].astype(jnp.float32), ep_count // 2)
    dispatch = jnp.where(code == wanted, 1.0, 0.0).astype(jnp.bfloat16)
    for copy in copies[1:]:
        copy.wait()
    outgoing_ref[...] = jnp.dot(
        dispatch, tokens_ref[...], preferred_element_type=jnp.float32
    ).astype(jnp.bfloat16)


def score(ep_count, chips, ids_ref, scores_ref, _, match_ref, weight_ref):
    ids = ids_ref[...].astype(jnp.float32)
    code, expert = slot_codes(ids, ep_count // 2)
    wanted = row_codes(iota(match_ref.shape, 1), second_order, ep_count, chips)
    match_ref[...] = jnp.where(to_column(code) == wanted, 1.0, 0.0).astype(jnp.bfloat16)
    squashed = jax.nn.sigmoid(scores_ref[...])
    chosen = jnp.sum(jnp.where(ids == expert, squashed, 0.0), axis=0, keepdims=True)
    weight_ref[...] = to_column(2.5 * chosen / jnp.sum(squashed, axis=0, keepdims=True))


def far_groups(order, ep_count, chips):
    return [
        [(z * chips + x) * 2 + (side + x) % 2 for x in range(chips) for z in order(ep_count, x)]
        for side in range(2)
    ]


def columns_of(chip, own, features):
    core = lax.rem(lax.axis_index("core") + lax.axis_index("chip") + chip + (0 if own else 1), 2)
    return pl.ds(pl.multiple_of((2 * chip + core) * features, features), features)


def in_order(values, held, wanted):
    if held == wanted:
        return values
    blocks = [values[held.index(z) * CAP : (held.index(z) + 1) * CAP, :] for z in wanted]
    return jnp.concatenate(blocks, axis=0)


def lift(chips, own, rows_ref, gate_ref, up_ref):
    part_rows, features = rows_ref.shape[0] // chips, rows_ref.shape[1]
    ep_count = part_rows // CAP
    total = jnp.zeros((part_rows, 2 * gate_ref.shape[2]), jnp.float32)
    for chip in range(chips):
        rows = rows_ref[chip * part_rows : (chip + 1) * part_rows, :]
        columns = columns_of(chip, own, features)
        both = jnp.concatenate([gate_ref[0, columns, :], up_ref[0, columns, :]], axis=1)
        acts = jnp.dot(rows, both, preferred_element_type=jnp.float32)
        total += in_order(acts, first_order(ep_count, chip), first_order(ep_count, 0))
    return total


def lower(chips, own, hidden, down_ref, out_ref):
    part_rows, features = out_ref.shape[0] // chips, out_ref.shape[1]
    ep_count = part_rows // CAP
    for chip in range(chips):
        columns = columns_of(chip, own, features)
        values = jnp.dot(hidden, down_ref[0, :, columns], preferred_element_type=jnp.float32)
        values = in_order(values, first_order(ep_count, 0), second_order(ep_count, chip))
        out_ref[chip * part_rows : (chip + 1) * part_rows, :] = values.astype(jnp.bfloat16)


def begin(chips, rows_ref, gate_ref, up_ref, acts_ref):
    acts_ref[...] = lift(chips, True, rows_ref, gate_ref, up_ref)


def theirs(chips, rows_ref, acts_ref, gate_ref, up_ref, down_ref, hidden_ref, other_ref):
    width = gate_ref.shape[2]
    acts = acts_ref[...] + lift(chips, False, rows_ref, gate_ref, up_ref)
    gate_act, up_act = acts[:, :width], acts[:, width:]
    hidden = (gate_act / (1.0 + jnp.exp(-gate_act)) * up_act).astype(jnp.bfloat16)
    hidden_ref[...] = hidden
    lower(chips, False, hidden, down_ref, other_ref)


def ours(chips, hidden_ref, down_ref, mine_ref):
    lower(chips, True, hidden_ref[...], down_ref, mine_ref)


def add(mine_ref, other_ref, _, out_ref):
    total = mine_ref[...].astype(jnp.float32) + other_ref[...].astype(jnp.float32)
    out_ref[...] = total.astype(jnp.bfloat16)


def combine(match_ref, weight_ref, returned_ref, out_hbm, out_ref, sems):
    copies = []
    for part in range(out_ref.shape[0] // PIECE):
        rows = pl.ds(part * PIECE, PIECE)
        summed = jnp.dot(match_ref[rows, :], returned_ref[...], preferred_element_type=jnp.float32)
        out_ref[rows, :] = (weight_ref[rows, :] * summed).astype(jnp.bfloat16)
        copies.append(pltpu.make_async_copy(out_ref.at[rows, :], out_hbm.at[rows, :], sems.at[part]))
        copies[-1].start()
    for copy in copies:
        copy.wait()


def shards(tokens, expert_ids, route_scores, w_gate, w_up, w_down):
    row_count, features = tokens.shape
    top_count, hidden_count = expert_ids.shape[1], w_gate.shape[2]
    ep_count, chips = lax.axis_size("ep"), lax.axis_size("chip")
    slot_count = ep_count * CAP
    half = jax.ShapeDtypeStruct((chips * slot_count, features), jnp.bfloat16)
    ids, scores = expert_ids.T, route_scores.T
    hbm, vmem = (pl.BlockSpec(memory_space=space) for space in (pltpu.HBM, pltpu.VMEM))
    anywhere = pl.BlockSpec(memory_space=pl.ANY)

    def exchange(rows, order):
        groups = far_groups(order, ep_count, chips)
        return lax.all_to_all(rows, FAR, 0, 0, axis_index_groups=groups, tiled=True)

    def call(kernel, name, out_shape, **rest):
        return pl.pallas_call(kernel, out_shape=out_shape, name=name, compiler_params=LIMIT, **rest)

    outgoing = call(
        lambda *refs: route(ep_count, chips, *refs),
        "route",
        half,
        in_specs=[hbm] * 2,
        scratch_shapes=[
            pltpu.VMEM((top_count, row_count), jnp.int32),
            pltpu.VMEM((row_count, features), jnp.bfloat16),
            pltpu.SemaphoreType.DMA((row_count // FETCH + 1,)),
        ],
        cost_estimate=pl.CostEstimate(flops=2 * 10**9, bytes_accessed=0, transcendentals=0),
    )(*(pltpu.with_memory_space_constraint(value, pltpu.HBM) for value in (ids, tokens)))
    incoming = exchange(outgoing, first_order)
    across = lax.ppermute(incoming, "core", SWAP)
    acts = jax.ShapeDtypeStruct((slot_count, 2 * hidden_count), jnp.float32)
    begun = call(lambda *refs: begin(chips, *refs), "begin", acts)(incoming, w_gate, w_up)
    hidden_shape = jax.ShapeDtypeStruct((slot_count, hidden_count), jnp.bfloat16)
    hidden, other = call(lambda *refs: theirs(chips, *refs), "theirs", (hidden_shape, half))(
        across, begun, w_gate, w_up, w_down
    )
    crossed = lax.ppermute(other, "core", SWAP)
    mine = call(lambda *refs: ours(chips, *refs), "ours", half)(hidden, w_down)
    match, weight = call(
        lambda *refs: score(ep_count, chips, *refs),
        "score",
        (
            jax.ShapeDtypeStruct((row_count, chips * slot_count), jnp.bfloat16),
            jax.ShapeDtypeStruct((row_count, 1), jnp.float32),
        ),
        in_specs=[vmem] * 2 + [anywhere],
    )(ids, scores, other)
    summed = call(add, "add", half, in_specs=[vmem] * 2 + [anywhere])(mine, crossed, weight)
    returned = exchange(summed, second_order)
    return call(
        combine,
        "combine",
        jax.ShapeDtypeStruct((row_count, features), jnp.bfloat16),
        out_specs=hbm,
        scratch_shapes=[
            pltpu.VMEM((row_count, features), jnp.bfloat16),
            pltpu.SemaphoreType.DMA((row_count // PIECE,)),
        ],
    )(match, weight, returned)


def solution(mesh):
    groups, ep_count, tp_count = (mesh.shape[name] for name in ("groups", "ep", "tp"))
    split = jax.sharding.Mesh(
        mesh.devices.reshape(groups, ep_count, tp_count // 2, 2), ("groups", "ep", "chip", "core")
    )
    tp = ("chip", "core")
    placed = (
        P(("groups", "ep"), tp),
        P(("groups", "ep"), None),
        P(("groups", "ep"), None),
        P("ep", None, tp),
        P("ep", None, tp),
        P("ep", tp, None),
    )
    return jax.shard_map(
        shards, mesh=split, in_specs=placed, out_specs=P(("groups", "ep"), tp), check_vma=False
    )
```

```python
import jax
import jax.numpy as jnp
from jax import lax
from jax.experimental import pallas as pl
from jax.experimental.pallas import tpu as pltpu
from jax.sharding import PartitionSpec as P

CAP = 8
PIECE = 32
FETCH = 16
FAR = ("ep", "chip", "core")
SWAP = [(0, 1), (1, 0)]
LIMIT = pltpu.CompilerParams(vmem_limit_bytes=16 * 1024 * 1024)


def iota(shape, dim):
    return lax.broadcasted_iota(jnp.int32, shape, dim)


def to_column(row):
    size = row.shape[1]
    square = (size, size)
    return jnp.sum(jnp.where(iota(square, 0) == iota(square, 1), row, 0.0), axis=1, keepdims=True)


def slot_codes(ids, resident):
    row_count = ids.shape[1]
    expert = jnp.min(ids, axis=0, keepdims=True)
    onehot_shape = (-(-resident // 16) * 16, row_count)
    onehot = jnp.where(expert == iota(onehot_shape, 0).astype(jnp.float32), 1.0, 0.0)
    square = (row_count, row_count)
    earlier = jnp.where(iota(square, 0) < iota(square, 1), 1.0, 0.0).astype(jnp.bfloat16)
    counts = jnp.dot(onehot.astype(jnp.bfloat16), earlier, preferred_element_type=jnp.float32)
    return expert * CAP + jnp.sum(counts * onehot, axis=0, keepdims=True), expert


def first_order(ep_count, chip):
    listed = ((3, 2, 0, 1), (3, 2, 1, 0))[chip % 2]
    return [z // 4 * 4 + listed[z % 4] for z in range(ep_count)]


def second_order(ep_count, chip):
    listed = ((2, 1, 0, 3), (3, 2, 1, 0))[chip % 2]
    return [z // 4 * 4 + listed[z % 4] for z in range(ep_count)]


def row_codes(index, order, ep_count, chips):
    listed = [z for chip in range(chips) for z in order(ep_count, chip)]
    expert = sum(jnp.where(index // CAP == at, z // 2, 0) for at, z in enumerate(listed))
    return (expert * CAP + lax.rem(index, CAP)).astype(jnp.float32)


def route(ep_count, chips, ids_hbm, tokens_hbm, outgoing_ref, ids_ref, tokens_ref, sems):
    row_count = ids_ref.shape[1]
    parts = row_count // FETCH
    copies = [pltpu.make_async_copy(ids_hbm, ids_ref, sems.at[parts])] + [
        pltpu.make_async_copy(
            tokens_hbm.at[pl.ds(part * FETCH, FETCH), :],
            tokens_ref.at[pl.ds(part * FETCH, FETCH), :],
            sems.at[part],
        )
        for part in range(parts)
    ]
    for copy in copies:
        copy.start()
    wanted = row_codes(iota((outgoing_ref.shape[0], row_count), 0), first_order, ep_count, chips)
    copies[0].wait()
    code, _ = slot_codes(ids_ref[...].astype(jnp.float32), ep_count // 2)
    dispatch = jnp.where(code == wanted, 1.0, 0.0).astype(jnp.bfloat16)
    for copy in copies[1:]:
        copy.wait()
    outgoing_ref[...] = jnp.dot(
        dispatch, tokens_ref[...], preferred_element_type=jnp.float32
    ).astype(jnp.bfloat16)


def score(ep_count, chips, ids_ref, scores_ref, _, match_ref, weight_ref):
    ids = ids_ref[...].astype(jnp.float32)
    code, expert = slot_codes(ids, ep_count // 2)
    wanted = row_codes(iota(match_ref.shape, 1), second_order, ep_count, chips)
    match_ref[...] = jnp.where(to_column(code) == wanted, 1.0, 0.0).astype(jnp.bfloat16)
    squashed = jax.nn.sigmoid(scores_ref[...])
    chosen = jnp.sum(jnp.where(ids == expert, squashed, 0.0), axis=0, keepdims=True)
    weight_ref[...] = to_column(2.5 * chosen / jnp.sum(squashed, axis=0, keepdims=True))


def far_groups(order, ep_count, chips):
    return [
        [(z * chips + x) * 2 + (side + x) % 2 for x in range(chips) for z in order(ep_count, x)]
        for side in range(2)
    ]


def columns_of(chip, own, features):
    core = lax.rem(lax.axis_index("core") + lax.axis_index("chip") + chip + (0 if own else 1), 2)
    return pl.ds(pl.multiple_of((2 * chip + core) * features, features), features)


def in_order(values, held, wanted):
    if held == wanted:
        return values
    blocks = [values[held.index(z) * CAP : (held.index(z) + 1) * CAP, :] for z in wanted]
    return jnp.concatenate(blocks, axis=0)


def lift(chips, own, rows_ref, gate_ref, up_ref):
    part_rows, features = rows_ref.shape[0] // chips, rows_ref.shape[1]
    ep_count = part_rows // CAP
    total = jnp.zeros((part_rows, 2 * gate_ref.shape[2]), jnp.float32)
    for chip in range(chips):
        rows = rows_ref[chip * part_rows : (chip + 1) * part_rows, :]
        columns = columns_of(chip, own, features)
        both = jnp.concatenate([gate_ref[0, columns, :], up_ref[0, columns, :]], axis=1)
        acts = jnp.dot(rows, both, preferred_element_type=jnp.float32)
        total += in_order(acts, first_order(ep_count, chip), first_order(ep_count, 0))
    return total


def lower(chips, own, hidden, down_ref, out_ref):
    part_rows, features = out_ref.shape[0] // chips, out_ref.shape[1]
    ep_count = part_rows // CAP
    for chip in range(chips):
        columns = columns_of(chip, own, features)
        values = jnp.dot(hidden, down_ref[0, :, columns], preferred_element_type=jnp.float32)
        values = in_order(values, first_order(ep_count, 0), second_order(ep_count, chip))
        out_ref[chip * part_rows : (chip + 1) * part_rows, :] = values.astype(jnp.bfloat16)


def begin(chips, rows_ref, gate_ref, up_ref, acts_ref):
    acts_ref[...] = lift(chips, True, rows_ref, gate_ref, up_ref)


def theirs(chips, rows_ref, acts_ref, gate_ref, up_ref, down_ref, hidden_ref, other_ref):
    width = gate_ref.shape[2]
    acts = acts_ref[...] + lift(chips, False, rows_ref, gate_ref, up_ref)
    gate_act, up_act = acts[:, :width], acts[:, width:]
    hidden = (gate_act / (1.0 + jnp.exp(-gate_act)) * up_act).astype(jnp.bfloat16)
    hidden_ref[...] = hidden
    lower(chips, False, hidden, down_ref, other_ref)


def ours(chips, hidden_ref, down_ref, mine_ref):
    lower(chips, True, hidden_ref[...], down_ref, mine_ref)


def add(mine_ref, other_ref, _, out_ref):
    total = mine_ref[...].astype(jnp.float32) + other_ref[...].astype(jnp.float32)
    out_ref[...] = total.astype(jnp.bfloat16)


def combine(match_ref, weight_ref, returned_ref, out_hbm, out_ref, sems):
    copies = []
    for part in range(out_ref.shape[0] // PIECE):
        rows = pl.ds(part * PIECE, PIECE)
        summed = jnp.dot(match_ref[rows, :], returned_ref[...], preferred_element_type=jnp.float32)
        out_ref[rows, :] = (weight_ref[rows, :] * summed).astype(jnp.bfloat16)
        copies.append(pltpu.make_async_copy(out_ref.at[rows, :], out_hbm.at[rows, :], sems.at[part]))
        copies[-1].start()
    for copy in copies:
        copy.wait()


def shards(tokens, expert_ids, route_scores, w_gate, w_up, w_down):
    row_count, features = tokens.shape
    top_count, hidden_count = expert_ids.shape[1], w_gate.shape[2]
    ep_count, chips = lax.axis_size("ep"), lax.axis_size("chip")
    slot_count = ep_count * CAP
    half = jax.ShapeDtypeStruct((chips * slot_count, features), jnp.bfloat16)
    ids, scores = expert_ids.T, route_scores.T
    hbm, vmem = (pl.BlockSpec(memory_space=space) for space in (pltpu.HBM, pltpu.VMEM))
    anywhere = pl.BlockSpec(memory_space=pl.ANY)

    def exchange(rows, order):
        groups = far_groups(order, ep_count, chips)
        return lax.all_to_all(rows, FAR, 0, 0, axis_index_groups=groups, tiled=True)

    def call(kernel, name, out_shape, **rest):
        return pl.pallas_call(kernel, out_shape=out_shape, name=name, compiler_params=LIMIT, **rest)

    outgoing = call(
        lambda *refs: route(ep_count, chips, *refs),
        "route",
        half,
        in_specs=[hbm] * 2,
        scratch_shapes=[
            pltpu.VMEM((top_count, row_count), jnp.int32),
            pltpu.VMEM((row_count, features), jnp.bfloat16),
            pltpu.SemaphoreType.DMA((row_count // FETCH + 1,)),
        ],
        cost_estimate=pl.CostEstimate(flops=2 * 10**9, bytes_accessed=0, transcendentals=0),
    )(*(pltpu.with_memory_space_constraint(value, pltpu.HBM) for value in (ids, tokens)))
    incoming = exchange(outgoing, first_order)
    across = lax.ppermute(incoming, "core", SWAP)
    acts = jax.ShapeDtypeStruct((slot_count, 2 * hidden_count), jnp.float32)
    begun = call(lambda *refs: begin(chips, *refs), "begin", acts)(incoming, w_gate, w_up)
    hidden_shape = jax.ShapeDtypeStruct((slot_count, hidden_count), jnp.bfloat16)
    hidden, other = call(lambda *refs: theirs(chips, *refs), "theirs", (hidden_shape, half))(
        across, begun, w_gate, w_up, w_down
    )
    crossed = lax.ppermute(other, "core", SWAP)
    mine = call(lambda *refs: ours(chips, *refs), "ours", half)(hidden, w_down)
    match, weight = call(
        lambda *refs: score(ep_count, chips, *refs),
        "score",
        (
            jax.ShapeDtypeStruct((row_count, chips * slot_count), jnp.bfloat16),
            jax.ShapeDtypeStruct((row_count, 1), jnp.float32),
        ),
        in_specs=[vmem] * 2 + [anywhere],
    )(ids, scores, other)
    summed = call(add, "add", half, in_specs=[vmem] * 2 + [anywhere])(mine, crossed, weight)
    returned = exchange(summed, second_order)
    return call(
        combine,
        "combine",
        jax.ShapeDtypeStruct((row_count, features), jnp.bfloat16),
        out_specs=hbm,
        scratch_shapes=[
            pltpu.VMEM((row_count, features), jnp.bfloat16),
            pltpu.SemaphoreType.DMA((row_count // PIECE,)),
        ],
    )(match, weight, returned)


def solution(mesh):
    groups, ep_count, tp_count = (mesh.shape[name] for name in ("groups", "ep", "tp"))
    split = jax.sharding.Mesh(
        mesh.devices.reshape(groups, ep_count, tp_count // 2, 2), ("groups", "ep", "chip", "core")
    )
    tp = ("chip", "core")
    placed = (
        P(("groups", "ep"), tp),
        P(("groups", "ep"), None),
        P(("groups", "ep"), None),
        P("ep", None, tp),
        P("ep", None, tp),
        P("ep", tp, None),
    )
    return jax.shard_map(
        shards, mesh=split, in_specs=placed, out_specs=P(("groups", "ep"), tp), check_vma=False
    )
```

```python
import jax
import jax.numpy as jnp
from jax import lax
from jax.experimental import pallas as pl
from jax.experimental.pallas import tpu as pltpu
from jax.sharding import PartitionSpec as P

CAP = 8
PIECE = 32
FETCH = 16
FAR = ("ep", "chip", "core")
SWAP = [(0, 1), (1, 0)]
LIMIT = pltpu.CompilerParams(vmem_limit_bytes=16 * 1024 * 1024)


def iota(shape, dim):
    return lax.broadcasted_iota(jnp.int32, shape, dim)


def to_column(row):
    size = row.shape[1]
    square = (size, size)
    return jnp.sum(jnp.where(iota(square, 0) == iota(square, 1), row, 0.0), axis=1, keepdims=True)


def slot_codes(ids, resident):
    row_count = ids.shape[1]
    expert = jnp.min(ids, axis=0, keepdims=True)
    onehot_shape = (-(-resident // 16) * 16, row_count)
    onehot = jnp.where(expert == iota(onehot_shape, 0).astype(jnp.float32), 1.0, 0.0)
    square = (row_count, row_count)
    earlier = jnp.where(iota(square, 0) < iota(square, 1), 1.0, 0.0).astype(jnp.bfloat16)
    counts = jnp.dot(onehot.astype(jnp.bfloat16), earlier, preferred_element_type=jnp.float32)
    return expert * CAP + jnp.sum(counts * onehot, axis=0, keepdims=True), expert


def first_order(ep_count, chip):
    listed = ((2, 3, 0, 1), (2, 3, 1, 0))[chip % 2]
    return [z // 4 * 4 + listed[z % 4] for z in range(ep_count)]


def second_order(ep_count, chip):
    listed = ((2, 1, 0, 3), (3, 2, 0, 1))[chip % 2]
    return [z // 4 * 4 + listed[z % 4] for z in range(ep_count)]


def row_codes(index, order, ep_count, chips):
    listed = [z for chip in range(chips) for z in order(ep_count, chip)]
    expert = sum(jnp.where(index // CAP == at, z // 2, 0) for at, z in enumerate(listed))
    return (expert * CAP + lax.rem(index, CAP)).astype(jnp.float32)


def route(ep_count, chips, ids_hbm, tokens_hbm, outgoing_ref, ids_ref, tokens_ref, sems):
    row_count = ids_ref.shape[1]
    parts = row_count // FETCH
    copies = [pltpu.make_async_copy(ids_hbm, ids_ref, sems.at[parts])] + [
        pltpu.make_async_copy(
            tokens_hbm.at[pl.ds(part * FETCH, FETCH), :],
            tokens_ref.at[pl.ds(part * FETCH, FETCH), :],
            sems.at[part],
        )
        for part in range(parts)
    ]
    for copy in copies:
        copy.start()
    wanted = row_codes(iota((outgoing_ref.shape[0], row_count), 0), first_order, ep_count, chips)
    copies[0].wait()
    code, _ = slot_codes(ids_ref[...].astype(jnp.float32), ep_count // 2)
    dispatch = jnp.where(code == wanted, 1.0, 0.0).astype(jnp.bfloat16)
    for copy in copies[1:]:
        copy.wait()
    outgoing_ref[...] = jnp.dot(
        dispatch, tokens_ref[...], preferred_element_type=jnp.float32
    ).astype(jnp.bfloat16)


def score(ep_count, chips, ids_ref, scores_ref, _, match_ref, weight_ref):
    ids = ids_ref[...].astype(jnp.float32)
    code, expert = slot_codes(ids, ep_count // 2)
    wanted = row_codes(iota(match_ref.shape, 1), second_order, ep_count, chips)
    match_ref[...] = jnp.where(to_column(code) == wanted, 1.0, 0.0).astype(jnp.bfloat16)
    squashed = jax.nn.sigmoid(scores_ref[...])
    chosen = jnp.sum(jnp.where(ids == expert, squashed, 0.0), axis=0, keepdims=True)
    weight_ref[...] = to_column(2.5 * chosen / jnp.sum(squashed, axis=0, keepdims=True))


def far_groups(order, ep_count, chips):
    return [
        [(z * chips + x) * 2 + (side + x) % 2 for x in range(chips) for z in order(ep_count, x)]
        for side in range(2)
    ]


def columns_of(chip, own, features):
    core = lax.rem(lax.axis_index("core") + lax.axis_index("chip") + chip + (0 if own else 1), 2)
    return pl.ds(pl.multiple_of((2 * chip + core) * features, features), features)


def in_order(values, held, wanted):
    if held == wanted:
        return values
    blocks = [values[held.index(z) * CAP : (held.index(z) + 1) * CAP, :] for z in wanted]
    return jnp.concatenate(blocks, axis=0)


def lift(chips, own, rows_ref, gate_ref, up_ref):
    part_rows, features = rows_ref.shape[0] // chips, rows_ref.shape[1]
    ep_count = part_rows // CAP
    total = jnp.zeros((part_rows, 2 * gate_ref.shape[2]), jnp.float32)
    for chip in range(chips):
        rows = rows_ref[chip * part_rows : (chip + 1) * part_rows, :]
        columns = columns_of(chip, own, features)
        both = jnp.concatenate([gate_ref[0, columns, :], up_ref[0, columns, :]], axis=1)
        acts = jnp.dot(rows, both, preferred_element_type=jnp.float32)
        total += in_order(acts, first_order(ep_count, chip), first_order(ep_count, 0))
    return total


def lower(chips, own, hidden, down_ref, out_ref):
    part_rows, features = out_ref.shape[0] // chips, out_ref.shape[1]
    ep_count = part_rows // CAP
    for chip in range(chips):
        columns = columns_of(chip, own, features)
        values = jnp.dot(hidden, down_ref[0, :, columns], preferred_element_type=jnp.float32)
        values = in_order(values, first_order(ep_count, 0), second_order(ep_count, chip))
        out_ref[chip * part_rows : (chip + 1) * part_rows, :] = values.astype(jnp.bfloat16)


def begin(chips, rows_ref, gate_ref, up_ref, acts_ref):
    acts_ref[...] = lift(chips, True, rows_ref, gate_ref, up_ref)


def theirs(chips, rows_ref, acts_ref, gate_ref, up_ref, down_ref, hidden_ref, other_ref):
    width = gate_ref.shape[2]
    acts = acts_ref[...] + lift(chips, False, rows_ref, gate_ref, up_ref)
    gate_act, up_act = acts[:, :width], acts[:, width:]
    hidden = (gate_act / (1.0 + jnp.exp(-gate_act)) * up_act).astype(jnp.bfloat16)
    hidden_ref[...] = hidden
    lower(chips, False, hidden, down_ref, other_ref)


def ours(chips, hidden_ref, down_ref, mine_ref):
    lower(chips, True, hidden_ref[...], down_ref, mine_ref)


def add(mine_ref, other_ref, _, out_ref):
    total = mine_ref[...].astype(jnp.float32) + other_ref[...].astype(jnp.float32)
    out_ref[...] = total.astype(jnp.bfloat16)


def combine(match_ref, weight_ref, returned_ref, out_hbm, out_ref, sems):
    copies = []
    for part in range(out_ref.shape[0] // PIECE):
        rows = pl.ds(part * PIECE, PIECE)
        summed = jnp.dot(match_ref[rows, :], returned_ref[...], preferred_element_type=jnp.float32)
        out_ref[rows, :] = (weight_ref[rows, :] * summed).astype(jnp.bfloat16)
        copies.append(pltpu.make_async_copy(out_ref.at[rows, :], out_hbm.at[rows, :], sems.at[part]))
        copies[-1].start()
    for copy in copies:
        copy.wait()


def shards(tokens, expert_ids, route_scores, w_gate, w_up, w_down):
    row_count, features = tokens.shape
    top_count, hidden_count = expert_ids.shape[1], w_gate.shape[2]
    ep_count, chips = lax.axis_size("ep"), lax.axis_size("chip")
    slot_count = ep_count * CAP
    half = jax.ShapeDtypeStruct((chips * slot_count, features), jnp.bfloat16)
    ids, scores = expert_ids.T, route_scores.T
    hbm, vmem = (pl.BlockSpec(memory_space=space) for space in (pltpu.HBM, pltpu.VMEM))
    anywhere = pl.BlockSpec(memory_space=pl.ANY)

    def exchange(rows, order):
        groups = far_groups(order, ep_count, chips)
        return lax.all_to_all(rows, FAR, 0, 0, axis_index_groups=groups, tiled=True)

    def call(kernel, name, out_shape, **rest):
        return pl.pallas_call(kernel, out_shape=out_shape, name=name, compiler_params=LIMIT, **rest)

    outgoing = call(
        lambda *refs: route(ep_count, chips, *refs),
        "route",
        half,
        in_specs=[hbm] * 2,
        scratch_shapes=[
            pltpu.VMEM((top_count, row_count), jnp.int32),
            pltpu.VMEM((row_count, features), jnp.bfloat16),
            pltpu.SemaphoreType.DMA((row_count // FETCH + 1,)),
        ],
        cost_estimate=pl.CostEstimate(flops=2 * 10**9, bytes_accessed=0, transcendentals=0),
    )(*(pltpu.with_memory_space_constraint(value, pltpu.HBM) for value in (ids, tokens)))
    incoming = exchange(outgoing, first_order)
    across = lax.ppermute(incoming, "core", SWAP)
    acts = jax.ShapeDtypeStruct((slot_count, 2 * hidden_count), jnp.float32)
    begun = call(lambda *refs: begin(chips, *refs), "begin", acts)(incoming, w_gate, w_up)
    hidden_shape = jax.ShapeDtypeStruct((slot_count, hidden_count), jnp.bfloat16)
    hidden, other = call(lambda *refs: theirs(chips, *refs), "theirs", (hidden_shape, half))(
        across, begun, w_gate, w_up, w_down
    )
    crossed = lax.ppermute(other, "core", SWAP)
    mine = call(lambda *refs: ours(chips, *refs), "ours", half)(hidden, w_down)
    match, weight = call(
        lambda *refs: score(ep_count, chips, *refs),
        "score",
        (
            jax.ShapeDtypeStruct((row_count, chips * slot_count), jnp.bfloat16),
            jax.ShapeDtypeStruct((row_count, 1), jnp.float32),
        ),
        in_specs=[vmem] * 2 + [anywhere],
    )(ids, scores, other)
    summed = call(add, "add", half, in_specs=[vmem] * 2 + [anywhere])(mine, crossed, weight)
    returned = exchange(summed, second_order)
    return call(
        combine,
        "combine",
        jax.ShapeDtypeStruct((row_count, features), jnp.bfloat16),
        out_specs=hbm,
        scratch_shapes=[
            pltpu.VMEM((row_count, features), jnp.bfloat16),
            pltpu.SemaphoreType.DMA((row_count // PIECE,)),
        ],
    )(match, weight, returned)


def solution(mesh):
    groups, ep_count, tp_count = (mesh.shape[name] for name in ("groups", "ep", "tp"))
    split = jax.sharding.Mesh(
        mesh.devices.reshape(groups, ep_count, tp_count // 2, 2), ("groups", "ep", "chip", "core")
    )
    tp = ("chip", "core")
    placed = (
        P(("groups", "ep"), tp),
        P(("groups", "ep"), None),
        P(("groups", "ep"), None),
        P("ep", None, tp),
        P("ep", None, tp),
        P("ep", tp, None),
    )
    return jax.shard_map(
        shards, mesh=split, in_specs=placed, out_specs=P(("groups", "ep"), tp), check_vma=False
    )
```

```python
import jax
import jax.numpy as jnp
from jax import lax
from jax.experimental import pallas as pl
from jax.experimental.pallas import tpu as pltpu
from jax.sharding import PartitionSpec as P

CAP = 8
PIECE = 32
FETCH = 16
FIRST_MIRRORED = 1
SECOND_MIRRORED = 0
FAR = ("ep", "chip", "core")
SWAP = [(0, 1), (1, 0)]
LIMIT = pltpu.CompilerParams(vmem_limit_bytes=16 * 1024 * 1024)


def iota(shape, dim):
    return lax.broadcasted_iota(jnp.int32, shape, dim)


def to_column(row):
    size = row.shape[1]
    square = (size, size)
    return jnp.sum(jnp.where(iota(square, 0) == iota(square, 1), row, 0.0), axis=1, keepdims=True)


def slot_codes(ids, resident):
    row_count = ids.shape[1]
    expert = jnp.min(ids, axis=0, keepdims=True)
    onehot_shape = (-(-resident // 16) * 16, row_count)
    onehot = jnp.where(expert == iota(onehot_shape, 0).astype(jnp.float32), 1.0, 0.0)
    square = (row_count, row_count)
    earlier = jnp.where(iota(square, 0) < iota(square, 1), 1.0, 0.0).astype(jnp.bfloat16)
    counts = jnp.dot(onehot.astype(jnp.bfloat16), earlier, preferred_element_type=jnp.float32)
    return expert * CAP + jnp.sum(counts * onehot, axis=0, keepdims=True), expert


def first_order(ep_count, chip):
    listed = ((2, 3, 0, 1), (3, 2, 1, 0))[chip % 2]
    return [z // 4 * 4 + listed[z % 4] for z in range(ep_count)]


def second_order(ep_count, chip):
    listed = ((2, 1, 0, 3), (3, 2, 0, 1))[chip % 2]
    return [z // 4 * 4 + listed[z % 4] for z in range(ep_count)]


def row_codes(index, order, ep_count, chips):
    listed = [z for chip in range(chips) for z in order(ep_count, chip)]
    expert = sum(jnp.where(index // CAP == at, z // 2, 0) for at, z in enumerate(listed))
    return (expert * CAP + lax.rem(index, CAP)).astype(jnp.float32)


def route(ep_count, chips, ids_hbm, tokens_hbm, outgoing_ref, ids_ref, tokens_ref, sems):
    row_count = ids_ref.shape[1]
    parts = row_count // FETCH
    copies = [pltpu.make_async_copy(ids_hbm, ids_ref, sems.at[parts])] + [
        pltpu.make_async_copy(
            tokens_hbm.at[pl.ds(part * FETCH, FETCH), :],
            tokens_ref.at[pl.ds(part * FETCH, FETCH), :],
            sems.at[part],
        )
        for part in range(parts)
    ]
    for copy in copies:
        copy.start()
    wanted = row_codes(iota((outgoing_ref.shape[0], row_count), 0), first_order, ep_count, chips)
    copies[0].wait()
    code, _ = slot_codes(ids_ref[...].astype(jnp.float32), ep_count // 2)
    dispatch = jnp.where(code == wanted, 1.0, 0.0).astype(jnp.bfloat16)
    for copy in copies[1:]:
        copy.wait()
    outgoing_ref[...] = jnp.dot(
        dispatch, tokens_ref[...], preferred_element_type=jnp.float32
    ).astype(jnp.bfloat16)


def score(ep_count, chips, ids_ref, scores_ref, _, match_ref, weight_ref):
    ids = ids_ref[...].astype(jnp.float32)
    code, expert = slot_codes(ids, ep_count // 2)
    wanted = row_codes(iota(match_ref.shape, 1), second_order, ep_count, chips)
    match_ref[...] = jnp.where(to_column(code) == wanted, 1.0, 0.0).astype(jnp.bfloat16)
    squashed = jax.nn.sigmoid(scores_ref[...])
    chosen = jnp.sum(jnp.where(ids == expert, squashed, 0.0), axis=0, keepdims=True)
    weight_ref[...] = to_column(2.5 * chosen / jnp.sum(squashed, axis=0, keepdims=True))


def far_groups(order, mirrored, ep_count, chips):
    return [
        [
            (z * chips + x) * 2 + (side + x) % 2
            for block in range(chips)
            for x in [(block + side * mirrored) % chips]
            for z in order(ep_count, block)
        ]
        for side in range(2)
    ]


def columns_of(block, own, mirrored, features):
    side = lax.rem(lax.axis_index("core") + lax.axis_index("chip") + (0 if own else 1), 2)
    chip = lax.rem(block + side * mirrored, lax.axis_size("chip"))
    core = lax.rem(side + chip, 2)
    return pl.ds(pl.multiple_of((2 * chip + core) * features, features), features)


def in_order(values, held, wanted):
    if held == wanted:
        return values
    blocks = [values[held.index(z) * CAP : (held.index(z) + 1) * CAP, :] for z in wanted]
    return jnp.concatenate(blocks, axis=0)


def lift(chips, own, rows_ref, gate_ref, up_ref):
    part_rows, features = rows_ref.shape[0] // chips, rows_ref.shape[1]
    ep_count = part_rows // CAP
    total = jnp.zeros((part_rows, 2 * gate_ref.shape[2]), jnp.float32)
    for chip in range(chips):
        rows = rows_ref[chip * part_rows : (chip + 1) * part_rows, :]
        columns = columns_of(chip, own, FIRST_MIRRORED, features)
        both = jnp.concatenate([gate_ref[0, columns, :], up_ref[0, columns, :]], axis=1)
        acts = jnp.dot(rows, both, preferred_element_type=jnp.float32)
        total += in_order(acts, first_order(ep_count, chip), first_order(ep_count, 0))
    return total


def lower(chips, own, hidden, down_ref, out_ref):
    part_rows, features = out_ref.shape[0] // chips, out_ref.shape[1]
    ep_count = part_rows // CAP
    for chip in range(chips):
        columns = columns_of(chip, own, SECOND_MIRRORED, features)
        values = jnp.dot(hidden, down_ref[0, :, columns], preferred_element_type=jnp.float32)
        values = in_order(values, first_order(ep_count, 0), second_order(ep_count, chip))
        out_ref[chip * part_rows : (chip + 1) * part_rows, :] = values.astype(jnp.bfloat16)


def begin(chips, rows_ref, gate_ref, up_ref, acts_ref):
    acts_ref[...] = lift(chips, True, rows_ref, gate_ref, up_ref)


def theirs(chips, rows_ref, acts_ref, gate_ref, up_ref, down_ref, hidden_ref, other_ref):
    width = gate_ref.shape[2]
    acts = acts_ref[...] + lift(chips, False, rows_ref, gate_ref, up_ref)
    gate_act, up_act = acts[:, :width], acts[:, width:]
    hidden = (gate_act / (1.0 + jnp.exp(-gate_act)) * up_act).astype(jnp.bfloat16)
    hidden_ref[...] = hidden
    lower(chips, False, hidden, down_ref, other_ref)


def ours(chips, hidden_ref, down_ref, mine_ref):
    lower(chips, True, hidden_ref[...], down_ref, mine_ref)


def add(mine_ref, other_ref, _, out_ref):
    total = mine_ref[...].astype(jnp.float32) + other_ref[...].astype(jnp.float32)
    out_ref[...] = total.astype(jnp.bfloat16)


def combine(match_ref, weight_ref, returned_ref, out_hbm, out_ref, sems):
    copies = []
    for part in range(out_ref.shape[0] // PIECE):
        rows = pl.ds(part * PIECE, PIECE)
        summed = jnp.dot(match_ref[rows, :], returned_ref[...], preferred_element_type=jnp.float32)
        out_ref[rows, :] = (weight_ref[rows, :] * summed).astype(jnp.bfloat16)
        copies.append(pltpu.make_async_copy(out_ref.at[rows, :], out_hbm.at[rows, :], sems.at[part]))
        copies[-1].start()
    for copy in copies:
        copy.wait()


def shards(tokens, expert_ids, route_scores, w_gate, w_up, w_down):
    row_count, features = tokens.shape
    top_count, hidden_count = expert_ids.shape[1], w_gate.shape[2]
    ep_count, chips = lax.axis_size("ep"), lax.axis_size("chip")
    slot_count = ep_count * CAP
    half = jax.ShapeDtypeStruct((chips * slot_count, features), jnp.bfloat16)
    ids, scores = expert_ids.T, route_scores.T
    hbm, vmem = (pl.BlockSpec(memory_space=space) for space in (pltpu.HBM, pltpu.VMEM))
    anywhere = pl.BlockSpec(memory_space=pl.ANY)

    def exchange(rows, order, mirrored):
        groups = far_groups(order, mirrored, ep_count, chips)
        return lax.all_to_all(rows, FAR, 0, 0, axis_index_groups=groups, tiled=True)

    def call(kernel, name, out_shape, **rest):
        return pl.pallas_call(kernel, out_shape=out_shape, name=name, compiler_params=LIMIT, **rest)

    outgoing = call(
        lambda *refs: route(ep_count, chips, *refs),
        "route",
        half,
        in_specs=[hbm] * 2,
        scratch_shapes=[
            pltpu.VMEM((top_count, row_count), jnp.int32),
            pltpu.VMEM((row_count, features), jnp.bfloat16),
            pltpu.SemaphoreType.DMA((row_count // FETCH + 1,)),
        ],
        cost_estimate=pl.CostEstimate(flops=2 * 10**9, bytes_accessed=0, transcendentals=0),
    )(*(pltpu.with_memory_space_constraint(value, pltpu.HBM) for value in (ids, tokens)))
    incoming = exchange(outgoing, first_order, FIRST_MIRRORED)
    across = lax.ppermute(incoming, "core", SWAP)
    acts = jax.ShapeDtypeStruct((slot_count, 2 * hidden_count), jnp.float32)
    begun = call(lambda *refs: begin(chips, *refs), "begin", acts)(incoming, w_gate, w_up)
    hidden_shape = jax.ShapeDtypeStruct((slot_count, hidden_count), jnp.bfloat16)
    hidden, other = call(lambda *refs: theirs(chips, *refs), "theirs", (hidden_shape, half))(
        across, begun, w_gate, w_up, w_down
    )
    crossed = lax.ppermute(other, "core", SWAP)
    mine = call(lambda *refs: ours(chips, *refs), "ours", half)(hidden, w_down)
    match, weight = call(
        lambda *refs: score(ep_count, chips, *refs),
        "score",
        (
            jax.ShapeDtypeStruct((row_count, chips * slot_count), jnp.bfloat16),
            jax.ShapeDtypeStruct((row_count, 1), jnp.float32),
        ),
        in_specs=[vmem] * 2 + [anywhere],
    )(ids, scores, other)
    summed = call(add, "add", half, in_specs=[vmem] * 2 + [anywhere])(mine, crossed, weight)
    returned = exchange(summed, second_order, SECOND_MIRRORED)
    return call(
        combine,
        "combine",
        jax.ShapeDtypeStruct((row_count, features), jnp.bfloat16),
        out_specs=hbm,
        scratch_shapes=[
            pltpu.VMEM((row_count, features), jnp.bfloat16),
            pltpu.SemaphoreType.DMA((row_count // PIECE,)),
        ],
    )(match, weight, returned)


def solution(mesh):
    groups, ep_count, tp_count = (mesh.shape[name] for name in ("groups", "ep", "tp"))
    split = jax.sharding.Mesh(
        mesh.devices.reshape(groups, ep_count, tp_count // 2, 2), ("groups", "ep", "chip", "core")
    )
    tp = ("chip", "core")
    placed = (
        P(("groups", "ep"), tp),
        P(("groups", "ep"), None),
        P(("groups", "ep"), None),
        P("ep", None, tp),
        P("ep", None, tp),
        P("ep", tp, None),
    )
    return jax.shard_map(
        shards, mesh=split, in_specs=placed, out_specs=P(("groups", "ep"), tp), check_vma=False
    )
```

```python
import jax
import jax.numpy as jnp
from jax import lax
from jax.experimental import pallas as pl
from jax.experimental.pallas import tpu as pltpu
from jax.sharding import PartitionSpec as P

CAP = 8
PIECE = 32
FETCH = 16
FAR = ("ep", "chip", "core")
SWAP = [(0, 1), (1, 0)]
LIMIT = pltpu.CompilerParams(vmem_limit_bytes=16 * 1024 * 1024)


def iota(shape, dim):
    return lax.broadcasted_iota(jnp.int32, shape, dim)


def to_column(row):
    size = row.shape[1]
    square = (size, size)
    return jnp.sum(jnp.where(iota(square, 0) == iota(square, 1), row, 0.0), axis=1, keepdims=True)


def slot_codes(ids, resident):
    row_count = ids.shape[1]
    expert = jnp.min(ids, axis=0, keepdims=True)
    onehot_shape = (-(-resident // 16) * 16, row_count)
    onehot = jnp.where(expert == iota(onehot_shape, 0).astype(jnp.float32), 1.0, 0.0)
    square = (row_count, row_count)
    earlier = jnp.where(iota(square, 0) < iota(square, 1), 1.0, 0.0).astype(jnp.bfloat16)
    counts = jnp.dot(onehot.astype(jnp.bfloat16), earlier, preferred_element_type=jnp.float32)
    return expert * CAP + jnp.sum(counts * onehot, axis=0, keepdims=True), expert


def first_order(ep_count, chip):
    listed = ((2, 3, 1, 0), (3, 2, 1, 0))[chip % 2]
    return [z // 4 * 4 + listed[z % 4] for z in range(ep_count)]


def second_order(ep_count, chip):
    listed = ((2, 1, 0, 3), (3, 2, 1, 0))[chip % 2]
    return [z // 4 * 4 + listed[z % 4] for z in range(ep_count)]


def row_codes(index, order, ep_count, chips):
    listed = [z for chip in range(chips) for z in order(ep_count, chip)]
    expert = sum(jnp.where(index // CAP == at, z // 2, 0) for at, z in enumerate(listed))
    return (expert * CAP + lax.rem(index, CAP)).astype(jnp.float32)


def route(ep_count, chips, ids_hbm, tokens_hbm, outgoing_ref, ids_ref, tokens_ref, sems):
    row_count = ids_ref.shape[1]
    parts = row_count // FETCH
    copies = [pltpu.make_async_copy(ids_hbm, ids_ref, sems.at[parts])] + [
        pltpu.make_async_copy(
            tokens_hbm.at[pl.ds(part * FETCH, FETCH), :],
            tokens_ref.at[pl.ds(part * FETCH, FETCH), :],
            sems.at[part],
        )
        for part in range(parts)
    ]
    for copy in copies:
        copy.start()
    wanted = row_codes(iota((outgoing_ref.shape[0], row_count), 0), first_order, ep_count, chips)
    copies[0].wait()
    code, _ = slot_codes(ids_ref[...].astype(jnp.float32), ep_count // 2)
    dispatch = jnp.where(code == wanted, 1.0, 0.0).astype(jnp.bfloat16)
    for copy in copies[1:]:
        copy.wait()
    outgoing_ref[...] = jnp.dot(
        dispatch, tokens_ref[...], preferred_element_type=jnp.float32
    ).astype(jnp.bfloat16)


def score(ep_count, chips, ids_ref, scores_ref, _, match_ref, weight_ref):
    ids = ids_ref[...].astype(jnp.float32)
    code, expert = slot_codes(ids, ep_count // 2)
    wanted = row_codes(iota(match_ref.shape, 1), second_order, ep_count, chips)
    match_ref[...] = jnp.where(to_column(code) == wanted, 1.0, 0.0).astype(jnp.bfloat16)
    squashed = jax.nn.sigmoid(scores_ref[...])
    chosen = jnp.sum(jnp.where(ids == expert, squashed, 0.0), axis=0, keepdims=True)
    weight_ref[...] = to_column(2.5 * chosen / jnp.sum(squashed, axis=0, keepdims=True))


def far_groups(order, ep_count, chips):
    return [
        [(z * chips + x) * 2 + (side + x) % 2 for x in range(chips) for z in order(ep_count, x)]
        for side in range(2)
    ]


def columns_of(chip, own, features):
    core = lax.rem(lax.axis_index("core") + lax.axis_index("chip") + chip + (0 if own else 1), 2)
    return pl.ds(pl.multiple_of((2 * chip + core) * features, features), features)


def in_order(values, held, wanted):
    if held == wanted:
        return values
    blocks = [values[held.index(z) * CAP : (held.index(z) + 1) * CAP, :] for z in wanted]
    return jnp.concatenate(blocks, axis=0)


def lift(chips, own, rows_ref, gate_ref, up_ref):
    part_rows, features = rows_ref.shape[0] // chips, rows_ref.shape[1]
    ep_count = part_rows // CAP
    total = jnp.zeros((part_rows, 2 * gate_ref.shape[2]), jnp.float32)
    for chip in range(chips):
        rows = rows_ref[chip * part_rows : (chip + 1) * part_rows, :]
        columns = columns_of(chip, own, features)
        both = jnp.concatenate([gate_ref[0, columns, :], up_ref[0, columns, :]], axis=1)
        acts = jnp.dot(rows, both, preferred_element_type=jnp.float32)
        total += in_order(acts, first_order(ep_count, chip), first_order(ep_count, 0))
    return total


def lower(chips, own, hidden, down_ref, out_ref):
    part_rows, features = out_ref.shape[0] // chips, out_ref.shape[1]
    ep_count = part_rows // CAP
    for chip in range(chips):
        columns = columns_of(chip, own, features)
        values = jnp.dot(hidden, down_ref[0, :, columns], preferred_element_type=jnp.float32)
        values = in_order(values, first_order(ep_count, 0), second_order(ep_count, chip))
        out_ref[chip * part_rows : (chip + 1) * part_rows, :] = values.astype(jnp.bfloat16)


def begin(chips, rows_ref, gate_ref, up_ref, acts_ref):
    acts_ref[...] = lift(chips, True, rows_ref, gate_ref, up_ref)


def theirs(chips, rows_ref, acts_ref, gate_ref, up_ref, down_ref, hidden_ref, other_ref):
    width = gate_ref.shape[2]
    acts = acts_ref[...] + lift(chips, False, rows_ref, gate_ref, up_ref)
    gate_act, up_act = acts[:, :width], acts[:, width:]
    hidden = (gate_act / (1.0 + jnp.exp(-gate_act)) * up_act).astype(jnp.bfloat16)
    hidden_ref[...] = hidden
    lower(chips, False, hidden, down_ref, other_ref)


def ours(chips, hidden_ref, down_ref, mine_ref):
    lower(chips, True, hidden_ref[...], down_ref, mine_ref)


def add(mine_ref, other_ref, _, out_ref):
    total = mine_ref[...].astype(jnp.float32) + other_ref[...].astype(jnp.float32)
    out_ref[...] = total.astype(jnp.bfloat16)


def combine(match_ref, weight_ref, returned_ref, out_hbm, out_ref, sems):
    copies = []
    for part in range(out_ref.shape[0] // PIECE):
        rows = pl.ds(part * PIECE, PIECE)
        summed = jnp.dot(match_ref[rows, :], returned_ref[...], preferred_element_type=jnp.float32)
        out_ref[rows, :] = (weight_ref[rows, :] * summed).astype(jnp.bfloat16)
        copies.append(pltpu.make_async_copy(out_ref.at[rows, :], out_hbm.at[rows, :], sems.at[part]))
        copies[-1].start()
    for copy in copies:
        copy.wait()


def shards(tokens, expert_ids, route_scores, w_gate, w_up, w_down):
    row_count, features = tokens.shape
    top_count, hidden_count = expert_ids.shape[1], w_gate.shape[2]
    ep_count, chips = lax.axis_size("ep"), lax.axis_size("chip")
    slot_count = ep_count * CAP
    half = jax.ShapeDtypeStruct((chips * slot_count, features), jnp.bfloat16)
    ids, scores = expert_ids.T, route_scores.T
    hbm, vmem = (pl.BlockSpec(memory_space=space) for space in (pltpu.HBM, pltpu.VMEM))
    anywhere = pl.BlockSpec(memory_space=pl.ANY)

    def exchange(rows, order):
        groups = far_groups(order, ep_count, chips)
        return lax.all_to_all(rows, FAR, 0, 0, axis_index_groups=groups, tiled=True)

    def call(kernel, name, out_shape, **rest):
        return pl.pallas_call(kernel, out_shape=out_shape, name=name, compiler_params=LIMIT, **rest)

    outgoing = call(
        lambda *refs: route(ep_count, chips, *refs),
        "route",
        half,
        in_specs=[hbm] * 2,
        scratch_shapes=[
            pltpu.VMEM((top_count, row_count), jnp.int32),
            pltpu.VMEM((row_count, features), jnp.bfloat16),
            pltpu.SemaphoreType.DMA((row_count // FETCH + 1,)),
        ],
        cost_estimate=pl.CostEstimate(flops=2 * 10**9, bytes_accessed=0, transcendentals=0),
    )(*(pltpu.with_memory_space_constraint(value, pltpu.HBM) for value in (ids, tokens)))
    incoming = exchange(outgoing, first_order)
    across = lax.ppermute(incoming, "core", SWAP)
    acts = jax.ShapeDtypeStruct((slot_count, 2 * hidden_count), jnp.float32)
    begun = call(lambda *refs: begin(chips, *refs), "begin", acts)(incoming, w_gate, w_up)
    hidden_shape = jax.ShapeDtypeStruct((slot_count, hidden_count), jnp.bfloat16)
    hidden, other = call(lambda *refs: theirs(chips, *refs), "theirs", (hidden_shape, half))(
        across, begun, w_gate, w_up, w_down
    )
    crossed = lax.ppermute(other, "core", SWAP)
    mine = call(lambda *refs: ours(chips, *refs), "ours", half)(hidden, w_down)
    match, weight = call(
        lambda *refs: score(ep_count, chips, *refs),
        "score",
        (
            jax.ShapeDtypeStruct((row_count, chips * slot_count), jnp.bfloat16),
            jax.ShapeDtypeStruct((row_count, 1), jnp.float32),
        ),
        in_specs=[vmem] * 2 + [anywhere],
    )(ids, scores, other)
    summed = call(add, "add", half, in_specs=[vmem] * 2 + [anywhere])(mine, crossed, weight)
    returned = exchange(summed, second_order)
    return call(
        combine,
        "combine",
        jax.ShapeDtypeStruct((row_count, features), jnp.bfloat16),
        out_specs=hbm,
        scratch_shapes=[
            pltpu.VMEM((row_count, features), jnp.bfloat16),
            pltpu.SemaphoreType.DMA((row_count // PIECE,)),
        ],
    )(match, weight, returned)


def solution(mesh):
    groups, ep_count, tp_count = (mesh.shape[name] for name in ("groups", "ep", "tp"))
    split = jax.sharding.Mesh(
        mesh.devices.reshape(groups, ep_count, tp_count // 2, 2), ("groups", "ep", "chip", "core")
    )
    tp = ("chip", "core")
    placed = (
        P(("groups", "ep"), tp),
        P(("groups", "ep"), None),
        P(("groups", "ep"), None),
        P("ep", None, tp),
        P("ep", None, tp),
        P("ep", tp, None),
    )
    return jax.shard_map(
        shards, mesh=split, in_specs=placed, out_specs=P(("groups", "ep"), tp), check_vma=False
    )
```

```python
import jax
import jax.numpy as jnp
from jax import lax
from jax.experimental import pallas as pl
from jax.experimental.pallas import tpu as pltpu
from jax.sharding import PartitionSpec as P

CAP = 8
PIECE = 32
FETCH = 16
FAR = ("ep", "chip", "core")
SWAP = [(0, 1), (1, 0)]
LIMIT = pltpu.CompilerParams(vmem_limit_bytes=16 * 1024 * 1024)


def iota(shape, dim):
    return lax.broadcasted_iota(jnp.int32, shape, dim)


def to_column(row):
    size = row.shape[1]
    square = (size, size)
    return jnp.sum(jnp.where(iota(square, 0) == iota(square, 1), row, 0.0), axis=1, keepdims=True)


def slot_codes(ids, resident):
    row_count = ids.shape[1]
    expert = jnp.min(ids, axis=0, keepdims=True)
    onehot_shape = (-(-resident // 16) * 16, row_count)
    onehot = jnp.where(expert == iota(onehot_shape, 0).astype(jnp.float32), 1.0, 0.0)
    square = (row_count, row_count)
    earlier = jnp.where(iota(square, 0) < iota(square, 1), 1.0, 0.0).astype(jnp.bfloat16)
    counts = jnp.dot(onehot.astype(jnp.bfloat16), earlier, preferred_element_type=jnp.float32)
    return expert * CAP + jnp.sum(counts * onehot, axis=0, keepdims=True), expert


def first_members(ep_count, chips):
    return [(x, z) for z in range(ep_count) for x in range(chips)]


def second_order(ep_count, chip):
    listed = ((2, 1, 0, 3), (3, 2, 0, 1))[chip % 2]
    return [z // 4 * 4 + listed[z % 4] for z in range(ep_count)]


def second_members(ep_count, chips):
    return [(x, z) for x in range(chips) for z in second_order(ep_count, x)]


def row_codes(index, members, ep_count, chips):
    listed = members(ep_count, chips)
    expert = sum(jnp.where(index // CAP == at, z // 2, 0) for at, (_, z) in enumerate(listed))
    return (expert * CAP + lax.rem(index, CAP)).astype(jnp.float32)


def route(ep_count, chips, ids_hbm, tokens_hbm, outgoing_ref, ids_ref, tokens_ref, sems):
    row_count = ids_ref.shape[1]
    parts = row_count // FETCH
    copies = [pltpu.make_async_copy(ids_hbm, ids_ref, sems.at[parts])] + [
        pltpu.make_async_copy(
            tokens_hbm.at[pl.ds(part * FETCH, FETCH), :],
            tokens_ref.at[pl.ds(part * FETCH, FETCH), :],
            sems.at[part],
        )
        for part in range(parts)
    ]
    for copy in copies:
        copy.start()
    wanted = row_codes(iota((outgoing_ref.shape[0], row_count), 0), first_members, ep_count, chips)
    copies[0].wait()
    code, _ = slot_codes(ids_ref[...].astype(jnp.float32), ep_count // 2)
    dispatch = jnp.where(code == wanted, 1.0, 0.0).astype(jnp.bfloat16)
    for copy in copies[1:]:
        copy.wait()
    outgoing_ref[...] = jnp.dot(
        dispatch, tokens_ref[...], preferred_element_type=jnp.float32
    ).astype(jnp.bfloat16)


def score(ep_count, chips, ids_ref, scores_ref, _, match_ref, weight_ref):
    ids = ids_ref[...].astype(jnp.float32)
    code, expert = slot_codes(ids, ep_count // 2)
    wanted = row_codes(iota(match_ref.shape, 1), second_members, ep_count, chips)
    match_ref[...] = jnp.where(to_column(code) == wanted, 1.0, 0.0).astype(jnp.bfloat16)
    squashed = jax.nn.sigmoid(scores_ref[...])
    chosen = jnp.sum(jnp.where(ids == expert, squashed, 0.0), axis=0, keepdims=True)
    weight_ref[...] = to_column(2.5 * chosen / jnp.sum(squashed, axis=0, keepdims=True))


def far_groups(members, ep_count, chips):
    return [
        [(z * chips + x) * 2 + (side + x) % 2 for x, z in members(ep_count, chips)]
        for side in range(2)
    ]


def columns_of(chip, own, features):
    core = lax.rem(lax.axis_index("core") + lax.axis_index("chip") + chip + (0 if own else 1), 2)
    return pl.ds(pl.multiple_of((2 * chip + core) * features, features), features)


def in_order(values, held, wanted):
    if held == wanted:
        return values
    blocks = [values[held.index(z) * CAP : (held.index(z) + 1) * CAP, :] for z in wanted]
    return jnp.concatenate(blocks, axis=0)


def lift(chips, own, rows_ref, gate_ref, up_ref):
    rows, features = rows_ref[...], rows_ref.shape[1]
    ep_count = rows_ref.shape[0] // (CAP * chips)
    members = first_members(ep_count, chips)
    total = jnp.zeros((ep_count * CAP, 2 * gate_ref.shape[2]), jnp.float32)
    for chip in range(chips):
        columns = columns_of(chip, own, features)
        both = jnp.concatenate([gate_ref[0, columns, :], up_ref[0, columns, :]], axis=1)
        acts = jnp.dot(rows, both, preferred_element_type=jnp.float32)
        places = [members.index((chip, z)) * CAP for z in range(ep_count)]
        total += jnp.concatenate([acts[at : at + CAP, :] for at in places], axis=0)
    return total


def lower(chips, own, hidden, down_ref, out_ref):
    part_rows, features = out_ref.shape[0] // chips, out_ref.shape[1]
    ep_count = part_rows // CAP
    for chip in range(chips):
        columns = columns_of(chip, own, features)
        values = jnp.dot(hidden, down_ref[0, :, columns], preferred_element_type=jnp.float32)
        values = in_order(values, list(range(ep_count)), second_order(ep_count, chip))
        out_ref[chip * part_rows : (chip + 1) * part_rows, :] = values.astype(jnp.bfloat16)


def begin(chips, rows_ref, gate_ref, up_ref, acts_ref):
    acts_ref[...] = lift(chips, True, rows_ref, gate_ref, up_ref)


def theirs(chips, rows_ref, acts_ref, gate_ref, up_ref, down_ref, hidden_ref, other_ref):
    width = gate_ref.shape[2]
    acts = acts_ref[...] + lift(chips, False, rows_ref, gate_ref, up_ref)
    gate_act, up_act = acts[:, :width], acts[:, width:]
    hidden = (gate_act / (1.0 + jnp.exp(-gate_act)) * up_act).astype(jnp.bfloat16)
    hidden_ref[...] = hidden
    lower(chips, False, hidden, down_ref, other_ref)


def ours(chips, hidden_ref, down_ref, mine_ref):
    lower(chips, True, hidden_ref[...], down_ref, mine_ref)


def add(mine_ref, other_ref, _, out_ref):
    total = mine_ref[...].astype(jnp.float32) + other_ref[...].astype(jnp.float32)
    out_ref[...] = total.astype(jnp.bfloat16)


def combine(match_ref, weight_ref, returned_ref, out_hbm, out_ref, sems):
    copies = []
    for part in range(out_ref.shape[0] // PIECE):
        rows = pl.ds(part * PIECE, PIECE)
        summed = jnp.dot(match_ref[rows, :], returned_ref[...], preferred_element_type=jnp.float32)
        out_ref[rows, :] = (weight_ref[rows, :] * summed).astype(jnp.bfloat16)
        copies.append(pltpu.make_async_copy(out_ref.at[rows, :], out_hbm.at[rows, :], sems.at[part]))
        copies[-1].start()
    for copy in copies:
        copy.wait()


def shards(tokens, expert_ids, route_scores, w_gate, w_up, w_down):
    row_count, features = tokens.shape
    top_count, hidden_count = expert_ids.shape[1], w_gate.shape[2]
    ep_count, chips = lax.axis_size("ep"), lax.axis_size("chip")
    slot_count = ep_count * CAP
    half = jax.ShapeDtypeStruct((chips * slot_count, features), jnp.bfloat16)
    ids, scores = expert_ids.T, route_scores.T
    hbm, vmem = (pl.BlockSpec(memory_space=space) for space in (pltpu.HBM, pltpu.VMEM))
    anywhere = pl.BlockSpec(memory_space=pl.ANY)

    def exchange(rows, members):
        groups = far_groups(members, ep_count, chips)
        return lax.all_to_all(rows, FAR, 0, 0, axis_index_groups=groups, tiled=True)

    def call(kernel, name, out_shape, **rest):
        return pl.pallas_call(kernel, out_shape=out_shape, name=name, compiler_params=LIMIT, **rest)

    outgoing = call(
        lambda *refs: route(ep_count, chips, *refs),
        "route",
        half,
        in_specs=[hbm] * 2,
        scratch_shapes=[
            pltpu.VMEM((top_count, row_count), jnp.int32),
            pltpu.VMEM((row_count, features), jnp.bfloat16),
            pltpu.SemaphoreType.DMA((row_count // FETCH + 1,)),
        ],
        cost_estimate=pl.CostEstimate(flops=2 * 10**9, bytes_accessed=0, transcendentals=0),
    )(*(pltpu.with_memory_space_constraint(value, pltpu.HBM) for value in (ids, tokens)))
    incoming = exchange(outgoing, first_members)
    across = lax.ppermute(incoming, "core", SWAP)
    acts = jax.ShapeDtypeStruct((slot_count, 2 * hidden_count), jnp.float32)
    begun = call(lambda *refs: begin(chips, *refs), "begin", acts)(incoming, w_gate, w_up)
    hidden_shape = jax.ShapeDtypeStruct((slot_count, hidden_count), jnp.bfloat16)
    hidden, other = call(lambda *refs: theirs(chips, *refs), "theirs", (hidden_shape, half))(
        across, begun, w_gate, w_up, w_down
    )
    crossed = lax.ppermute(other, "core", SWAP)
    mine = call(lambda *refs: ours(chips, *refs), "ours", half)(hidden, w_down)
    match, weight = call(
        lambda *refs: score(ep_count, chips, *refs),
        "score",
        (
            jax.ShapeDtypeStruct((row_count, chips * slot_count), jnp.bfloat16),
            jax.ShapeDtypeStruct((row_count, 1), jnp.float32),
        ),
        in_specs=[vmem] * 2 + [anywhere],
    )(ids, scores, other)
    summed = call(add, "add", half, in_specs=[vmem] * 2 + [anywhere])(mine, crossed, weight)
    returned = exchange(summed, second_members)
    return call(
        combine,
        "combine",
        jax.ShapeDtypeStruct((row_count, features), jnp.bfloat16),
        out_specs=hbm,
        scratch_shapes=[
            pltpu.VMEM((row_count, features), jnp.bfloat16),
            pltpu.SemaphoreType.DMA((row_count // PIECE,)),
        ],
    )(match, weight, returned)


def solution(mesh):
    groups, ep_count, tp_count = (mesh.shape[name] for name in ("groups", "ep", "tp"))
    split = jax.sharding.Mesh(
        mesh.devices.reshape(groups, ep_count, tp_count // 2, 2), ("groups", "ep", "chip", "core")
    )
    tp = ("chip", "core")
    placed = (
        P(("groups", "ep"), tp),
        P(("groups", "ep"), None),
        P(("groups", "ep"), None),
        P("ep", None, tp),
        P("ep", None, tp),
        P("ep", tp, None),
    )
    return jax.shard_map(
        shards, mesh=split, in_specs=placed, out_specs=P(("groups", "ep"), tp), check_vma=False
    )
```

```python
import jax
import jax.numpy as jnp
from jax import lax
from jax.experimental import pallas as pl
from jax.experimental.pallas import tpu as pltpu
from jax.sharding import PartitionSpec as P

CAP = 8
PIECE = 32
FETCH = 16
FAR = ("ep", "chip", "core")
SWAP = [(0, 1), (1, 0)]
LIMIT = pltpu.CompilerParams(vmem_limit_bytes=16 * 1024 * 1024)


def iota(shape, dim):
    return lax.broadcasted_iota(jnp.int32, shape, dim)


def to_column(row):
    size = row.shape[1]
    square = (size, size)
    return jnp.sum(jnp.where(iota(square, 0) == iota(square, 1), row, 0.0), axis=1, keepdims=True)


def slot_codes(ids, resident):
    row_count = ids.shape[1]
    expert = jnp.min(ids, axis=0, keepdims=True)
    onehot_shape = (-(-resident // 16) * 16, row_count)
    onehot = jnp.where(expert == iota(onehot_shape, 0).astype(jnp.float32), 1.0, 0.0)
    square = (row_count, row_count)
    earlier = jnp.where(iota(square, 0) < iota(square, 1), 1.0, 0.0).astype(jnp.bfloat16)
    counts = jnp.dot(onehot.astype(jnp.bfloat16), earlier, preferred_element_type=jnp.float32)
    return expert * CAP + jnp.sum(counts * onehot, axis=0, keepdims=True), expert


def first_order(ep_count, chip):
    listed = ((2, 3, 0, 1), (1, 0, 3, 2))[chip % 2]
    return [z // 4 * 4 + listed[z % 4] for z in range(ep_count)]


def second_order(ep_count, chip):
    listed = ((2, 1, 0, 3), (3, 2, 0, 1))[chip % 2]
    return [z // 4 * 4 + listed[z % 4] for z in range(ep_count)]


def row_codes(index, order, ep_count, chips):
    listed = [z for chip in range(chips) for z in order(ep_count, chip)]
    expert = sum(jnp.where(index // CAP == at, z // 2, 0) for at, z in enumerate(listed))
    return (expert * CAP + lax.rem(index, CAP)).astype(jnp.float32)


def route(ep_count, chips, ids_hbm, tokens_hbm, outgoing_ref, ids_ref, tokens_ref, sems):
    row_count = ids_ref.shape[1]
    parts = row_count // FETCH
    copies = [pltpu.make_async_copy(ids_hbm, ids_ref, sems.at[parts])] + [
        pltpu.make_async_copy(
            tokens_hbm.at[pl.ds(part * FETCH, FETCH), :],
            tokens_ref.at[pl.ds(part * FETCH, FETCH), :],
            sems.at[part],
        )
        for part in range(parts)
    ]
    for copy in copies:
        copy.start()
    wanted = row_codes(iota((outgoing_ref.shape[0], row_count), 0), first_order, ep_count, chips)
    copies[0].wait()
    code, _ = slot_codes(ids_ref[...].astype(jnp.float32), ep_count // 2)
    dispatch = jnp.where(code == wanted, 1.0, 0.0).astype(jnp.bfloat16)
    for copy in copies[1:]:
        copy.wait()
    outgoing_ref[...] = jnp.dot(
        dispatch, tokens_ref[...], preferred_element_type=jnp.float32
    ).astype(jnp.bfloat16)


def score(ep_count, chips, ids_ref, scores_ref, _, match_ref, weight_ref):
    ids = ids_ref[...].astype(jnp.float32)
    code, expert = slot_codes(ids, ep_count // 2)
    wanted = row_codes(iota(match_ref.shape, 1), second_order, ep_count, chips)
    match_ref[...] = jnp.where(to_column(code) == wanted, 1.0, 0.0).astype(jnp.bfloat16)
    squashed = jax.nn.sigmoid(scores_ref[...])
    chosen = jnp.sum(jnp.where(ids == expert, squashed, 0.0), axis=0, keepdims=True)
    weight_ref[...] = to_column(2.5 * chosen / jnp.sum(squashed, axis=0, keepdims=True))


def far_groups(order, ep_count, chips):
    return [
        [(z * chips + x) * 2 + (side + x) % 2 for x in range(chips) for z in order(ep_count, x)]
        for side in range(2)
    ]


def columns_of(chip, own, features):
    core = lax.rem(lax.axis_index("core") + lax.axis_index("chip") + chip + (0 if own else 1), 2)
    return pl.ds(pl.multiple_of((2 * chip + core) * features, features), features)


def in_order(values, held, wanted):
    if held == wanted:
        return values
    blocks = [values[held.index(z) * CAP : (held.index(z) + 1) * CAP, :] for z in wanted]
    return jnp.concatenate(blocks, axis=0)


def lift(chips, own, rows_ref, gate_ref, up_ref):
    part_rows, features = rows_ref.shape[0] // chips, rows_ref.shape[1]
    ep_count = part_rows // CAP
    total = jnp.zeros((part_rows, 2 * gate_ref.shape[2]), jnp.float32)
    for chip in range(chips):
        rows = rows_ref[chip * part_rows : (chip + 1) * part_rows, :]
        columns = columns_of(chip, own, features)
        both = jnp.concatenate([gate_ref[0, columns, :], up_ref[0, columns, :]], axis=1)
        acts = jnp.dot(rows, both, preferred_element_type=jnp.float32)
        total += in_order(acts, first_order(ep_count, chip), first_order(ep_count, 0))
    return total


def lower(chips, own, hidden, down_ref, out_ref):
    part_rows, features = out_ref.shape[0] // chips, out_ref.shape[1]
    ep_count = part_rows // CAP
    for chip in range(chips):
        columns = columns_of(chip, own, features)
        values = jnp.dot(hidden, down_ref[0, :, columns], preferred_element_type=jnp.float32)
        values = in_order(values, first_order(ep_count, 0), second_order(ep_count, chip))
        out_ref[chip * part_rows : (chip + 1) * part_rows, :] = values.astype(jnp.bfloat16)


def begin(chips, rows_ref, gate_ref, up_ref, acts_ref):
    acts_ref[...] = lift(chips, True, rows_ref, gate_ref, up_ref)


def theirs(chips, rows_ref, acts_ref, gate_ref, up_ref, down_ref, hidden_ref, other_ref):
    width = gate_ref.shape[2]
    acts = acts_ref[...] + lift(chips, False, rows_ref, gate_ref, up_ref)
    gate_act, up_act = acts[:, :width], acts[:, width:]
    hidden = (gate_act / (1.0 + jnp.exp(-gate_act)) * up_act).astype(jnp.bfloat16)
    hidden_ref[...] = hidden
    lower(chips, False, hidden, down_ref, other_ref)


def ours(chips, hidden_ref, down_ref, mine_ref):
    lower(chips, True, hidden_ref[...], down_ref, mine_ref)


def add(mine_ref, other_ref, _, out_ref):
    total = mine_ref[...].astype(jnp.float32) + other_ref[...].astype(jnp.float32)
    out_ref[...] = total.astype(jnp.bfloat16)


def combine(match_ref, weight_ref, returned_ref, out_hbm, out_ref, sems):
    copies = []
    for part in range(out_ref.shape[0] // PIECE):
        rows = pl.ds(part * PIECE, PIECE)
        summed = jnp.dot(match_ref[rows, :], returned_ref[...], preferred_element_type=jnp.float32)
        out_ref[rows, :] = (weight_ref[rows, :] * summed).astype(jnp.bfloat16)
        copies.append(pltpu.make_async_copy(out_ref.at[rows, :], out_hbm.at[rows, :], sems.at[part]))
        copies[-1].start()
    for copy in copies:
        copy.wait()


def shards(tokens, expert_ids, route_scores, w_gate, w_up, w_down):
    row_count, features = tokens.shape
    top_count, hidden_count = expert_ids.shape[1], w_gate.shape[2]
    ep_count, chips = lax.axis_size("ep"), lax.axis_size("chip")
    slot_count = ep_count * CAP
    half = jax.ShapeDtypeStruct((chips * slot_count, features), jnp.bfloat16)
    ids, scores = expert_ids.T, route_scores.T
    hbm, vmem = (pl.BlockSpec(memory_space=space) for space in (pltpu.HBM, pltpu.VMEM))
    anywhere = pl.BlockSpec(memory_space=pl.ANY)

    def exchange(rows, order):
        groups = far_groups(order, ep_count, chips)
        return lax.all_to_all(rows, FAR, 0, 0, axis_index_groups=groups, tiled=True)

    def call(kernel, name, out_shape, **rest):
        return pl.pallas_call(kernel, out_shape=out_shape, name=name, compiler_params=LIMIT, **rest)

    outgoing = call(
        lambda *refs: route(ep_count, chips, *refs),
        "route",
        half,
        in_specs=[hbm] * 2,
        scratch_shapes=[
            pltpu.VMEM((top_count, row_count), jnp.int32),
            pltpu.VMEM((row_count, features), jnp.bfloat16),
            pltpu.SemaphoreType.DMA((row_count // FETCH + 1,)),
        ],
        cost_estimate=pl.CostEstimate(flops=2 * 10**9, bytes_accessed=0, transcendentals=0),
    )(*(pltpu.with_memory_space_constraint(value, pltpu.HBM) for value in (ids, tokens)))
    incoming = exchange(outgoing, first_order)
    across = lax.ppermute(incoming, "core", SWAP)
    acts = jax.ShapeDtypeStruct((slot_count, 2 * hidden_count), jnp.float32)
    begun = call(lambda *refs: begin(chips, *refs), "begin", acts)(incoming, w_gate, w_up)
    hidden_shape = jax.ShapeDtypeStruct((slot_count, hidden_count), jnp.bfloat16)
    hidden, other = call(lambda *refs: theirs(chips, *refs), "theirs", (hidden_shape, half))(
        across, begun, w_gate, w_up, w_down
    )
    crossed = lax.ppermute(other, "core", SWAP)
    mine = call(lambda *refs: ours(chips, *refs), "ours", half)(hidden, w_down)
    match, weight = call(
        lambda *refs: score(ep_count, chips, *refs),
        "score",
        (
            jax.ShapeDtypeStruct((row_count, chips * slot_count), jnp.bfloat16),
            jax.ShapeDtypeStruct((row_count, 1), jnp.float32),
        ),
        in_specs=[vmem] * 2 + [anywhere],
    )(ids, scores, other)
    summed = call(add, "add", half, in_specs=[vmem] * 2 + [anywhere])(mine, crossed, weight)
    returned = exchange(summed, second_order)
    return call(
        combine,
        "combine",
        jax.ShapeDtypeStruct((row_count, features), jnp.bfloat16),
        out_specs=hbm,
        scratch_shapes=[
            pltpu.VMEM((row_count, features), jnp.bfloat16),
            pltpu.SemaphoreType.DMA((row_count // PIECE,)),
        ],
    )(match, weight, returned)


def solution(mesh):
    groups, ep_count, tp_count = (mesh.shape[name] for name in ("groups", "ep", "tp"))
    split = jax.sharding.Mesh(
        mesh.devices.reshape(groups, ep_count, tp_count // 2, 2), ("groups", "ep", "chip", "core")
    )
    tp = ("chip", "core")
    placed = (
        P(("groups", "ep"), tp),
        P(("groups", "ep"), None),
        P(("groups", "ep"), None),
        P("ep", None, tp),
        P("ep", None, tp),
        P("ep", tp, None),
    )
    return jax.shard_map(
        shards, mesh=split, in_specs=placed, out_specs=P(("groups", "ep"), tp), check_vma=False
    )
```

```python
import jax
import jax.numpy as jnp
from jax import lax
from jax.experimental import pallas as pl
from jax.experimental.pallas import tpu as pltpu
from jax.sharding import PartitionSpec as P

CAP = 8
PIECE = 32
FETCH = 16
FAR = ("ep", "chip", "core")
SWAP = [(0, 1), (1, 0)]
LIMIT = pltpu.CompilerParams(vmem_limit_bytes=16 * 1024 * 1024)


def iota(shape, dim):
    return lax.broadcasted_iota(jnp.int32, shape, dim)


def to_column(row):
    size = row.shape[1]
    square = (size, size)
    return jnp.sum(jnp.where(iota(square, 0) == iota(square, 1), row, 0.0), axis=1, keepdims=True)


def slot_codes(ids, resident):
    row_count = ids.shape[1]
    expert = jnp.min(ids, axis=0, keepdims=True)
    onehot_shape = (-(-resident // 16) * 16, row_count)
    onehot = jnp.where(expert == iota(onehot_shape, 0).astype(jnp.float32), 1.0, 0.0)
    square = (row_count, row_count)
    earlier = jnp.where(iota(square, 0) < iota(square, 1), 1.0, 0.0).astype(jnp.bfloat16)
    counts = jnp.dot(onehot.astype(jnp.bfloat16), earlier, preferred_element_type=jnp.float32)
    return expert * CAP + jnp.sum(counts * onehot, axis=0, keepdims=True), expert


def first_order(ep_count, chip):
    listed = ((2, 3, 0, 1), (2, 3, 0, 1))[chip % 2]
    return [z // 4 * 4 + listed[z % 4] for z in range(ep_count)]


def second_order(ep_count, chip):
    listed = ((2, 1, 0, 3), (3, 2, 0, 1))[chip % 2]
    return [z // 4 * 4 + listed[z % 4] for z in range(ep_count)]


def row_codes(index, order, ep_count, chips):
    listed = [z for chip in range(chips) for z in order(ep_count, chip)]
    expert = sum(jnp.where(index // CAP == at, z // 2, 0) for at, z in enumerate(listed))
    return (expert * CAP + lax.rem(index, CAP)).astype(jnp.float32)


def route(ep_count, chips, ids_hbm, tokens_hbm, outgoing_ref, ids_ref, tokens_ref, sems):
    row_count = ids_ref.shape[1]
    parts = row_count // FETCH
    copies = [pltpu.make_async_copy(ids_hbm, ids_ref, sems.at[parts])] + [
        pltpu.make_async_copy(
            tokens_hbm.at[pl.ds(part * FETCH, FETCH), :],
            tokens_ref.at[pl.ds(part * FETCH, FETCH), :],
            sems.at[part],
        )
        for part in range(parts)
    ]
    for copy in copies:
        copy.start()
    wanted = row_codes(iota((outgoing_ref.shape[0], row_count), 0), first_order, ep_count, chips)
    copies[0].wait()
    code, _ = slot_codes(ids_ref[...].astype(jnp.float32), ep_count // 2)
    dispatch = jnp.where(code == wanted, 1.0, 0.0).astype(jnp.bfloat16)
    for copy in copies[1:]:
        copy.wait()
    outgoing_ref[...] = jnp.dot(
        dispatch, tokens_ref[...], preferred_element_type=jnp.float32
    ).astype(jnp.bfloat16)


def score(ep_count, chips, ids_ref, scores_ref, _, match_ref, weight_ref):
    ids = ids_ref[...].astype(jnp.float32)
    code, expert = slot_codes(ids, ep_count // 2)
    wanted = row_codes(iota(match_ref.shape, 1), second_order, ep_count, chips)
    match_ref[...] = jnp.where(to_column(code) == wanted, 1.0, 0.0).astype(jnp.bfloat16)
    squashed = jax.nn.sigmoid(scores_ref[...])
    chosen = jnp.sum(jnp.where(ids == expert, squashed, 0.0), axis=0, keepdims=True)
    weight_ref[...] = to_column(2.5 * chosen / jnp.sum(squashed, axis=0, keepdims=True))


def far_groups(order, ep_count, chips):
    return [
        [(z * chips + x) * 2 + (side + x) % 2 for x in range(chips) for z in order(ep_count, x)]
        for side in range(2)
    ]


def columns_of(chip, own, features):
    core = lax.rem(lax.axis_index("core") + lax.axis_index("chip") + chip + (0 if own else 1), 2)
    return pl.ds(pl.multiple_of((2 * chip + core) * features, features), features)


def in_order(values, held, wanted):
    if held == wanted:
        return values
    blocks = [values[held.index(z) * CAP : (held.index(z) + 1) * CAP, :] for z in wanted]
    return jnp.concatenate(blocks, axis=0)


def lift(chips, own, rows_ref, gate_ref, up_ref):
    part_rows, features = rows_ref.shape[0] // chips, rows_ref.shape[1]
    ep_count = part_rows // CAP
    total = jnp.zeros((part_rows, 2 * gate_ref.shape[2]), jnp.float32)
    for chip in range(chips):
        rows = rows_ref[chip * part_rows : (chip + 1) * part_rows, :]
        columns = columns_of(chip, own, features)
        both = jnp.concatenate([gate_ref[0, columns, :], up_ref[0, columns, :]], axis=1)
        acts = jnp.dot(rows, both, preferred_element_type=jnp.float32)
        total += in_order(acts, first_order(ep_count, chip), first_order(ep_count, 0))
    return total


def lower(chips, own, hidden, down_ref, out_ref):
    part_rows, features = out_ref.shape[0] // chips, out_ref.shape[1]
    ep_count = part_rows // CAP
    for chip in range(chips):
        columns = columns_of(chip, own, features)
        values = jnp.dot(hidden, down_ref[0, :, columns], preferred_element_type=jnp.float32)
        values = in_order(values, first_order(ep_count, 0), second_order(ep_count, chip))
        out_ref[chip * part_rows : (chip + 1) * part_rows, :] = values.astype(jnp.bfloat16)


def begin(chips, rows_ref, gate_ref, up_ref, acts_ref):
    acts_ref[...] = lift(chips, True, rows_ref, gate_ref, up_ref)


def theirs(chips, rows_ref, acts_ref, gate_ref, up_ref, down_ref, hidden_ref, other_ref):
    width = gate_ref.shape[2]
    acts = acts_ref[...] + lift(chips, False, rows_ref, gate_ref, up_ref)
    gate_act, up_act = acts[:, :width], acts[:, width:]
    hidden = (gate_act / (1.0 + jnp.exp(-gate_act)) * up_act).astype(jnp.bfloat16)
    hidden_ref[...] = hidden
    lower(chips, False, hidden, down_ref, other_ref)


def ours(chips, hidden_ref, down_ref, mine_ref):
    lower(chips, True, hidden_ref[...], down_ref, mine_ref)


def add(mine_ref, other_ref, _, out_ref):
    total = mine_ref[...].astype(jnp.float32) + other_ref[...].astype(jnp.float32)
    out_ref[...] = total.astype(jnp.bfloat16)


def combine(match_ref, weight_ref, returned_ref, out_hbm, out_ref, sems):
    copies = []
    for part in range(out_ref.shape[0] // PIECE):
        rows = pl.ds(part * PIECE, PIECE)
        summed = jnp.dot(match_ref[rows, :], returned_ref[...], preferred_element_type=jnp.float32)
        out_ref[rows, :] = (weight_ref[rows, :] * summed).astype(jnp.bfloat16)
        copies.append(pltpu.make_async_copy(out_ref.at[rows, :], out_hbm.at[rows, :], sems.at[part]))
        copies[-1].start()
    for copy in copies:
        copy.wait()


def shards(tokens, expert_ids, route_scores, w_gate, w_up, w_down):
    row_count, features = tokens.shape
    top_count, hidden_count = expert_ids.shape[1], w_gate.shape[2]
    ep_count, chips = lax.axis_size("ep"), lax.axis_size("chip")
    slot_count = ep_count * CAP
    half = jax.ShapeDtypeStruct((chips * slot_count, features), jnp.bfloat16)
    ids, scores = expert_ids.T, route_scores.T
    hbm, vmem = (pl.BlockSpec(memory_space=space) for space in (pltpu.HBM, pltpu.VMEM))
    anywhere = pl.BlockSpec(memory_space=pl.ANY)

    def exchange(rows, order):
        groups = far_groups(order, ep_count, chips)
        return lax.all_to_all(rows, FAR, 0, 0, axis_index_groups=groups, tiled=True)

    def call(kernel, name, out_shape, **rest):
        return pl.pallas_call(kernel, out_shape=out_shape, name=name, compiler_params=LIMIT, **rest)

    outgoing = call(
        lambda *refs: route(ep_count, chips, *refs),
        "route",
        half,
        in_specs=[hbm] * 2,
        scratch_shapes=[
            pltpu.VMEM((top_count, row_count), jnp.int32),
            pltpu.VMEM((row_count, features), jnp.bfloat16),
            pltpu.SemaphoreType.DMA((row_count // FETCH + 1,)),
        ],
        cost_estimate=pl.CostEstimate(flops=2 * 10**9, bytes_accessed=0, transcendentals=0),
    )(*(pltpu.with_memory_space_constraint(value, pltpu.HBM) for value in (ids, tokens)))
    incoming = exchange(outgoing, first_order)
    across = lax.ppermute(incoming, "core", SWAP)
    acts = jax.ShapeDtypeStruct((slot_count, 2 * hidden_count), jnp.float32)
    begun = call(lambda *refs: begin(chips, *refs), "begin", acts)(incoming, w_gate, w_up)
    hidden_shape = jax.ShapeDtypeStruct((slot_count, hidden_count), jnp.bfloat16)
    hidden, other = call(lambda *refs: theirs(chips, *refs), "theirs", (hidden_shape, half))(
        across, begun, w_gate, w_up, w_down
    )
    crossed = lax.ppermute(other, "core", SWAP)
    mine = call(lambda *refs: ours(chips, *refs), "ours", half)(hidden, w_down)
    match, weight = call(
        lambda *refs: score(ep_count, chips, *refs),
        "score",
        (
            jax.ShapeDtypeStruct((row_count, chips * slot_count), jnp.bfloat16),
            jax.ShapeDtypeStruct((row_count, 1), jnp.float32),
        ),
        in_specs=[vmem] * 2 + [anywhere],
    )(ids, scores, other)
    summed = call(add, "add", half, in_specs=[vmem] * 2 + [anywhere])(mine, crossed, weight)
    returned = exchange(summed, second_order)
    return call(
        combine,
        "combine",
        jax.ShapeDtypeStruct((row_count, features), jnp.bfloat16),
        out_specs=hbm,
        scratch_shapes=[
            pltpu.VMEM((row_count, features), jnp.bfloat16),
            pltpu.SemaphoreType.DMA((row_count // PIECE,)),
        ],
    )(match, weight, returned)


def solution(mesh):
    groups, ep_count, tp_count = (mesh.shape[name] for name in ("groups", "ep", "tp"))
    split = jax.sharding.Mesh(
        mesh.devices.reshape(groups, ep_count, tp_count // 2, 2), ("groups", "ep", "chip", "core")
    )
    tp = ("chip", "core")
    placed = (
        P(("groups", "ep"), tp),
        P(("groups", "ep"), None),
        P(("groups", "ep"), None),
        P("ep", None, tp),
        P("ep", None, tp),
        P("ep", tp, None),
    )
    return jax.shard_map(
        shards, mesh=split, in_specs=placed, out_specs=P(("groups", "ep"), tp), check_vma=False
    )
```

```python
import jax
import jax.numpy as jnp
from jax import lax
from jax.experimental import pallas as pl
from jax.experimental.pallas import tpu as pltpu
from jax.sharding import PartitionSpec as P

CAP = 8
PIECE = 32
FAR = ("ep", "chip", "core")
SWAP = [(0, 1), (1, 0)]
LIMIT = pltpu.CompilerParams(vmem_limit_bytes=16 * 1024 * 1024)


def iota(shape, dim):
    return lax.broadcasted_iota(jnp.int32, shape, dim)


def to_column(row):
    size = row.shape[1]
    square = (size, size)
    return jnp.sum(jnp.where(iota(square, 0) == iota(square, 1), row, 0.0), axis=1, keepdims=True)


def slot_codes(ids, resident):
    row_count = ids.shape[1]
    expert = jnp.min(ids, axis=0, keepdims=True)
    onehot_shape = (-(-resident // 16) * 16, row_count)
    onehot = jnp.where(expert == iota(onehot_shape, 0).astype(jnp.float32), 1.0, 0.0)
    square = (row_count, row_count)
    earlier = jnp.where(iota(square, 0) < iota(square, 1), 1.0, 0.0).astype(jnp.bfloat16)
    counts = jnp.dot(onehot.astype(jnp.bfloat16), earlier, preferred_element_type=jnp.float32)
    return expert * CAP + jnp.sum(counts * onehot, axis=0, keepdims=True), expert


def first_order(ep_count, chip):
    listed = ((2, 3, 0, 1), (3, 2, 1, 0))[chip % 2]
    return [z // 4 * 4 + listed[z % 4] for z in range(ep_count)]


def second_order(ep_count, chip):
    listed = ((2, 1, 0, 3), (3, 2, 1, 0))[chip % 2]
    return [z // 4 * 4 + listed[z % 4] for z in range(ep_count)]


def row_codes(index, order, ep_count, chips):
    listed = [z for chip in range(chips) for z in order(ep_count, chip)]
    expert = sum(jnp.where(index // CAP == at, z // 2, 0) for at, z in enumerate(listed))
    return (expert * CAP + lax.rem(index, CAP)).astype(jnp.float32)


def route(ep_count, chips, ids_hbm, tokens_hbm, outgoing_ref, ids_ref, tokens_ref, sems):
    row_count = ids_ref.shape[1]
    parts = row_count // PIECE
    copies = [pltpu.make_async_copy(ids_hbm, ids_ref, sems.at[parts])] + [
        pltpu.make_async_copy(
            tokens_hbm.at[pl.ds(part * PIECE, PIECE), :],
            tokens_ref.at[pl.ds(part * PIECE, PIECE), :],
            sems.at[part],
        )
        for part in range(parts)
    ]
    for copy in copies:
        copy.start()
    wanted = row_codes(iota((outgoing_ref.shape[0], row_count), 0), first_order, ep_count, chips)
    copies[0].wait()
    code, _ = slot_codes(ids_ref[...].astype(jnp.float32), ep_count // 2)
    dispatch = jnp.where(code == wanted, 1.0, 0.0).astype(jnp.bfloat16)
    for copy in copies[1:]:
        copy.wait()
    outgoing_ref[...] = jnp.dot(
        dispatch, tokens_ref[...], preferred_element_type=jnp.float32
    ).astype(jnp.bfloat16)


def score(ep_count, chips, ids_ref, scores_ref, _, match_ref, weight_ref):
    ids = ids_ref[...].astype(jnp.float32)
    code, expert = slot_codes(ids, ep_count // 2)
    wanted = row_codes(iota(match_ref.shape, 1), second_order, ep_count, chips)
    match_ref[...] = jnp.where(to_column(code) == wanted, 1.0, 0.0).astype(jnp.bfloat16)
    squashed = jax.nn.sigmoid(scores_ref[...])
    chosen = jnp.sum(jnp.where(ids == expert, squashed, 0.0), axis=0, keepdims=True)
    weight_ref[...] = to_column(2.5 * chosen / jnp.sum(squashed, axis=0, keepdims=True))


def far_groups(order, ep_count, chips):
    return [
        [(z * chips + x) * 2 + (side + x) % 2 for x in range(chips) for z in order(ep_count, x)]
        for side in range(2)
    ]


def columns_of(chip, own, features):
    core = lax.rem(lax.axis_index("core") + lax.axis_index("chip") + chip + (0 if own else 1), 2)
    return pl.ds(pl.multiple_of((2 * chip + core) * features, features), features)


def in_order(values, held, wanted):
    if held == wanted:
        return values
    blocks = [values[held.index(z) * CAP : (held.index(z) + 1) * CAP, :] for z in wanted]
    return jnp.concatenate(blocks, axis=0)


def lift(chips, own, rows_ref, gate_ref, up_ref):
    part_rows, features = rows_ref.shape[0] // chips, rows_ref.shape[1]
    ep_count = part_rows // CAP
    total = jnp.zeros((part_rows, 2 * gate_ref.shape[2]), jnp.float32)
    for chip in range(chips):
        rows = rows_ref[chip * part_rows : (chip + 1) * part_rows, :]
        columns = columns_of(chip, own, features)
        both = jnp.concatenate([gate_ref[0, columns, :], up_ref[0, columns, :]], axis=1)
        acts = jnp.dot(rows, both, preferred_element_type=jnp.float32)
        total += in_order(acts, first_order(ep_count, chip), first_order(ep_count, 0))
    return total


def lower(chips, own, hidden, down_ref, out_ref):
    part_rows, features = out_ref.shape[0] // chips, out_ref.shape[1]
    ep_count = part_rows // CAP
    for chip in range(chips):
        columns = columns_of(chip, own, features)
        values = jnp.dot(hidden, down_ref[0, :, columns], preferred_element_type=jnp.float32)
        values = in_order(values, first_order(ep_count, 0), second_order(ep_count, chip))
        out_ref[chip * part_rows : (chip + 1) * part_rows, :] = values.astype(jnp.bfloat16)


def begin(chips, rows_ref, gate_ref, up_ref, acts_ref):
    acts_ref[...] = lift(chips, True, rows_ref, gate_ref, up_ref)


def theirs(chips, rows_ref, acts_ref, gate_ref, up_ref, down_ref, hidden_ref, other_ref):
    width = gate_ref.shape[2]
    acts = acts_ref[...] + lift(chips, False, rows_ref, gate_ref, up_ref)
    gate_act, up_act = acts[:, :width], acts[:, width:]
    hidden = (gate_act / (1.0 + jnp.exp(-gate_act)) * up_act).astype(jnp.bfloat16)
    hidden_ref[...] = hidden
    lower(chips, False, hidden, down_ref, other_ref)


def ours(chips, hidden_ref, down_ref, mine_ref):
    lower(chips, True, hidden_ref[...], down_ref, mine_ref)


def add(mine_ref, other_ref, _, out_ref):
    total = mine_ref[...].astype(jnp.float32) + other_ref[...].astype(jnp.float32)
    out_ref[...] = total.astype(jnp.bfloat16)


def combine(match_ref, weight_ref, returned_ref, out_hbm, out_ref, sems):
    copies = []
    for part in range(out_ref.shape[0] // PIECE):
        rows = pl.ds(part * PIECE, PIECE)
        summed = jnp.dot(match_ref[rows, :], returned_ref[...], preferred_element_type=jnp.float32)
        out_ref[rows, :] = (weight_ref[rows, :] * summed).astype(jnp.bfloat16)
        copies.append(pltpu.make_async_copy(out_ref.at[rows, :], out_hbm.at[rows, :], sems.at[part]))
        copies[-1].start()
    for copy in copies:
        copy.wait()


def shards(tokens, expert_ids, route_scores, w_gate, w_up, w_down):
    row_count, features = tokens.shape
    top_count, hidden_count = expert_ids.shape[1], w_gate.shape[2]
    ep_count, chips = lax.axis_size("ep"), lax.axis_size("chip")
    slot_count = ep_count * CAP
    half = jax.ShapeDtypeStruct((chips * slot_count, features), jnp.bfloat16)
    ids, scores = expert_ids.T, route_scores.T
    hbm, vmem = (pl.BlockSpec(memory_space=space) for space in (pltpu.HBM, pltpu.VMEM))
    anywhere = pl.BlockSpec(memory_space=pl.ANY)

    def exchange(rows, order):
        groups = far_groups(order, ep_count, chips)
        return lax.all_to_all(rows, FAR, 0, 0, axis_index_groups=groups, tiled=True)

    def call(kernel, name, out_shape, **rest):
        return pl.pallas_call(kernel, out_shape=out_shape, name=name, compiler_params=LIMIT, **rest)

    outgoing = call(
        lambda *refs: route(ep_count, chips, *refs),
        "route",
        half,
        in_specs=[hbm] * 2,
        scratch_shapes=[
            pltpu.VMEM((top_count, row_count), jnp.int32),
            pltpu.VMEM((row_count, features), jnp.bfloat16),
            pltpu.SemaphoreType.DMA((row_count // PIECE + 1,)),
        ],
        cost_estimate=pl.CostEstimate(flops=2 * 10**9, bytes_accessed=0, transcendentals=0),
    )(*(pltpu.with_memory_space_constraint(value, pltpu.HBM) for value in (ids, tokens)))
    incoming = exchange(outgoing, first_order)
    across = lax.ppermute(incoming, "core", SWAP)
    acts = jax.ShapeDtypeStruct((slot_count, 2 * hidden_count), jnp.float32)
    begun = call(lambda *refs: begin(chips, *refs), "begin", acts)(incoming, w_gate, w_up)
    hidden_shape = jax.ShapeDtypeStruct((slot_count, hidden_count), jnp.bfloat16)
    hidden, other = call(lambda *refs: theirs(chips, *refs), "theirs", (hidden_shape, half))(
        across, begun, w_gate, w_up, w_down
    )
    crossed = lax.ppermute(other, "core", SWAP)
    mine = call(lambda *refs: ours(chips, *refs), "ours", half)(hidden, w_down)
    match, weight = call(
        lambda *refs: score(ep_count, chips, *refs),
        "score",
        (
            jax.ShapeDtypeStruct((row_count, chips * slot_count), jnp.bfloat16),
            jax.ShapeDtypeStruct((row_count, 1), jnp.float32),
        ),
        in_specs=[vmem] * 2 + [anywhere],
    )(ids, scores, other)
    summed = call(add, "add", half, in_specs=[vmem] * 2 + [anywhere])(mine, crossed, weight)
    returned = exchange(summed, second_order)
    return call(
        combine,
        "combine",
        jax.ShapeDtypeStruct((row_count, features), jnp.bfloat16),
        out_specs=hbm,
        scratch_shapes=[
            pltpu.VMEM((row_count, features), jnp.bfloat16),
            pltpu.SemaphoreType.DMA((row_count // PIECE,)),
        ],
    )(match, weight, returned)


def solution(mesh):
    groups, ep_count, tp_count = (mesh.shape[name] for name in ("groups", "ep", "tp"))
    split = jax.sharding.Mesh(
        mesh.devices.reshape(groups, ep_count, tp_count // 2, 2), ("groups", "ep", "chip", "core")
    )
    tp = ("chip", "core")
    placed = (
        P(("groups", "ep"), tp),
        P(("groups", "ep"), None),
        P(("groups", "ep"), None),
        P("ep", None, tp),
        P("ep", None, tp),
        P("ep", tp, None),
    )
    return jax.shard_map(
        shards, mesh=split, in_specs=placed, out_specs=P(("groups", "ep"), tp), check_vma=False
    )
```

```python
import jax
import jax.numpy as jnp
from jax import lax
from jax.experimental import pallas as pl
from jax.experimental.pallas import tpu as pltpu
from jax.sharding import PartitionSpec as P

CAP = 8
PIECE = 32
WRITE = 64
FAR = ("ep", "chip", "core")
SWAP = [(0, 1), (1, 0)]
LIMIT = pltpu.CompilerParams(vmem_limit_bytes=16 * 1024 * 1024)


def iota(shape, dim):
    return lax.broadcasted_iota(jnp.int32, shape, dim)


def to_column(row):
    size = row.shape[1]
    square = (size, size)
    return jnp.sum(jnp.where(iota(square, 0) == iota(square, 1), row, 0.0), axis=1, keepdims=True)


def slot_codes(ids, resident):
    row_count = ids.shape[1]
    expert = jnp.min(ids, axis=0, keepdims=True)
    onehot_shape = (-(-resident // 16) * 16, row_count)
    onehot = jnp.where(expert == iota(onehot_shape, 0).astype(jnp.float32), 1.0, 0.0)
    square = (row_count, row_count)
    earlier = jnp.where(iota(square, 0) < iota(square, 1), 1.0, 0.0).astype(jnp.bfloat16)
    counts = jnp.dot(onehot.astype(jnp.bfloat16), earlier, preferred_element_type=jnp.float32)
    return expert * CAP + jnp.sum(counts * onehot, axis=0, keepdims=True), expert


def first_order(ep_count, chip):
    listed = ((2, 3, 0, 1), (3, 2, 1, 0))[chip % 2]
    return [z // 4 * 4 + listed[z % 4] for z in range(ep_count)]


def second_order(ep_count, chip):
    listed = ((2, 1, 0, 3), (3, 2, 0, 1))[chip % 2]
    return [z // 4 * 4 + listed[z % 4] for z in range(ep_count)]


def row_codes(index, order, ep_count, chips):
    listed = [z for chip in range(chips) for z in order(ep_count, chip)]
    expert = sum(jnp.where(index // CAP == at, z // 2, 0) for at, z in enumerate(listed))
    return (expert * CAP + lax.rem(index, CAP)).astype(jnp.float32)


def route(ep_count, chips, ids_hbm, tokens_hbm, outgoing_ref, ids_ref, tokens_ref, sems):
    row_count = ids_ref.shape[1]
    parts = row_count // PIECE
    copies = [pltpu.make_async_copy(ids_hbm, ids_ref, sems.at[parts])] + [
        pltpu.make_async_copy(
            tokens_hbm.at[pl.ds(part * PIECE, PIECE), :],
            tokens_ref.at[pl.ds(part * PIECE, PIECE), :],
            sems.at[part],
        )
        for part in range(parts)
    ]
    for copy in copies:
        copy.start()
    wanted = row_codes(iota((outgoing_ref.shape[0], row_count), 0), first_order, ep_count, chips)
    copies[0].wait()
    code, _ = slot_codes(ids_ref[...].astype(jnp.float32), ep_count // 2)
    dispatch = jnp.where(code == wanted, 1.0, 0.0).astype(jnp.bfloat16)
    for copy in copies[1:]:
        copy.wait()
    outgoing_ref[...] = jnp.dot(
        dispatch, tokens_ref[...], preferred_element_type=jnp.float32
    ).astype(jnp.bfloat16)


def score(ep_count, chips, ids_ref, scores_ref, _, match_ref, weight_ref):
    ids = ids_ref[...].astype(jnp.float32)
    code, expert = slot_codes(ids, ep_count // 2)
    wanted = row_codes(iota(match_ref.shape, 1), second_order, ep_count, chips)
    match_ref[...] = jnp.where(to_column(code) == wanted, 1.0, 0.0).astype(jnp.bfloat16)
    squashed = jax.nn.sigmoid(scores_ref[...])
    chosen = jnp.sum(jnp.where(ids == expert, squashed, 0.0), axis=0, keepdims=True)
    weight_ref[...] = to_column(2.5 * chosen / jnp.sum(squashed, axis=0, keepdims=True))


def far_groups(order, ep_count, chips):
    return [
        [(z * chips + x) * 2 + (side + x) % 2 for x in range(chips) for z in order(ep_count, x)]
        for side in range(2)
    ]


def columns_of(chip, own, features):
    core = lax.rem(lax.axis_index("core") + lax.axis_index("chip") + chip + (0 if own else 1), 2)
    return pl.ds(pl.multiple_of((2 * chip + core) * features, features), features)


def in_order(values, held, wanted):
    if held == wanted:
        return values
    blocks = [values[held.index(z) * CAP : (held.index(z) + 1) * CAP, :] for z in wanted]
    return jnp.concatenate(blocks, axis=0)


def lift(chips, own, rows_ref, gate_ref, up_ref):
    part_rows, features = rows_ref.shape[0] // chips, rows_ref.shape[1]
    ep_count = part_rows // CAP
    total = jnp.zeros((part_rows, 2 * gate_ref.shape[2]), jnp.float32)
    for chip in range(chips):
        rows = rows_ref[chip * part_rows : (chip + 1) * part_rows, :]
        columns = columns_of(chip, own, features)
        both = jnp.concatenate([gate_ref[0, columns, :], up_ref[0, columns, :]], axis=1)
        acts = jnp.dot(rows, both, preferred_element_type=jnp.float32)
        total += in_order(acts, first_order(ep_count, chip), first_order(ep_count, 0))
    return total


def lower(chips, own, hidden, down_ref, out_ref):
    part_rows, features = out_ref.shape[0] // chips, out_ref.shape[1]
    ep_count = part_rows // CAP
    for chip in range(chips):
        columns = columns_of(chip, own, features)
        values = jnp.dot(hidden, down_ref[0, :, columns], preferred_element_type=jnp.float32)
        values = in_order(values, first_order(ep_count, 0), second_order(ep_count, chip))
        out_ref[chip * part_rows : (chip + 1) * part_rows, :] = values.astype(jnp.bfloat16)


def begin(chips, rows_ref, gate_ref, up_ref, acts_ref):
    acts_ref[...] = lift(chips, True, rows_ref, gate_ref, up_ref)


def theirs(chips, rows_ref, acts_ref, gate_ref, up_ref, down_ref, hidden_ref, other_ref):
    width = gate_ref.shape[2]
    acts = acts_ref[...] + lift(chips, False, rows_ref, gate_ref, up_ref)
    gate_act, up_act = acts[:, :width], acts[:, width:]
    hidden = (gate_act / (1.0 + jnp.exp(-gate_act)) * up_act).astype(jnp.bfloat16)
    hidden_ref[...] = hidden
    lower(chips, False, hidden, down_ref, other_ref)


def ours(chips, hidden_ref, down_ref, mine_ref):
    lower(chips, True, hidden_ref[...], down_ref, mine_ref)


def add(mine_ref, other_ref, _, out_ref):
    total = mine_ref[...].astype(jnp.float32) + other_ref[...].astype(jnp.float32)
    out_ref[...] = total.astype(jnp.bfloat16)


def combine(match_ref, weight_ref, returned_ref, out_hbm, out_ref, sems):
    copies = []
    for part in range(out_ref.shape[0] // WRITE):
        rows = pl.ds(part * WRITE, WRITE)
        summed = jnp.dot(match_ref[rows, :], returned_ref[...], preferred_element_type=jnp.float32)
        out_ref[rows, :] = (weight_ref[rows, :] * summed).astype(jnp.bfloat16)
        copies.append(pltpu.make_async_copy(out_ref.at[rows, :], out_hbm.at[rows, :], sems.at[part]))
        copies[-1].start()
    for copy in copies:
        copy.wait()


def shards(tokens, expert_ids, route_scores, w_gate, w_up, w_down):
    row_count, features = tokens.shape
    top_count, hidden_count = expert_ids.shape[1], w_gate.shape[2]
    ep_count, chips = lax.axis_size("ep"), lax.axis_size("chip")
    slot_count = ep_count * CAP
    half = jax.ShapeDtypeStruct((chips * slot_count, features), jnp.bfloat16)
    ids, scores = expert_ids.T, route_scores.T
    hbm, vmem = (pl.BlockSpec(memory_space=space) for space in (pltpu.HBM, pltpu.VMEM))
    anywhere = pl.BlockSpec(memory_space=pl.ANY)

    def exchange(rows, order):
        groups = far_groups(order, ep_count, chips)
        return lax.all_to_all(rows, FAR, 0, 0, axis_index_groups=groups, tiled=True)

    def call(kernel, name, out_shape, **rest):
        return pl.pallas_call(kernel, out_shape=out_shape, name=name, compiler_params=LIMIT, **rest)

    outgoing = call(
        lambda *refs: route(ep_count, chips, *refs),
        "route",
        half,
        in_specs=[hbm] * 2,
        scratch_shapes=[
            pltpu.VMEM((top_count, row_count), jnp.int32),
            pltpu.VMEM((row_count, features), jnp.bfloat16),
            pltpu.SemaphoreType.DMA((row_count // PIECE + 1,)),
        ],
        cost_estimate=pl.CostEstimate(flops=2 * 10**9, bytes_accessed=0, transcendentals=0),
    )(*(pltpu.with_memory_space_constraint(value, pltpu.HBM) for value in (ids, tokens)))
    incoming = exchange(outgoing, first_order)
    across = lax.ppermute(incoming, "core", SWAP)
    acts = jax.ShapeDtypeStruct((slot_count, 2 * hidden_count), jnp.float32)
    begun = call(lambda *refs: begin(chips, *refs), "begin", acts)(incoming, w_gate, w_up)
    hidden_shape = jax.ShapeDtypeStruct((slot_count, hidden_count), jnp.bfloat16)
    hidden, other = call(lambda *refs: theirs(chips, *refs), "theirs", (hidden_shape, half))(
        across, begun, w_gate, w_up, w_down
    )
    crossed = lax.ppermute(other, "core", SWAP)
    mine = call(lambda *refs: ours(chips, *refs), "ours", half)(hidden, w_down)
    match, weight = call(
        lambda *refs: score(ep_count, chips, *refs),
        "score",
        (
            jax.ShapeDtypeStruct((row_count, chips * slot_count), jnp.bfloat16),
            jax.ShapeDtypeStruct((row_count, 1), jnp.float32),
        ),
        in_specs=[vmem] * 2 + [anywhere],
    )(ids, scores, other)
    summed = call(add, "add", half, in_specs=[vmem] * 2 + [anywhere])(mine, crossed, weight)
    returned = exchange(summed, second_order)
    return call(
        combine,
        "combine",
        jax.ShapeDtypeStruct((row_count, features), jnp.bfloat16),
        out_specs=hbm,
        scratch_shapes=[
            pltpu.VMEM((row_count, features), jnp.bfloat16),
            pltpu.SemaphoreType.DMA((row_count // WRITE,)),
        ],
    )(match, weight, returned)


def solution(mesh):
    groups, ep_count, tp_count = (mesh.shape[name] for name in ("groups", "ep", "tp"))
    split = jax.sharding.Mesh(
        mesh.devices.reshape(groups, ep_count, tp_count // 2, 2), ("groups", "ep", "chip", "core")
    )
    tp = ("chip", "core")
    placed = (
        P(("groups", "ep"), tp),
        P(("groups", "ep"), None),
        P(("groups", "ep"), None),
        P("ep", None, tp),
        P("ep", None, tp),
        P("ep", tp, None),
    )
    return jax.shard_map(
        shards, mesh=split, in_specs=placed, out_specs=P(("groups", "ep"), tp), check_vma=False
    )
```
